32 devices in a mesh: seq: 4 (over x, core), batch: 8 (over z, y).
Axes of the slice: x: 2, y: 2, z: 4, core: 2. Of those that a mesh axis runs over, the one named last changes fastest.
Arguments:
- hidden: bfloat16 [24, 1024, 768], P('batch', 'seq'), may hold values from -6 to 6
- cond: float32 [24, 128], P('batch'), may hold values from -6 to 6
- lengths: int32 [24, 8], P('batch'), may hold values from 1 to 1017, as said below
- ln1_gain: float32 [768], replicated, may hold values from 0.25 to 1.75
- w_qkv: bfloat16 [768, 2304], replicated, may hold values from -0.21875 to 0.21875
- w_out: bfloat16 [768, 768], replicated, may hold values from -1.75 to 1.75
- ln2_gain: float32 [768], replicated, may hold values from 0.25 to 1.75
- w_fc1: bfloat16 [768, 3072], replicated, may hold values from -0.21875 to 0.21875
- b_fc1: float32 [3072], replicated, may hold values from -3 to 3
- w_fc2: bfloat16 [3072, 768], replicated, may hold values from -0.109375 to 0.109375
- b_fc2: float32 [768], replicated, may hold values from -2 to 2
- w_ada: bfloat16 [128, 4608], replicated, may hold values from -0.25 to 0.25
- b_ada: float32 [4608], replicated, may hold values from -2 to 2
- cotangent: bfloat16 [24, 1024, 768], P('batch', 'seq'), may hold values from -6 to 6
Outputs:
- output: bfloat16 [24, 1024, 768], P('batch', 'seq')
- hidden_grad: bfloat16 [24, 1024, 768], P('batch', 'seq')
- cond_grad: float32 [24, 128], P('batch')
- ln1_gain_grad: float32 [768], replicated
- w_qkv_grad: float32 [768, 2304], replicated
- w_out_grad: float32 [768, 768], replicated
- ln2_gain_grad: float32 [768], replicated
- w_fc1_grad: float32 [768, 3072], replicated
- b_fc1_grad: float32 [3072], replicated
- w_fc2_grad: float32 [3072, 768], replicated
- b_fc2_grad: float32 [768], replicated
- w_ada_grad: float32 [128, 4608], replicated
- b_ada_grad: float32 [4608], replicated
The draws below stay inside these ranges and needn't reach their ends.
Inputs may be any that keep to these rules, and one draw needn't show every extreme that they name: Each row's 8 lengths sum to 1024; in every row one document starts within the first 256 slots and ends within the last 256 slots.
All inputs are finite; a program needn't handle non-finite values.
Results may differ from the reference program's by a relative error of at most 0.015.
The reference program's roundings to bfloat16 on the way count: a program that leaves them out, or rounds other values in their place, can miss the bound.
Values may be sent and summed in bfloat16 or wider, within the bound.
No kernel may reach another device: no remote copies, remote signals or barrier semaphores. Data moves between devices by JAX's collectives and lax.ppermute only.
A program may use at most 320 MiB of HBM per device.

```python
import jax
import jax.numpy as jnp
from jax import lax

D = 768
HEADS = 12
HEAD = 64
FF = 3072
COND = 128
ROW_LEN = 1024
DOCS = 8
SPAN = 256
ROWS = 24


def split_amount(weights, chosen, pieces, amount):
    masked = jnp.where(chosen, weights, 0)
    cumulative = jnp.cumsum(masked, axis=1)
    overall = jnp.maximum(cumulative[:, -1:], 1)
    surplus = (amount - pieces)[:, None]
    shares = surplus * cumulative // overall
    previous = jnp.concatenate([jnp.zeros_like(shares[:, :1]), shares[:, :-1]], axis=1)
    return jnp.where(chosen, 1 + shares - previous, 0)


def draw_lengths(key, part):
    key = jax.random.fold_in(key, 7)
    key_set = jax.random.split(key, 4)
    anchor = jax.random.randint(key_set[0], (ROWS,), 0, DOCS)
    trailing_count = DOCS - 1 - anchor
    first_row = jnp.arange(ROWS) == 0
    leading_amount = anchor + jnp.where(first_row, 0, jax.random.randint(key_set[1], (ROWS,), 0, SPAN - anchor))
    trailing_amount = trailing_count + jnp.where(first_row, 0, jax.random.randint(key_set[2], (ROWS,), 0, SPAN - trailing_count))
    weights = jax.random.randint(key_set[3], (ROWS, DOCS), 1, 64)
    slot_index = jnp.arange(DOCS)[None, :]
    leading = split_amount(weights, slot_index < anchor[:, None], anchor, leading_amount)
    trailing = split_amount(weights, slot_index > anchor[:, None], trailing_count, trailing_amount)
    longest = ROW_LEN - leading_amount - trailing_amount
    return (leading + trailing + jnp.where(slot_index == anchor[:, None], longest[:, None], 0)).astype(jnp.int32)


def levels(rng, extent, shards, least, top_value):
    level, own = 1.0, jax.random.fold_in(rng, 6)
    for position, blocks in shards:
        heights = jnp.exp(jax.random.uniform(jax.random.fold_in(own, position), (blocks,), jnp.float32, least / len(shards), top_value / len(shards)))
        level = level * jnp.repeat(heights, extent[position] // blocks).reshape([-1 if axis == position else 1 for axis in range(len(extent))])
    return level


def bell_draw(key, dims, scale, bound, shards=(), kind=jnp.bfloat16):
    level = levels(key, dims, shards, -0.22, 0.18) if shards else 1.0
    array = jax.random.normal(key, dims, jnp.float32) * scale * level
    return jnp.minimum(jnp.maximum(array, -bound), bound).astype(kind)


def setup_inputs(seed: int = 0) -> dict:
    splits = jax.random.split(jax.random.key(seed), 15)
    return {
        "hidden": bell_draw(splits[0], (ROWS, ROW_LEN, D), 1.0, 6.0, ((0, 8), (1, 4))),
        "cond": bell_draw(splits[1], (ROWS, COND), 1.0, 6.0, ((0, 8),), jnp.float32),
        "lengths": draw_lengths(jax.random.fold_in(splits[14], 71), 0),
        "ln1_gain": jnp.clip(1.0 + 0.15 * jax.random.normal(splits[3], (D,), jnp.float32), 0.25, 1.75),
        "w_qkv": bell_draw(splits[4], (D, 3 * D), D ** -0.5, 0.21875),
        "w_out": bell_draw(splits[5], (D, D), (D // 64) ** -0.5, 1.75),
        "ln2_gain": jnp.clip(1.0 + 0.15 * jax.random.normal(splits[6], (D,), jnp.float32), 0.25, 1.75),
        "w_fc1": bell_draw(splits[7], (D, FF), D ** -0.5, 0.21875),
        "b_fc1": bell_draw(splits[8], (FF,), 0.5, 3.0, (), jnp.float32),
        "w_fc2": bell_draw(splits[9], (FF, D), FF ** -0.5, 0.109375),
        "b_fc2": bell_draw(splits[10], (D,), 0.3, 2.0, (), jnp.float32),
        "w_ada": bell_draw(splits[11], (COND, 6 * D), (4 * COND) ** -0.5, 0.25),
        "b_ada": bell_draw(splits[12], (6 * D,), 0.3, 2.0, (), jnp.float32),
        "cotangent": bell_draw(splits[13], (ROWS, ROW_LEN, D), 1.0, 6.0, ((0, 8), (1, 4))),
    }


@jax.custom_vjp
def low(v):
    return lax.optimization_barrier(v.astype(jnp.bfloat16)).astype(jnp.float32)

@jax.custom_vjp
def low_back(v):
    return v

def low_keep(v):
    return (low(v), None)

def low_pass(kept, grad):
    return (grad,)

def back_keep(v):
    return (v, None)

def back_low(kept, grad):
    return (low(grad),)
low.defvjp(low_keep, low_pass)
low_back.defvjp(back_keep, back_low)
highest = lax.Precision.HIGHEST

def layer_norm(values, gain):
    center = values - lax.optimization_barrier(jnp.mean(values, axis=-1, keepdims=True))
    spread = lax.optimization_barrier(jnp.mean(center * center, axis=-1, keepdims=True))
    return center * lax.rsqrt(spread + 1e-05) * gain

def rotate(values, places):
    shape_in = values.shape
    heads_view = values.reshape(shape_in[0], shape_in[1], HEADS, HEAD)
    half_dim = HEAD // 2
    inverse_freq = 10000.0 ** (-jnp.arange(half_dim, dtype=jnp.float32) * 2.0 / HEAD)
    angles = places.astype(jnp.float32)[:, :, None] * inverse_freq
    cosine = jnp.cos(angles)[:, :, None, :]
    sine = jnp.sin(angles)[:, :, None, :]
    front = heads_view[..., :half_dim]
    behind = heads_view[..., half_dim:]
    turned = jnp.concatenate([front * cosine - behind * sine, behind * cosine + front * sine], axis=-1)
    return turned.reshape(shape_in)

def doc_layout(lengths, slots):
    bounds = jnp.cumsum(lengths, axis=1)
    passed = (slots[None, :, None] >= bounds[:, None, :]).astype(jnp.int32)
    segment = lax.optimization_barrier(jnp.sum(passed, axis=2)).astype(jnp.int32)
    doc_start = lax.optimization_barrier(jnp.sum(passed * lengths[:, None, :], axis=2)).astype(jnp.int32)
    return (segment, slots[None, :] - doc_start)

def layer(weights, inputs, conds, segment, places):
    gain_one, w_qkv, w_out, gain_two, w_fc1, b_fc1, w_fc2, b_fc2, w_ada, b_ada = weights
    group_rows = inputs.shape[0]
    modulation = jnp.dot(conds, w_ada, precision=highest, preferred_element_type=jnp.float32) + b_ada
    shift_one, scale_one, gate_one, shift_two, scale_two, gate_two = [column[:, None, :] for column in jnp.split(modulation, 6, axis=1)]
    normed = low(layer_norm(inputs, gain_one) * (1.0 + scale_one) + shift_one)
    merged = low_back(jnp.dot(normed.reshape(-1, D), w_qkv, precision=highest, preferred_element_type=jnp.float32))
    merged = merged.reshape(group_rows, ROW_LEN, 3 * D)
    query = low(rotate(merged[..., :D], places)).reshape(group_rows, ROW_LEN, HEADS, HEAD)
    keys = low(rotate(merged[..., D:2 * D], places)).reshape(group_rows, ROW_LEN, HEADS, HEAD)
    values = low(merged[..., 2 * D:]).reshape(group_rows, ROW_LEN, HEADS, HEAD)
    scores = low_back(jnp.einsum('gqhd,gkhd->ghqk', query, keys, precision=highest) * 0.125)
    same_doc = segment[:, None, :, None] == segment[:, None, None, :]
    scores = jnp.where(same_doc, scores, -1e+30)
    peak = lax.optimization_barrier(jnp.max(scores, axis=-1, keepdims=True))
    expo = jnp.exp(scores - peak)
    probs = low(expo / lax.optimization_barrier(jnp.sum(expo, axis=-1, keepdims=True)))
    mixed = jnp.einsum('ghqk,gkhd->gqhd', probs, values, precision=highest).reshape(group_rows, ROW_LEN, D)
    mixed = low(low_back(mixed))
    attended = low_back(jnp.dot(mixed.reshape(-1, D), w_out, precision=highest, preferred_element_type=jnp.float32))
    resid = inputs + gate_one * attended.reshape(group_rows, ROW_LEN, D)
    second = low(layer_norm(resid, gain_two) * (1.0 + scale_two) + shift_two)
    hidden_pre = low_back(jnp.dot(second.reshape(-1, D), w_fc1, precision=highest, preferred_element_type=jnp.float32)) + b_fc1
    active = low(jax.nn.gelu(hidden_pre, approximate=True))
    branch = low_back(jnp.dot(active, w_fc2, precision=highest, preferred_element_type=jnp.float32)) + b_fc2
    return resid + gate_two * branch.reshape(group_rows, ROW_LEN, D)

def reference(hidden, cond, lengths, ln1_gain, w_qkv, w_out, ln2_gain, w_fc1, b_fc1, w_fc2, b_fc2, w_ada, b_ada, cotangent):
    slots = jnp.arange(ROW_LEN, dtype=jnp.int32)
    segment, places = doc_layout(lengths, slots)
    weights = tuple((tensor.astype(jnp.float32) for tensor in (ln1_gain, w_qkv, w_out, ln2_gain, w_fc1, b_fc1, w_fc2, b_fc2, w_ada, b_ada)))
    group = 2 if ROWS % 2 == 0 else 1
    blocks = ROWS // group

    def regroup(tensor):
        return tensor.reshape((blocks, group) + tensor.shape[1:])
    block_items = (regroup(hidden.astype(jnp.float32)), regroup(cond.astype(jnp.float32)), regroup(cotangent.astype(jnp.float32)), regroup(segment), regroup(places))

    def advance(totals, items):
        inputs, conds, cotan, seg_block, place_block = items

        def forward(params, feature_in, cond_in):
            return layer(params, feature_in, cond_in, seg_block, place_block)
        result, back_fn = jax.vjp(forward, weights, inputs, conds)
        grads, input_grad, cond_part = back_fn(cotan)
        totals = tuple((held + added for held, added in zip(totals, grads)))
        return (totals, (result.astype(jnp.bfloat16), input_grad.astype(jnp.bfloat16), cond_part))
    zeros = tuple((jnp.zeros_like(tensor) for tensor in weights))
    totals, (outputs, input_grads, cond_grads) = lax.scan(advance, zeros, block_items)
    return (outputs.reshape(ROWS, ROW_LEN, D), input_grads.reshape(ROWS, ROW_LEN, D), cond_grads.reshape(ROWS, COND), totals[0], totals[1], totals[2], totals[3], totals[4], totals[5], totals[6], totals[7], totals[8], totals[9])
```

```python
import jax
import jax.numpy as jnp
from jax import lax
from jax.experimental import pallas as pl
from jax.experimental.pallas import tpu as pltpu
from jax.sharding import PartitionSpec as P

HEADS = 12
HEAD = 64
VMEM_LIMIT = 48 * 2**20


highest = lax.Precision.HIGHEST


def layer_norm(values, gain):
    center = values - jnp.mean(values, axis=-1, keepdims=True)
    spread = jnp.mean(center * center, axis=-1, keepdims=True)
    return center * lax.rsqrt(spread + 1e-05) * gain


def modulate(values, gain, shift, scale):
    return layer_norm(values, gain) * (1.0 + scale) + shift


def gelu_tanh(values):
    return jax.nn.gelu(values, approximate=True)


def rotate(values, places):
    shape_in = values.shape
    heads_view = values.reshape(shape_in[0], shape_in[1], HEADS, HEAD)
    half_dim = HEAD // 2
    inverse_freq = 10000.0 ** (-jnp.arange(half_dim, dtype=jnp.float32) * 2.0 / HEAD)
    angles = places.astype(jnp.float32)[:, :, None] * inverse_freq
    cosine = jnp.cos(angles)[:, :, None, :]
    sine = jnp.sin(angles)[:, :, None, :]
    front = heads_view[..., :half_dim]
    behind = heads_view[..., half_dim:]
    turned = jnp.concatenate(
        [front * cosine - behind * sine, behind * cosine + front * sine], axis=-1
    )
    return turned.reshape(shape_in)


def doc_layout(lengths, slots):
    bounds = jnp.cumsum(lengths, axis=1)
    passed = (slots[None, :, None] >= bounds[:, None, :]).astype(jnp.int32)
    segment = jnp.sum(passed, axis=2)
    doc_start = jnp.sum(passed * lengths[:, None, :], axis=2)
    return (segment, slots[None, :] - doc_start)


def outer(left, right):
    return lax.dot_general(
        left, right, (((0,), (0,)), ((), ())), preferred_element_type=jnp.float32
    )


def against(values, weight):
    return lax.dot_general(
        values, weight, (((1,), (1,)), ((), ())), preferred_element_type=jnp.float32
    )


def scores_of(query, keys, query_seg, key_seg):
    query_heads = query.reshape(query.shape[0], HEADS, HEAD)
    key_heads = keys.reshape(keys.shape[0], HEADS, HEAD)
    scores = (
        jnp.einsum("chd,khd->hck", query_heads, key_heads, preferred_element_type=jnp.float32)
        * 0.125
    )
    return jnp.where(query_seg[None, :, None] == key_seg[None, None, :], scores, -1e30)


def attend(operands):
    query, keys, values, query_seg, key_seg = operands
    scores = scores_of(query, keys, query_seg, key_seg)
    peak = jnp.max(scores, axis=-1, keepdims=True)
    expo = jnp.exp(scores - peak)
    total_sum = jnp.sum(expo, axis=-1, keepdims=True)
    probs = (expo / total_sum).astype(jnp.bfloat16)
    value_heads = values.reshape(values.shape[0], HEADS, HEAD)
    mixed = jnp.einsum("hck,khd->chd", probs, value_heads, preferred_element_type=jnp.float32)
    return (mixed.reshape(query.shape[0], HEADS * HEAD), peak[..., 0] + jnp.log(total_sum[..., 0]))


def attend_back(operands):
    query, keys, values, mixed_grad, logsum, query_seg, key_seg = operands
    scores = scores_of(query, keys, query_seg, key_seg)
    probs = jnp.exp(scores - logsum[:, :, None])
    probs_low = probs.astype(jnp.bfloat16)
    grad_heads = mixed_grad.reshape(query.shape[0], HEADS, HEAD)
    query_heads = query.reshape(query.shape[0], HEADS, HEAD)
    key_heads = keys.reshape(keys.shape[0], HEADS, HEAD)
    value_heads = values.reshape(values.shape[0], HEADS, HEAD)
    value_grad = jnp.einsum(
        "hck,chd->khd", probs_low, grad_heads, preferred_element_type=jnp.float32
    )
    prob_grad = jnp.einsum(
        "chd,khd->hck", grad_heads, value_heads, preferred_element_type=jnp.float32
    )
    score_grad = (probs * (prob_grad - jnp.sum(probs * prob_grad, axis=-1, keepdims=True))).astype(
        jnp.bfloat16
    )
    query_grad = 0.125 * jnp.einsum(
        "hck,khd->chd", score_grad, key_heads, preferred_element_type=jnp.float32
    )
    key_grad = 0.125 * jnp.einsum(
        "hck,chd->khd", score_grad, query_heads, preferred_element_type=jnp.float32
    )
    return (
        query_grad.reshape(query.shape[0], -1),
        key_grad.reshape(keys.shape[0], -1),
        value_grad.reshape(keys.shape[0], -1),
    )


def swap(values, axis, bit):
    count = lax.axis_size(axis)
    return lax.ppermute(values, axis, [(i, i ^ bit) for i in range(count)])


def bit_of(axis, bit):
    return (lax.axis_index(axis) // bit) % 2


def batch_bits():
    count = lax.axis_size("batch")
    bits = []
    bit = 1
    while bit < count:
        bits.append(bit)
        bit *= 2
    return bits


def split_orders():
    bits = batch_bits()
    chip = ("seq", 2)
    split = [("batch", b) for b in bits[:3]]
    rest = [("batch", b) for b in bits[3:]]
    return ([chip] + split, split[:1] + [chip] + split[1:], rest)


def position_in(order):
    place = jnp.int32(0)
    for axis, bit in order:
        place = place * 2 + bit_of(axis, bit)
    return place


def total_of(parts):
    total = parts[0].astype(jnp.float32)
    for part in parts[1:]:
        total = total + part.astype(jnp.float32)
    return total.astype(jnp.bfloat16)


def scatter_group(first, second, order, rest):
    parts = [(first, 0), (second, 0)]
    rows = first.shape[0]
    for axis, bit in order:
        rows //= 2
        mine = bit_of(axis, bit)
        send = total_of(
            [lax.dynamic_slice_in_dim(p, at + (1 - mine) * rows, rows, 0) for p, at in parts]
        )
        parts = [(p, at + mine * rows) for p, at in parts] + [(swap(send, axis, bit), 0)]
    held = total_of([lax.dynamic_slice_in_dim(p, at, rows, 0) for p, at in parts])
    for axis, bit in rest:
        held = total_of([held, swap(held, axis, bit)])
    return held


def gather_group(held, order):
    blocks = held[None]
    for axis, bit in reversed(order):
        blocks = jnp.concatenate([blocks, swap(blocks, axis, bit)], axis=0)
    return blocks


def sync_piece(send, keep):
    order_a, order_b, rest = split_orders()
    got = swap(send, "seq", 1)
    out = []
    for g, order in ((0, order_a), (1, order_b)):
        held = scatter_group(keep[g], got[g], order, rest)
        full = gather_group(held, order)
        out.append((full, swap(full, "seq", 1)))
    (own_a, far_a), (own_b, far_b) = out
    return own_a, own_b, far_a, far_b


def place_scalars():
    order_a, order_b, _ = split_orders()
    return jnp.stack(
        [lax.axis_index("seq") % 2, position_in(order_a), position_in(order_b)]
    ).astype(jnp.int32)


def chunk_at(step, core):
    return jnp.where(step < 2, 2 * (1 - core) + step, 2 * core + step - 2)


def weight_grad_kernel(places_ref, left_ref, right_ref, send_ref, keep_ref):
    step = pl.program_id(0)
    result = outer(left_ref[...], right_ref[...]).astype(jnp.bfloat16)

    @pl.when(step < 2)
    def _():
        send_ref[0] = result

    @pl.when(step >= 2)
    def _():
        keep_ref[0] = result


def weight_grad(places, left, right, left_moves):
    tokens = left.shape[0]
    width = 768

    def left_map(i, at):
        return (0, chunk_at(i, at[0]) if left_moves else 0)

    def right_map(i, at):
        return (0, 0 if left_moves else chunk_at(i, at[0]))

    return pl.pallas_call(
        weight_grad_kernel,
        grid_spec=pltpu.PrefetchScalarGridSpec(
            num_scalar_prefetch=1,
            grid=(4,),
            in_specs=[
                pl.BlockSpec((tokens, width), left_map),
                pl.BlockSpec((tokens, width), right_map),
            ],
            out_specs=[
                pl.BlockSpec((1, width, width), lambda i, at: (jnp.minimum(i, 1), 0, 0)),
                pl.BlockSpec((1, width, width), lambda i, at: (jnp.maximum(i - 2, 0), 0, 0)),
            ],
        ),
        out_shape=[jax.ShapeDtypeStruct((2, width, width), jnp.bfloat16)] * 2,
        compiler_params=pltpu.CompilerParams(vmem_limit_bytes=VMEM_LIMIT),
        cost_estimate=pl.CostEstimate(
            flops=2 * tokens * 4 * width * width,
            bytes_accessed=2 * (5 * tokens * width + 4 * width * width),
            transcendentals=0,
        ),
    )(places, left, right)


def attention_grad_kernel(
    places_ref, normed_ref, merged_ref, mixed_ref, out_ref, send_ref, keep_ref
):
    step = pl.program_id(0)
    chunk = chunk_at(step, places_ref[0])

    def put(result):
        @pl.when(step < 2)
        def _():
            send_ref[0] = result

        @pl.when(step >= 2)
        def _():
            keep_ref[0] = result

    @pl.when(chunk < 3)
    def _():
        put(outer(normed_ref[...], merged_ref[...]).astype(jnp.bfloat16))

    @pl.when(chunk == 3)
    def _():
        put(outer(mixed_ref[...], out_ref[...]).astype(jnp.bfloat16))


def attention_grad(places, normed, merged, mixed, out_low):
    tokens = normed.shape[0]
    width = 768
    whole = pl.BlockSpec((tokens, width), lambda i, at: (0, 0))
    return pl.pallas_call(
        attention_grad_kernel,
        grid_spec=pltpu.PrefetchScalarGridSpec(
            num_scalar_prefetch=1,
            grid=(4,),
            in_specs=[
                whole,
                pl.BlockSpec(
                    (tokens, width), lambda i, at: (0, jnp.minimum(chunk_at(i, at[0]), 2))
                ),
                whole,
                whole,
            ],
            out_specs=[
                pl.BlockSpec((1, width, width), lambda i, at: (jnp.minimum(i, 1), 0, 0)),
                pl.BlockSpec((1, width, width), lambda i, at: (jnp.maximum(i - 2, 0), 0, 0)),
            ],
        ),
        out_shape=[jax.ShapeDtypeStruct((2, width, width), jnp.bfloat16)] * 2,
        compiler_params=pltpu.CompilerParams(vmem_limit_bytes=VMEM_LIMIT),
        cost_estimate=pl.CostEstimate(
            flops=2 * tokens * 4 * width * width,
            bytes_accessed=2 * (6 * tokens * width + 4 * width * width),
            transcendentals=0,
        ),
    )(places, normed, merged, mixed, out_low)


def spread_blocks(places_ref, blocks_ref, group, out_ref):
    count, rows, _ = blocks_ref.shape
    for j in range(count):
        row = pl.multiple_of((places_ref[1 + group] ^ j) * rows, 16)
        out_ref[pl.ds(row, rows), :] = blocks_ref[j].astype(jnp.float32)


def finish_kernel(places_ref, own_a, own_b, far_a, far_b, out_ref):
    step = pl.program_id(0)
    for k, (ref, group) in enumerate(((own_a, 0), (own_b, 1), (far_a, 0), (far_b, 1))):

        @pl.when(step == k)
        def _(ref=ref, group=group):
            spread_blocks(places_ref, ref, group, out_ref)


def finish_two_kernel(places_ref, own_a, own_b, far_a, far_b, merged_ref, out_ref):
    step = pl.program_id(0)
    chunk = chunk_at(step, 1 - places_ref[0])
    for k, (ref, group) in enumerate(((own_a, 0), (own_b, 1), (far_a, 0), (far_b, 1))):

        @pl.when((step == k) & (chunk < 3))
        def _(ref=ref, group=group):
            spread_blocks(places_ref, ref, group, merged_ref)

        @pl.when((step == k) & (chunk == 3))
        def _(ref=ref, group=group):
            spread_blocks(places_ref, ref, group, out_ref)


def finish_piece(places, pieces, kind):
    count, rows, width = pieces[0].shape
    whole = pl.BlockSpec((count, rows, width), lambda i, at: (0, 0, 0))
    side = count * rows

    def own_first(i, at):
        return chunk_at(i, 1 - at[0])

    if kind == "rows":
        kernel = finish_kernel
        out_specs = pl.BlockSpec((side, width), lambda i, at: (own_first(i, at), 0))
        out_shape = jax.ShapeDtypeStruct((4 * side, width), jnp.float32)
    elif kind == "columns":
        kernel = finish_kernel
        out_specs = pl.BlockSpec((side, width), lambda i, at: (0, own_first(i, at)))
        out_shape = jax.ShapeDtypeStruct((side, 4 * width), jnp.float32)
    else:
        kernel = finish_two_kernel
        out_specs = [
            pl.BlockSpec((side, width), lambda i, at: (0, jnp.minimum(own_first(i, at), 2))),
            pl.BlockSpec((side, width), lambda i, at: (0, 0)),
        ]
        out_shape = [
            jax.ShapeDtypeStruct((side, 3 * width), jnp.float32),
            jax.ShapeDtypeStruct((side, width), jnp.float32),
        ]
    return pl.pallas_call(
        kernel,
        grid_spec=pltpu.PrefetchScalarGridSpec(
            num_scalar_prefetch=1, grid=(4,), in_specs=[whole] * 4, out_specs=out_specs
        ),
        out_shape=out_shape,
        compiler_params=pltpu.CompilerParams(vmem_limit_bytes=VMEM_LIMIT),
        cost_estimate=pl.CostEstimate(
            flops=0, bytes_accessed=6 * 4 * side * width, transcendentals=0
        ),
    )(places, *pieces)


def sum_small(vectors, mod_rows, cond):
    rows = vectors.shape[0]
    both = jnp.concatenate([vectors, mod_rows.reshape(-1, vectors.shape[1])], axis=0)
    for bit in (1, 2):
        both = both + swap(both, "seq", bit)
    vectors, own = both[:rows], both[rows:]
    everyone, conds = own, cond
    for bit in batch_bits():
        got = swap(jnp.concatenate([vectors, everyone], axis=0), "batch", bit)
        vectors = vectors + got[:rows]
        everyone = jnp.concatenate([everyone, got[rows:]], axis=0)
        conds = jnp.concatenate([conds, swap(conds, "batch", bit)], axis=0)
    return vectors, own.reshape(cond.shape[0], -1), everyone.reshape(conds.shape[0], -1), conds


def shards(
    hidden,
    cond,
    lengths,
    ln1_gain,
    w_qkv,
    w_out,
    ln2_gain,
    w_fc1,
    b_fc1,
    w_fc2,
    b_fc2,
    w_ada,
    b_ada,
    cotangent,
):
    row_count, span_len, features = hidden.shape
    places = place_scalars()
    full_len = span_len * lax.axis_size("seq")
    offset = lax.axis_index("seq") * span_len
    query_seg, query_place = doc_layout(lengths, offset + jnp.arange(span_len, dtype=jnp.int32))
    key_seg, key_place = doc_layout(lengths, jnp.arange(full_len, dtype=jnp.int32))
    inputs = hidden.astype(jnp.float32)
    ada_full = w_ada.astype(jnp.float32)
    modulation = (
        jnp.dot(cond, ada_full, precision=highest, preferred_element_type=jnp.float32) + b_ada
    )
    shift_one, scale_one, gate_one, shift_two, scale_two, gate_two = [
        column[:, None, :] for column in jnp.split(modulation, 6, axis=1)
    ]
    normed, norm_one_back = jax.vjp(modulate, inputs, ln1_gain, shift_one, scale_one)
    normed_low = normed.astype(jnp.bfloat16)
    merged = jnp.dot(normed_low.reshape(-1, features), w_qkv, preferred_element_type=jnp.float32)
    merged = merged.reshape(row_count, span_len, 3 * features)

    def rotate_pair(query_in, key_in):
        return (rotate(query_in, query_place), rotate(key_in, query_place))

    (query_rot, key_rot), rotate_back = jax.vjp(
        rotate_pair, merged[..., :features], merged[..., features : 2 * features]
    )
    query_low = query_rot.astype(jnp.bfloat16)
    key_low = key_rot.astype(jnp.bfloat16)
    value_low = merged[..., 2 * features :].astype(jnp.bfloat16)
    keys_all, values_all = (
        lax.all_gather(key_low, "seq", axis=1, tiled=True),
        lax.all_gather(value_low, "seq", axis=1, tiled=True),
    )
    mixed, logsum = lax.map(attend, (query_low, keys_all, values_all, query_seg, key_seg))
    mixed_low = mixed.astype(jnp.bfloat16)
    attended = jnp.dot(
        mixed_low.reshape(-1, features), w_out, preferred_element_type=jnp.float32
    ).reshape(row_count, span_len, features)
    resid = inputs + gate_one * attended
    second, norm_two_back = jax.vjp(modulate, resid, ln2_gain, shift_two, scale_two)
    second_low = second.astype(jnp.bfloat16).reshape(-1, features)
    hidden_pre = jnp.dot(second_low, w_fc1, preferred_element_type=jnp.float32) + b_fc1
    active, gelu_back = jax.vjp(gelu_tanh, hidden_pre)
    active_low = active.astype(jnp.bfloat16)
    branch = (jnp.dot(active_low, w_fc2, preferred_element_type=jnp.float32) + b_fc2).reshape(
        row_count, span_len, features
    )
    output = (resid + gate_two * branch).astype(jnp.bfloat16)
    upstream = cotangent.astype(jnp.float32)
    gate_two_grad = jnp.sum(upstream * branch, axis=1)
    branch_grad = gate_two * upstream
    branch_low = branch_grad.astype(jnp.bfloat16).reshape(-1, features)
    fc2_pieces = sync_piece(*weight_grad(places, active_low, branch_low, True))
    fc2_bias_grad = jnp.sum(branch_grad, axis=(0, 1))
    active_grad = against(branch_low, w_fc2)
    pre_grad = gelu_back(active_grad)[0]
    pre_low = pre_grad.astype(jnp.bfloat16)
    fc1_bias_grad = jnp.sum(pre_grad, axis=0)
    fc1_pieces = sync_piece(*weight_grad(places, second_low, pre_low, False))
    second_grad = against(pre_low, w_fc1).reshape(row_count, span_len, features)
    resid_part, gain_two_grad, shift_two_grad, scale_two_grad = norm_two_back(second_grad)
    resid_grad = upstream + resid_part
    gate_one_grad = jnp.sum(resid_grad * attended, axis=1)
    attended_low = (gate_one * resid_grad).astype(jnp.bfloat16).reshape(-1, features)
    mixed_grad = (
        against(attended_low, w_out).astype(jnp.bfloat16).reshape(row_count, span_len, features)
    )
    query_grad, key_grad_all, value_grad_all = lax.map(
        attend_back, (query_low, keys_all, values_all, mixed_grad, logsum, query_seg, key_seg)
    )
    key_grad, value_grad = (
        lax.psum_scatter(
            key_grad_all.astype(jnp.bfloat16), "seq", scatter_dimension=1, tiled=True
        ).astype(jnp.float32),
        lax.psum_scatter(
            value_grad_all.astype(jnp.bfloat16), "seq", scatter_dimension=1, tiled=True
        ).astype(jnp.float32),
    )
    query_pre, key_pre = rotate_back((query_grad, key_grad))
    merged_grad = (
        jnp.concatenate([query_pre, key_pre, value_grad], axis=-1)
        .astype(jnp.bfloat16)
        .reshape(-1, 3 * features)
    )
    att_pieces = sync_piece(
        *attention_grad(
            places,
            normed_low.reshape(-1, features),
            merged_grad,
            mixed_low.reshape(-1, features),
            attended_low,
        )
    )
    normed_grad = against(merged_grad, w_qkv).reshape(row_count, span_len, features)
    input_part, gain_one_grad, shift_one_grad, scale_one_grad = norm_one_back(normed_grad)
    hidden_grad = (resid_grad + input_part).astype(jnp.bfloat16)
    mod_local = jnp.concatenate(
        [
            shift_one_grad[:, 0, :],
            scale_one_grad[:, 0, :],
            gate_one_grad,
            shift_two_grad[:, 0, :],
            scale_two_grad[:, 0, :],
            gate_two_grad,
        ],
        axis=1,
    )
    vectors = jnp.concatenate(
        [
            gain_one_grad[None],
            gain_two_grad[None],
            fc1_bias_grad.reshape(-1, features),
            fc2_bias_grad[None],
        ],
        axis=0,
    )
    vectors, mod_total, mod_all, cond_all = sum_small(vectors, mod_local, cond)
    ada_grad = jnp.dot(cond_all.T, mod_all, precision=highest, preferred_element_type=jnp.float32)
    cond_grad = jnp.dot(
        mod_total, ada_full.T, precision=highest, preferred_element_type=jnp.float32
    )
    qkv_grad, out_grad = finish_piece(places, att_pieces, "both")
    return (
        output,
        hidden_grad,
        cond_grad,
        vectors[0],
        qkv_grad,
        out_grad,
        vectors[1],
        finish_piece(places, fc1_pieces, "columns"),
        vectors[2 : 2 + w_fc1.shape[1] // features].reshape(-1),
        finish_piece(places, fc2_pieces, "rows"),
        vectors[-1],
        ada_grad,
        jnp.sum(mod_all, axis=0),
    )


def solution(mesh):
    return jax.shard_map(
        shards,
        mesh=mesh,
        in_specs=(
            P("batch", "seq", None),
            P("batch", None),
            P("batch", None),
            P(),
            P(),
            P(),
            P(),
            P(),
            P(),
            P(),
            P(),
            P(),
            P(),
            P("batch", "seq", None),
        ),
        out_specs=(
            P("batch", "seq", None),
            P("batch", "seq", None),
            P("batch", None),
            P(),
            P(),
            P(),
            P(),
            P(),
            P(),
            P(),
            P(),
            P(),
            P(),
        ),
        check_vma=False,
    )
```

```python
import functools

import jax
import jax.numpy as jnp
from jax import lax
from jax.experimental import pallas as pl
from jax.experimental.pallas import tpu as pltpu
from jax.sharding import PartitionSpec as P

HEADS = 12
HEAD = 64
DOCS = 8
LANES = 128
GELU_A = 0.7978845608
GELU_B = 0.044715
VMEM_LIMIT = 60 * 2**20


highest = lax.Precision.HIGHEST


def dot_nt(left, right):
    return lax.dot_general(
        left, right, (((1,), (1,)), ((), ())), preferred_element_type=jnp.float32
    )


def dot_tn(left, right):
    return lax.dot_general(
        left, right, (((0,), (0,)), ((), ())), preferred_element_type=jnp.float32
    )


def dot_nn(left, right):
    return jnp.dot(left, right, preferred_element_type=jnp.float32)


def column_sum(values):
    return jnp.sum(values, axis=0, keepdims=True)


def row_mean(values):
    return jnp.mean(values, axis=-1, keepdims=True)


def normalized(values):
    center = values - row_mean(values)
    inverse = lax.rsqrt(row_mean(center * center) + 1e-05)
    return center * inverse, inverse


def documents_of(slots, layout_ref, group):
    end = jnp.int32(0)
    segment = jnp.zeros_like(slots)
    start = jnp.zeros_like(slots)
    for i in range(DOCS):
        length = layout_ref[group * DOCS + i]
        end = end + length
        passed = slots >= end
        segment = segment + passed.astype(jnp.int32)
        start = start + jnp.where(passed, length, 0)
    return segment, slots - start


def base_of(layout_ref, block):
    return layout_ref[2 * DOCS + block]


def turned(values, cosine, sine):
    lanes = lax.broadcasted_iota(jnp.int32, cosine.shape, 1)
    first = lanes % HEAD < HEAD // 2
    pieces = []
    for c in range(values.shape[1] // LANES):
        u = values[:, c * LANES : (c + 1) * LANES]
        other = jnp.where(
            first, pltpu.roll(u, LANES - HEAD // 2, 1), pltpu.roll(u, HEAD // 2, 1)
        )
        pieces.append(u * cosine + other * sine)
    return pieces


def project_kernel(groups, bases, layout_ref, *refs):
    count = len(groups)
    hidden = refs[:count]
    mod_ref, gain_ref, speed_ref, weight_ref = refs[count : count + 4]
    normed = refs[count + 4 : 2 * count + 4]
    query = refs[2 * count + 4 : 3 * count + 4]
    keyval = refs[3 * count + 4 : 4 * count + 4]
    angle = refs[4 * count + 4 : 5 * count + 4]
    step = pl.program_id(0)
    span = hidden[0].shape[0]

    @pl.when(step == 0)
    def _():
        for b in range(count):
            values, _ = normalized(hidden[b][...].astype(jnp.float32))
            scale = mod_ref[groups[b], 1:2, :]
            shift = mod_ref[groups[b], 0:1, :]
            normed[b][...] = (values * gain_ref[...] * (1.0 + scale) + shift).astype(jnp.bfloat16)
            slots = base_of(layout_ref, bases[b]) + lax.broadcasted_iota(
                jnp.int32, (span, LANES), 0
            )
            _, place = documents_of(slots, layout_ref, groups[b])
            lanes = lax.broadcasted_iota(jnp.int32, (span, LANES), 1)
            angles = place.astype(jnp.float32) * speed_ref[...]
            sine = jnp.sin(angles)
            angle[b][0] = jnp.cos(angles)
            angle[b][1] = jnp.where(lanes % HEAD < HEAD // 2, -sine, sine)

    for b in range(count):
        merged = dot_nn(normed[b][...], weight_ref[...])

        @pl.when(step == 0)
        def _(b=b, merged=merged):
            for c, piece in enumerate(turned(merged, angle[b][0], angle[b][1])):
                query[b][:, c * LANES : (c + 1) * LANES] = (piece * 0.125).astype(jnp.bfloat16)

        @pl.when(step == 1)
        def _(b=b, merged=merged):
            for c, piece in enumerate(turned(merged, angle[b][0], angle[b][1])):
                keyval[b][c, :, :LANES] = piece.astype(jnp.bfloat16)

        @pl.when(step == 2)
        def _(b=b, merged=merged):
            for c in range(merged.shape[1] // LANES):
                keyval[b][c, :, LANES:] = merged[:, c * LANES : (c + 1) * LANES].astype(
                    jnp.bfloat16
                )


def speeds():
    half = 10000.0 ** (-jnp.arange(HEAD // 2, dtype=jnp.float32) * 2.0 / HEAD)
    return jnp.tile(half, LANES // (HEAD // 2))[None]


def project(layout, hidden, mod, gain, weight, groups, bases):
    count = len(hidden)
    span, width = hidden[0].shape
    pairs = width // LANES
    whole = pl.BlockSpec((span, width), lambda i, at: (0, 0))
    return pl.pallas_call(
        functools.partial(project_kernel, groups, bases),
        grid_spec=pltpu.PrefetchScalarGridSpec(
            num_scalar_prefetch=1,
            grid=(3,),
            in_specs=[whole] * count
            + [
                pl.BlockSpec(mod.shape, lambda i, at: (0, 0, 0)),
                pl.BlockSpec(gain.shape, lambda i, at: (0, 0)),
                pl.BlockSpec((1, LANES), lambda i, at: (0, 0)),
                pl.BlockSpec((width, width), lambda i, at: (0, i)),
            ],
            out_specs=[whole] * (2 * count)
            + [pl.BlockSpec((pairs, span, 2 * LANES), lambda i, at: (0, 0, 0))] * count
            + [pl.BlockSpec((2, span, LANES), lambda i, at: (0, 0, 0))] * count,
        ),
        out_shape=[jax.ShapeDtypeStruct((span, width), jnp.bfloat16)] * (2 * count)
        + [jax.ShapeDtypeStruct((pairs, span, 2 * LANES), jnp.bfloat16)] * count
        + [jax.ShapeDtypeStruct((2, span, LANES), jnp.float32)] * count,
        compiler_params=pltpu.CompilerParams(vmem_limit_bytes=VMEM_LIMIT),
        cost_estimate=pl.CostEstimate(
            flops=6 * count * span * width * width,
            bytes_accessed=2 * (5 * count * span * width + 3 * width * width),
            transcendentals=0,
        ),
    )(layout, *hidden, mod, gain, speeds(), weight)


def mask_into(bias_ref, layout_ref, group, query_blocks):
    span = bias_ref.shape[-1]
    rows = lax.broadcasted_iota(jnp.int32, (span, span), 0)
    columns = lax.broadcasted_iota(jnp.int32, (span, span), 1)
    for k in range(4):
        key_segment, _ = documents_of(base_of(layout_ref, k) + rows, layout_ref, group)
        for q in range(query_blocks):
            query_segment, _ = documents_of(base_of(layout_ref, q) + columns, layout_ref, group)
            bias_ref[q, k] = jnp.where(key_segment == query_segment, 0.0, -1e30)


def one_head(values, head):
    lanes = lax.broadcasted_iota(jnp.int32, values.shape, 1)
    return jnp.where(lanes // HEAD == head, values, jnp.zeros_like(values))


def attend_kernel(group, count, layout_ref, *refs):
    query = refs[:count]
    keyval = refs[count : count + 4]
    mixed = refs[count + 4 : 2 * count + 4]
    logsum = refs[2 * count + 4 : 3 * count + 4]
    bias_ref, score_ref = refs[3 * count + 4 :]

    @pl.when(pl.program_id(0) == 0)
    def _():
        mask_into(bias_ref, layout_ref, group, count)

    turned_values = [keyval[k][0, :, LANES:].T for k in range(4)]
    for q in range(count):
        heads = []
        for h in range(2):
            chosen = one_head(query[q][...], h)
            peak = None
            for k in range(4):
                scores = dot_nt(keyval[k][0, :, :LANES], chosen) + bias_ref[q, k]
                score_ref[h, k] = scores
                top = jnp.max(scores, axis=0, keepdims=True)
                peak = top if peak is None else jnp.maximum(peak, top)
            total = None
            sums = None
            for k in range(4):
                expo = jnp.exp(score_ref[h, k] - peak)
                part = jnp.sum(expo, axis=0, keepdims=True)
                total = part if total is None else total + part
                values = turned_values[k][h * HEAD : (h + 1) * HEAD, :]
                term = dot_nn(values, expo.astype(jnp.bfloat16))
                sums = term if sums is None else sums + term
            heads.append(sums / total)
            logsum[q][0, h : h + 1, :] = peak + jnp.log(total)
        mixed[q][...] = jnp.concatenate(heads, axis=0).T.astype(jnp.bfloat16)


def attend(layout, query, keyval, group):
    count = len(query)
    span, width = query[0].shape
    pairs = width // LANES
    by_pair = pl.BlockSpec((span, LANES), lambda i, at: (0, i))
    return pl.pallas_call(
        functools.partial(attend_kernel, group, count),
        grid_spec=pltpu.PrefetchScalarGridSpec(
            num_scalar_prefetch=1,
            grid=(pairs,),
            in_specs=[by_pair] * count
            + [pl.BlockSpec((1, span, 2 * LANES), lambda i, at: (i, 0, 0))] * 4,
            out_specs=[by_pair] * count
            + [pl.BlockSpec((1, 2, span), lambda i, at: (i, 0, 0))] * count,
            scratch_shapes=[
                pltpu.VMEM((count, 4, span, span), jnp.float32),
                pltpu.VMEM((2, 4, span, span), jnp.float32),
            ],
        ),
        out_shape=[jax.ShapeDtypeStruct((span, width), jnp.bfloat16)] * count
        + [jax.ShapeDtypeStruct((pairs, 2, span), jnp.float32)] * count,
        compiler_params=pltpu.CompilerParams(vmem_limit_bytes=VMEM_LIMIT),
        cost_estimate=pl.CostEstimate(
            flops=16 * count * span * 4 * span * width,
            bytes_accessed=2 * (2 * count + 8) * span * width,
            transcendentals=0,
        ),
    )(layout, *query, *keyval)


def attend_back_kernel(group, count, layout_ref, *refs):
    query = refs[:count]
    mixed = refs[count : 2 * count]
    grad = refs[2 * count : 3 * count]
    logsum = refs[3 * count : 4 * count]
    keyval = refs[4 * count : 4 * count + 4]
    query_grad = refs[4 * count + 4 : 5 * count + 4]
    near_ref, far_ref, bias_ref = refs[5 * count + 4 :]

    @pl.when(pl.program_id(0) == 0)
    def _():
        mask_into(bias_ref, layout_ref, group, count)

    turned_keys = [keyval[k][0, :, :LANES].T for k in range(4)]
    key_grads = [None] * 4
    value_grads = [None] * 4
    for q in range(count):
        weighed = (mixed[q][...].astype(jnp.float32) * grad[q][...].astype(jnp.float32)).T
        heads = []
        for h in range(2):
            chosen = one_head(query[q][...], h)
            chosen_grad = one_head(grad[q][...], h)
            delta = jnp.sum(weighed[h * HEAD : (h + 1) * HEAD, :], axis=0, keepdims=True)
            spread = logsum[q][0, h : h + 1, :]
            sums = None
            for k in range(4):
                scores = dot_nt(keyval[k][0, :, :LANES], chosen) + bias_ref[q, k]
                probs = jnp.exp(scores - spread)
                term = dot_nn(probs.astype(jnp.bfloat16), chosen_grad)
                value_grads[k] = term if value_grads[k] is None else value_grads[k] + term
                prob_grad = dot_nt(keyval[k][0, :, LANES:], chosen_grad)
                score_grad = (probs * (prob_grad - delta)).astype(jnp.bfloat16)
                term = dot_nn(score_grad, chosen)
                key_grads[k] = term if key_grads[k] is None else key_grads[k] + term
                term = dot_nn(turned_keys[k][h * HEAD : (h + 1) * HEAD, :], score_grad)
                sums = term if sums is None else sums + term
            heads.append(sums)
        query_grad[q][...] = jnp.concatenate(heads, axis=0).T * 0.125
    for k in range(4):
        ref = near_ref if k < 2 else far_ref
        ref[k % 2, 0, :, :LANES] = key_grads[k].astype(ref.dtype)
        ref[k % 2, 0, :, LANES:] = value_grads[k].astype(ref.dtype)


def attend_back(layout, query, mixed, grad, logsum, keyval, group):
    count = len(query)
    span, width = query[0].shape
    pairs = width // LANES
    by_pair = pl.BlockSpec((span, LANES), lambda i, at: (0, i))
    two_blocks = pl.BlockSpec((2, 1, span, 2 * LANES), lambda i, at: (0, i, 0, 0))
    return pl.pallas_call(
        functools.partial(attend_back_kernel, group, count),
        grid_spec=pltpu.PrefetchScalarGridSpec(
            num_scalar_prefetch=1,
            grid=(pairs,),
            in_specs=[by_pair] * (3 * count)
            + [pl.BlockSpec((1, 2, span), lambda i, at: (i, 0, 0))] * count
            + [pl.BlockSpec((1, span, 2 * LANES), lambda i, at: (i, 0, 0))] * 4,
            out_specs=[by_pair] * count + [two_blocks] * 2,
            scratch_shapes=[pltpu.VMEM((count, 4, span, span), jnp.float32)],
        ),
        out_shape=[jax.ShapeDtypeStruct((span, width), jnp.float32)] * count
        + [
            jax.ShapeDtypeStruct((2, pairs, span, 2 * LANES), jnp.float32),
            jax.ShapeDtypeStruct((2, pairs, span, 2 * LANES), jnp.bfloat16),
        ],
        compiler_params=pltpu.CompilerParams(vmem_limit_bytes=VMEM_LIMIT),
        cost_estimate=pl.CostEstimate(
            flops=40 * count * span * 4 * span * width,
            bytes_accessed=2 * (5 * count + 20) * span * width,
            transcendentals=0,
        ),
    )(layout, *query, *mixed, *grad, *logsum, *keyval)


def group_of(block):
    return 0 if block < 2 else 1


def feed_kernel(places_ref, *refs):
    mixed, hidden, cotan = refs[0:3], refs[3:6], refs[6:9]
    mod_ref, gain_ref, w_out_ref, w_one_ref, b_one_ref, w_two_ref, b_two_ref = refs[9:16]
    result, mixed_grad = refs[16:19], refs[19:22]
    resid_ref, low_ref, send_one, keep_one, send_two, keep_two, b_one_grad, sums_ref = refs[22:30]
    second_ref, turned_ref, branch_low_ref, branch_ref, second_grad_ref, act_ref, pre_ref = refs[30:]
    step = pl.program_id(0)
    span = hidden[0].shape[0]

    def modulation(block, which):
        return mod_ref[group_of(block), which : which + 1, :]

    @pl.when(step == 0)
    def _():
        bias_sum = None
        for b in range(3):
            rows = slice(b * span, (b + 1) * span)
            attended = dot_nn(mixed[b][...], w_out_ref[...])
            resid = hidden[b][...].astype(jnp.float32) + modulation(b, 2) * attended
            resid_ref[rows, :] = resid
            values, _ = normalized(resid)
            second = values * gain_ref[...] * (1.0 + modulation(b, 4)) + modulation(b, 3)
            second = second.astype(jnp.bfloat16)
            second_ref[rows, :] = second
            turned_ref[:, rows] = second.T
            branch_grad = modulation(b, 5) * cotan[b][...].astype(jnp.float32)
            branch_low_ref[rows, :] = branch_grad.astype(jnp.bfloat16)
            part = column_sum(branch_grad)
            bias_sum = part if bias_sum is None else bias_sum + part
        sums_ref[...] = jnp.zeros_like(sums_ref)
        sums_ref[1:2, :] = bias_sum
        branch_ref[...] = jnp.zeros_like(branch_ref)
        second_grad_ref[...] = jnp.zeros_like(second_grad_ref)

    b_one_grad[...] = jnp.zeros_like(b_one_grad)

    @pl.loop(0, 3)
    def _(b):
        rows = pl.ds(pl.multiple_of(b * span, span), span)
        pre = dot_nn(second_ref[rows, :], w_one_ref[...]) + b_one_ref[...]
        square = pre * pre
        tanh = jnp.tanh(GELU_A * pre * (1.0 + GELU_B * square))
        half = 0.5 * (1.0 + tanh)
        active = (pre * half).astype(jnp.bfloat16)
        act_ref[rows, :] = active
        branch_ref[rows, :] += dot_nn(active, w_two_ref[...])
        slope = half + 0.5 * GELU_A * pre * (1.0 - tanh * tanh) * (1.0 + 3.0 * GELU_B * square)
        pre_grad = dot_nt(branch_low_ref[rows, :], w_two_ref[...]) * slope
        b_one_grad[0] += column_sum(pre_grad)
        pre_low = pre_grad.astype(jnp.bfloat16)
        pre_ref[rows, :] = pre_low
        second_grad_ref[rows, :] += dot_nt(pre_low, w_one_ref[...])

    two_grad = dot_tn(act_ref[...], branch_low_ref[...]).astype(jnp.bfloat16)
    one_grad = dot_nn(turned_ref[...], pre_ref[...]).astype(jnp.bfloat16)

    @pl.when(step < 2)
    def _():
        send_two[0] = two_grad
        send_one[0] = one_grad

    @pl.when(step >= 2)
    def _():
        keep_two[0] = two_grad
        keep_one[0] = one_grad

    @pl.when(step == 3)
    def _():
        for b in range(3):
            at = 2 + 4 * group_of(b)
            rows = slice(b * span, (b + 1) * span)
            resid = resid_ref[rows, :]
            branch = branch_ref[rows, :] + b_two_ref[...]
            result[b][...] = (resid + modulation(b, 5) * branch).astype(jnp.bfloat16)
            upstream = cotan[b][...].astype(jnp.float32)
            sums_ref[at + 3 : at + 4, :] += column_sum(upstream * branch)
            values, inverse = normalized(resid)
            grad = second_grad_ref[rows, :]
            sums_ref[at + 1 : at + 2, :] += column_sum(grad)
            weighed = column_sum(grad * values)
            sums_ref[at + 2 : at + 3, :] += weighed * gain_ref[...]
            sums_ref[0:1, :] += weighed * (1.0 + modulation(b, 4))
            inner = grad * ((1.0 + modulation(b, 4)) * gain_ref[...])
            back = (inner - row_mean(inner) - values * row_mean(inner * values)) * inverse
            resid_grad = upstream + back
            resid_ref[rows, :] = resid_grad
            attended = dot_nn(mixed[b][...], w_out_ref[...])
            sums_ref[at : at + 1, :] += column_sum(resid_grad * attended)
            low = (modulation(b, 2) * resid_grad).astype(jnp.bfloat16)
            low_ref[rows, :] = low
            mixed_grad[b][...] = dot_nt(low, w_out_ref[...]).astype(jnp.bfloat16)


def feed(places, mixed, hidden, cotan, mod, gain, w_out, w_one, b_one, w_two, b_two):
    span, width = hidden[0].shape
    tokens = 3 * span
    once = pl.Buffered(1)
    block = pl.BlockSpec((span, width), lambda i, at: (0, 0), pipeline_mode=once)
    out_block = pl.BlockSpec((span, width), lambda i, at: (0, 0))
    every = pl.BlockSpec((tokens, width), lambda i, at: (0, 0))
    row = pl.BlockSpec((1, width), lambda i, at: (0, 0))
    send = pl.BlockSpec((1, width, width), lambda i, at: (jnp.minimum(i, 1), 0, 0))
    keep = pl.BlockSpec((1, width, width), lambda i, at: (jnp.maximum(i - 2, 0), 0, 0))
    low_block = jax.ShapeDtypeStruct((span, width), jnp.bfloat16)
    chunk_pair = jax.ShapeDtypeStruct((2, width, width), jnp.bfloat16)
    return pl.pallas_call(
        feed_kernel,
        grid_spec=pltpu.PrefetchScalarGridSpec(
            num_scalar_prefetch=1,
            grid=(4,),
            in_specs=[block] * 9
            + [
                pl.BlockSpec(mod.shape, lambda i, at: (0, 0, 0)),
                row,
                pl.BlockSpec((width, width), lambda i, at: (0, 0), pipeline_mode=once),
                pl.BlockSpec((width, width), lambda i, at: (0, chunk_at(i, at[0]))),
                pl.BlockSpec((1, width), lambda i, at: (0, chunk_at(i, at[0]))),
                pl.BlockSpec((width, width), lambda i, at: (chunk_at(i, at[0]), 0)),
                row,
            ],
            out_specs=[out_block] * 6
            + [every, every, send, keep, send, keep]
            + [
                pl.BlockSpec((1, 1, width), lambda i, at: (chunk_at(i, at[0]), 0, 0)),
                pl.BlockSpec((16, width), lambda i, at: (0, 0)),
            ],
            scratch_shapes=[
                pltpu.VMEM((tokens, width), jnp.bfloat16),
                pltpu.VMEM((width, tokens), jnp.bfloat16),
                pltpu.VMEM((tokens, width), jnp.bfloat16),
                pltpu.VMEM((tokens, width), jnp.float32),
                pltpu.VMEM((tokens, width), jnp.float32),
                pltpu.VMEM((tokens, width), jnp.bfloat16),
                pltpu.VMEM((tokens, width), jnp.bfloat16),
            ],
        ),
        out_shape=[low_block] * 6
        + [
            jax.ShapeDtypeStruct((tokens, width), jnp.float32),
            jax.ShapeDtypeStruct((tokens, width), jnp.bfloat16),
        ]
        + [chunk_pair] * 4
        + [
            jax.ShapeDtypeStruct((4, 1, width), jnp.float32),
            jax.ShapeDtypeStruct((16, width), jnp.float32),
        ],
        compiler_params=pltpu.CompilerParams(vmem_limit_bytes=VMEM_LIMIT),
        cost_estimate=pl.CostEstimate(
            flops=2 * tokens * 26 * width * width,
            bytes_accessed=2 * (14 * tokens * width + 17 * width * width),
            transcendentals=0,
        ),
    )(places, *mixed, *hidden, *cotan, mod, gain, w_out, w_one, b_one, w_two, b_two)


def merge_kernel(places_ref, *refs):
    query_grad = refs[0:3]
    near_own, got_own, near_split, got_split, got_chip = refs[3:8]
    angle, normed, mixed, hidden = refs[8:11], refs[11:14], refs[14:17], refs[17:20]
    low_ref, resid_grad_ref, mod_ref, gain_ref, weight_ref = refs[20:25]
    hidden_grad = refs[25:28]
    send_ref, keep_ref, sums_ref = refs[28:31]
    normed_ref, mixed_ref, grad_ref, total_ref = refs[31:]
    step = pl.program_id(0)
    chunk = chunk_at(step, places_ref[0])
    span = hidden[0].shape[0]
    pairs = hidden[0].shape[1] // LANES

    @pl.when(step == 0)
    def _():
        for b in range(3):
            rows = slice(b * span, (b + 1) * span)
            normed_ref[:, rows] = normed[b][...].T
            mixed_ref[:, rows] = mixed[b][...].T
        total_ref[...] = jnp.zeros_like(total_ref)

    def keyval_sum(block, pair, lanes):
        if block < 2:
            own, got = near_own, got_own
            at = block
        else:
            own, got = near_split, got_split
            at = 0
        total = own[at, pair, :, lanes] + got[at, pair, :, lanes].astype(jnp.float32)
        if block == 2:
            total = total + got_chip[pair, :, lanes].astype(jnp.float32)
        return total

    def put(result):
        @pl.when(step < 2)
        def _():
            send_ref[0] = result

        @pl.when(step >= 2)
        def _():
            keep_ref[0] = result

    @pl.when(chunk < 3)
    def _():
        for b in range(3):
            rows = slice(b * span, (b + 1) * span)
            for c in range(pairs):
                lanes = slice(c * LANES, (c + 1) * LANES)

                @pl.when(chunk == 0)
                def _(b=b, rows=rows, lanes=lanes):
                    (piece,) = turned(query_grad[b][:, lanes], angle[b][0], -angle[b][1])
                    grad_ref[rows, lanes] = piece.astype(jnp.bfloat16)

                @pl.when(chunk == 1)
                def _(b=b, c=c, rows=rows, lanes=lanes):
                    values = keyval_sum(b, c, slice(0, LANES))
                    (piece,) = turned(values, angle[b][0], -angle[b][1])
                    grad_ref[rows, lanes] = piece.astype(jnp.bfloat16)

                @pl.when(chunk == 2)
                def _(b=b, c=c, rows=rows, lanes=lanes):
                    values = keyval_sum(b, c, slice(LANES, 2 * LANES))
                    grad_ref[rows, lanes] = values.astype(jnp.bfloat16)

        put(dot_nn(normed_ref[...], grad_ref[...]).astype(jnp.bfloat16))
        total_ref[...] += dot_nt(grad_ref[...], weight_ref[...])

    @pl.when(chunk == 3)
    def _():
        put(dot_nn(mixed_ref[...], low_ref[...]).astype(jnp.bfloat16))

    @pl.when(step == 3)
    def _():
        sums_ref[...] = jnp.zeros_like(sums_ref)
        for b in range(3):
            group = group_of(b)
            at = 1 + 2 * group
            rows = slice(b * span, (b + 1) * span)
            values, inverse = normalized(hidden[b][...].astype(jnp.float32))
            grad = total_ref[rows, :]
            scaled = 1.0 + mod_ref[group, 1:2, :]
            weighed = column_sum(grad * values)
            sums_ref[0:1, :] += weighed * scaled
            sums_ref[at : at + 1, :] += column_sum(grad)
            sums_ref[at + 1 : at + 2, :] += weighed * gain_ref[...]
            inner = grad * (scaled * gain_ref[...])
            back = (inner - row_mean(inner) - values * row_mean(inner * values)) * inverse
            hidden_grad[b][...] = (resid_grad_ref[rows, :] + back).astype(jnp.bfloat16)


def merge_back(
    places, query_grad, keyval_grads, angle, normed, mixed, hidden, low, resid_grad, mod, gain, weight
):
    span, width = hidden[0].shape
    tokens = 3 * span
    once = pl.Buffered(1)

    def whole(array):
        return pl.BlockSpec(
            array.shape, lambda i, at: (0,) * len(array.shape), pipeline_mode=once
        )

    operands = [
        *query_grad, *keyval_grads, *angle, *normed, *mixed, *hidden, low, resid_grad, mod, gain
    ]
    return pl.pallas_call(
        merge_kernel,
        grid_spec=pltpu.PrefetchScalarGridSpec(
            num_scalar_prefetch=1,
            grid=(4,),
            in_specs=[whole(array) for array in operands]
            + [
                pl.BlockSpec(
                    (width, width), lambda i, at: (0, jnp.minimum(chunk_at(i, at[0]), 2))
                )
            ],
            out_specs=[pl.BlockSpec((span, width), lambda i, at: (0, 0))] * 3
            + [
                pl.BlockSpec((1, width, width), lambda i, at: (jnp.minimum(i, 1), 0, 0)),
                pl.BlockSpec((1, width, width), lambda i, at: (jnp.maximum(i - 2, 0), 0, 0)),
                pl.BlockSpec((8, width), lambda i, at: (0, 0)),
            ],
            scratch_shapes=[
                pltpu.VMEM((width, tokens), jnp.bfloat16),
                pltpu.VMEM((width, tokens), jnp.bfloat16),
                pltpu.VMEM((tokens, width), jnp.bfloat16),
                pltpu.VMEM((tokens, width), jnp.float32),
            ],
        ),
        out_shape=[jax.ShapeDtypeStruct((span, width), jnp.bfloat16)] * 3
        + [jax.ShapeDtypeStruct((2, width, width), jnp.bfloat16)] * 2
        + [jax.ShapeDtypeStruct((8, width), jnp.float32)],
        compiler_params=pltpu.CompilerParams(vmem_limit_bytes=VMEM_LIMIT),
        cost_estimate=pl.CostEstimate(
            flops=2 * tokens * 7 * width * width,
            bytes_accessed=2 * (18 * tokens * width + 7 * width * width),
            transcendentals=0,
        ),
    )(places, *operands, weight)


def swap(values, axis, bit):
    count = lax.axis_size(axis)
    return lax.ppermute(values, axis, [(i, i ^ bit) for i in range(count)])


def bit_of(axis, bit):
    return (lax.axis_index(axis) // bit) % 2


def batch_bits():
    count = lax.axis_size("batch")
    bits = []
    bit = 1
    while bit < count:
        bits.append(bit)
        bit *= 2
    return bits


def split_orders():
    bits = batch_bits()
    chip = ("seq", 2)
    split = [("batch", b) for b in bits[:3]]
    rest = [("batch", b) for b in bits[3:]]
    return ([chip] + split, split[:1] + [chip] + split[1:], rest)


def position_in(order):
    place = jnp.int32(0)
    for axis, bit in order:
        place = place * 2 + bit_of(axis, bit)
    return place


def total_of(parts):
    total = parts[0].astype(jnp.float32)
    for part in parts[1:]:
        total = total + part.astype(jnp.float32)
    return total.astype(jnp.bfloat16)


def scatter_group(first, second, order, rest):
    parts = [(first, 0), (second, 0)]
    rows = first.shape[0]
    for axis, bit in order:
        rows //= 2
        mine = bit_of(axis, bit)
        send = total_of(
            [lax.dynamic_slice_in_dim(p, at + (1 - mine) * rows, rows, 0) for p, at in parts]
        )
        parts = [(p, at + mine * rows) for p, at in parts] + [(swap(send, axis, bit), 0)]
    held = total_of([lax.dynamic_slice_in_dim(p, at, rows, 0) for p, at in parts])
    for axis, bit in rest:
        held = total_of([held, swap(held, axis, bit)])
    return held


def gather_group(held, order):
    blocks = held[None]
    for axis, bit in reversed(order):
        blocks = jnp.concatenate([blocks, swap(blocks, axis, bit)], axis=0)
    return blocks


def sync_piece(send, keep):
    order_a, order_b, rest = split_orders()
    got = swap(send, "seq", 1)
    out = []
    for g, order in ((0, order_a), (1, order_b)):
        held = scatter_group(keep[g], got[g], order, rest)
        full = gather_group(held, order)
        out.append((full, swap(full, "seq", 1)))
    (own_a, far_a), (own_b, far_b) = out
    return own_a, own_b, far_a, far_b


def place_scalars():
    order_a, order_b, _ = split_orders()
    return jnp.stack(
        [lax.axis_index("seq") % 2, position_in(order_a), position_in(order_b)]
    ).astype(jnp.int32)


def chunk_at(step, core):
    return jnp.where(step < 2, 2 * (1 - core) + step, 2 * core + step - 2)


def spread_blocks(places_ref, blocks_ref, group, out_ref):
    count, rows, _ = blocks_ref.shape
    for j in range(count):
        row = pl.multiple_of((places_ref[1 + group] ^ j) * rows, 16)
        out_ref[pl.ds(row, rows), :] = blocks_ref[j].astype(jnp.float32)


def finish_kernel(places_ref, own_a, own_b, far_a, far_b, out_ref):
    step = pl.program_id(0)
    for k, (ref, group) in enumerate(((own_a, 0), (own_b, 1), (far_a, 0), (far_b, 1))):

        @pl.when(step == k)
        def _(ref=ref, group=group):
            spread_blocks(places_ref, ref, group, out_ref)


def finish_two_kernel(places_ref, own_a, own_b, far_a, far_b, merged_ref, out_ref):
    step = pl.program_id(0)
    chunk = chunk_at(step, 1 - places_ref[0])
    for k, (ref, group) in enumerate(((own_a, 0), (own_b, 1), (far_a, 0), (far_b, 1))):

        @pl.when((step == k) & (chunk < 3))
        def _(ref=ref, group=group):
            spread_blocks(places_ref, ref, group, merged_ref)

        @pl.when((step == k) & (chunk == 3))
        def _(ref=ref, group=group):
            spread_blocks(places_ref, ref, group, out_ref)


def finish_piece(places, pieces, kind):
    count, rows, width = pieces[0].shape
    whole = pl.BlockSpec((count, rows, width), lambda i, at: (0, 0, 0))
    side = count * rows

    def own_first(i, at):
        return chunk_at(i, 1 - at[0])

    if kind == "rows":
        kernel = finish_kernel
        out_specs = pl.BlockSpec((side, width), lambda i, at: (own_first(i, at), 0))
        out_shape = jax.ShapeDtypeStruct((4 * side, width), jnp.float32)
    elif kind == "columns":
        kernel = finish_kernel
        out_specs = pl.BlockSpec((side, width), lambda i, at: (0, own_first(i, at)))
        out_shape = jax.ShapeDtypeStruct((side, 4 * width), jnp.float32)
    else:
        kernel = finish_two_kernel
        out_specs = [
            pl.BlockSpec((side, width), lambda i, at: (0, jnp.minimum(own_first(i, at), 2))),
            pl.BlockSpec((side, width), lambda i, at: (0, 0)),
        ]
        out_shape = [
            jax.ShapeDtypeStruct((side, 3 * width), jnp.float32),
            jax.ShapeDtypeStruct((side, width), jnp.float32),
        ]
    return pl.pallas_call(
        kernel,
        grid_spec=pltpu.PrefetchScalarGridSpec(
            num_scalar_prefetch=1, grid=(4,), in_specs=[whole] * 4, out_specs=out_specs
        ),
        out_shape=out_shape,
        compiler_params=pltpu.CompilerParams(vmem_limit_bytes=VMEM_LIMIT),
        cost_estimate=pl.CostEstimate(
            flops=0, bytes_accessed=6 * 4 * side * width, transcendentals=0
        ),
    )(places, *pieces)


def sum_small(vectors, mod_rows, cond):
    rows = vectors.shape[0]
    both = jnp.concatenate([vectors, mod_rows.reshape(-1, vectors.shape[1])], axis=0)
    for bit in (1, 2):
        both = both + swap(both, "seq", bit)
    vectors, own = both[:rows], both[rows:]
    everyone, conds = own, cond
    for bit in batch_bits():
        got = swap(jnp.concatenate([vectors, everyone], axis=0), "batch", bit)
        vectors = vectors + got[:rows]
        everyone = jnp.concatenate([everyone, got[rows:]], axis=0)
        conds = jnp.concatenate([conds, swap(conds, "batch", bit)], axis=0)
    return vectors, own.reshape(cond.shape[0], -1), everyone.reshape(conds.shape[0], -1), conds


def pick(values, index):
    return lax.dynamic_index_in_dim(values, index, 0, keepdims=False)


def rows_of(own, other, third, chip):
    first = jnp.where(chip == 0, own, other)
    second = jnp.where(chip == 0, other, own)
    return jnp.stack([first, second, third])


def shards(
    hidden,
    cond,
    lengths,
    ln1_gain,
    w_qkv,
    w_out,
    ln2_gain,
    w_fc1,
    b_fc1,
    w_fc2,
    b_fc2,
    w_ada,
    b_ada,
    cotangent,
):
    row_count, span, width = hidden.shape
    places = place_scalars()
    seat = lax.axis_index("seq")
    chip = seat // 2
    bases = jnp.stack([seat, seat ^ 2, seat ^ 1, seat ^ 3]) * span
    layout = jnp.concatenate(
        [pick(lengths, chip).reshape(-1), lengths[2], bases.astype(jnp.int32)]
    )
    hidden_far = swap(pick(hidden, 1 - chip), "seq", 2)
    blocks = [pick(hidden, chip), hidden_far, hidden[2]]
    ada_full = w_ada.astype(jnp.float32)
    modulation = (
        jnp.dot(cond, ada_full, precision=highest, preferred_element_type=jnp.float32) + b_ada
    )
    mod = jnp.stack([pick(modulation, chip), modulation[2]]).reshape(2, 6, width)
    gain_one, gain_two = ln1_gain[None], ln2_gain[None]

    normed_own, normed_split, query_own, query_split, kv_own, kv_split, angle_own, angle_split = (
        project(layout, [blocks[0], blocks[2]], mod, gain_one, w_qkv, (0, 1), (0, 0))
    )
    split_chip = swap(kv_split, "seq", 2)
    split_core = swap(kv_split, "seq", 1)
    split_cross = swap(split_chip, "seq", 1)
    own_core = swap(kv_own, "seq", 1)
    normed_far, query_far, kv_far, angle_far = project(
        layout, [blocks[1]], mod, gain_one, w_qkv, (0,), (1,)
    )
    far_core = swap(kv_far, "seq", 1)
    cotan_far = swap(pick(cotangent, 1 - chip), "seq", 2)
    cotan = [pick(cotangent, chip), cotan_far, cotangent[2]]
    kv_row = [kv_own, kv_far, own_core, far_core]
    kv_third = [kv_split, split_chip, split_core, split_cross]
    mixed_own, mixed_far, logsum_own, logsum_far = attend(
        layout, [query_own, query_far], kv_row, 0
    )
    mixed_split, logsum_split = attend(layout, [query_split], kv_third, 1)
    mixed = [mixed_own, mixed_far, mixed_split]
    (
        result_own,
        result_far,
        result_split,
        mixed_grad_own,
        mixed_grad_far,
        mixed_grad_split,
        resid_grad,
        low,
        send_one,
        keep_one,
        send_two,
        keep_two,
        b_one_grad,
        feed_sums,
    ) = feed(
        places,
        mixed,
        blocks,
        cotan,
        mod,
        gain_two,
        w_out,
        w_fc1,
        b_fc1[None],
        w_fc2,
        b_fc2[None],
    )
    fc2_pieces = sync_piece(send_two, keep_two)
    fc1_pieces = sync_piece(send_one, keep_one)
    output = rows_of(result_own, swap(result_far, "seq", 2), result_split, chip)

    query_grad_split, near_split, far_split = attend_back(
        layout, [query_split], [mixed_split], [mixed_grad_split], [logsum_split], kv_third, 1
    )
    got_split = swap(far_split, "seq", 1)
    chip_sum = (near_split[1] + got_split[1].astype(jnp.float32)).astype(jnp.bfloat16)
    got_chip = swap(chip_sum, "seq", 2)
    query_grad_own, query_grad_far, near_own, far_own = attend_back(
        layout,
        [query_own, query_far],
        [mixed_own, mixed_far],
        [mixed_grad_own, mixed_grad_far],
        [logsum_own, logsum_far],
        kv_row,
        0,
    )
    got_own = swap(far_own, "seq", 1)
    hidden_own_grad, hidden_far_grad, hidden_split_grad, send_att, keep_att, merge_sums = merge_back(
        places,
        [query_grad_own, query_grad_far, query_grad_split],
        [near_own, got_own, near_split, got_split, got_chip],
        [angle_own, angle_far, angle_split],
        [normed_own, normed_far, normed_split],
        mixed,
        blocks,
        low,
        resid_grad,
        mod,
        gain_one,
        w_qkv,
    )
    att_pieces = sync_piece(send_att, keep_att)
    hidden_grad = rows_of(hidden_own_grad, swap(hidden_far_grad, "seq", 2), hidden_split_grad, chip)

    vectors = jnp.concatenate(
        [merge_sums[0:1], feed_sums[0:1], feed_sums[1:2], b_one_grad.reshape(-1, width)], axis=0
    )

    def mod_row(group):
        at = 2 + 4 * group
        return jnp.concatenate(
            [
                merge_sums[1 + 2 * group : 3 + 2 * group],
                feed_sums[at : at + 4],
            ],
            axis=0,
        )

    row_own, row_split = mod_row(0), mod_row(1)
    nothing = jnp.zeros_like(row_own)
    mod_local = jnp.stack(
        [
            jnp.where(chip == 0, row_own, nothing),
            jnp.where(chip == 0, nothing, row_own),
            row_split,
        ]
    )
    vectors, mod_total, mod_all, cond_all = sum_small(vectors, mod_local, cond)
    ada_grad = jnp.dot(cond_all.T, mod_all, precision=highest, preferred_element_type=jnp.float32)
    cond_grad = jnp.dot(
        mod_total, ada_full.T, precision=highest, preferred_element_type=jnp.float32
    )
    qkv_grad, out_grad = finish_piece(places, att_pieces, "both")
    return (
        output,
        hidden_grad,
        cond_grad,
        vectors[0],
        qkv_grad,
        out_grad,
        vectors[1],
        finish_piece(places, fc1_pieces, "columns"),
        vectors[3:].reshape(-1),
        finish_piece(places, fc2_pieces, "rows"),
        vectors[2],
        ada_grad,
        jnp.sum(mod_all, axis=0),
    )


def solution(mesh):
    return jax.shard_map(
        shards,
        mesh=mesh,
        in_specs=(
            P("batch", "seq", None),
            P("batch", None),
            P("batch", None),
            P(),
            P(),
            P(),
            P(),
            P(),
            P(),
            P(),
            P(),
            P(),
            P(),
            P("batch", "seq", None),
        ),
        out_specs=(
            P("batch", "seq", None),
            P("batch", "seq", None),
            P("batch", None),
            P(),
            P(),
            P(),
            P(),
            P(),
            P(),
            P(),
            P(),
            P(),
            P(),
        ),
        check_vma=False,
    )
```

```python
import functools

import jax
import jax.numpy as jnp
from jax import lax
from jax.experimental import pallas as pl
from jax.experimental.pallas import tpu as pltpu
from jax.sharding import PartitionSpec as P

HEADS = 12
HEAD = 64
DOCS = 8
LANES = 128
GELU_A = 0.7978845608
GELU_B = 0.044715
VMEM_LIMIT = 60 * 2**20


highest = lax.Precision.HIGHEST


def dot_nt(left, right):
    return lax.dot_general(
        left, right, (((1,), (1,)), ((), ())), preferred_element_type=jnp.float32
    )


def dot_tn(left, right):
    return lax.dot_general(
        left, right, (((0,), (0,)), ((), ())), preferred_element_type=jnp.float32
    )


def dot_nn(left, right):
    return jnp.dot(left, right, preferred_element_type=jnp.float32)


def column_sum(values):
    return jnp.sum(values, axis=0, keepdims=True)


def row_mean(values):
    return jnp.mean(values, axis=-1, keepdims=True)


def normalized(values):
    center = values - row_mean(values)
    inverse = lax.rsqrt(row_mean(center * center) + 1e-05)
    return center * inverse, inverse


def documents_of(slots, layout_ref, group):
    end = jnp.int32(0)
    segment = jnp.zeros_like(slots)
    start = jnp.zeros_like(slots)
    for i in range(DOCS):
        length = layout_ref[group * DOCS + i]
        end = end + length
        passed = slots >= end
        segment = segment + passed.astype(jnp.int32)
        start = start + jnp.where(passed, length, 0)
    return segment, slots - start


def base_of(layout_ref, block):
    return layout_ref[2 * DOCS + block]


def slots_of(layout_ref, block, span):
    return base_of(layout_ref, block) + lax.broadcasted_iota(jnp.int32, (1, span), 1)


def segments_of(layout_ref, block, group, span):
    segment, _ = documents_of(slots_of(layout_ref, block, span), layout_ref, group)
    return segment.astype(jnp.float32)


def as_column(row):
    return jnp.broadcast_to(row, (LANES, row.shape[1])).T


def turned(values, cosine, sine):
    lanes = lax.broadcasted_iota(jnp.int32, cosine.shape, 1)
    first = lanes % HEAD < HEAD // 2
    pieces = []
    for c in range(values.shape[1] // LANES):
        u = values[:, c * LANES : (c + 1) * LANES]
        other = jnp.where(
            first, pltpu.roll(u, LANES - HEAD // 2, 1), pltpu.roll(u, HEAD // 2, 1)
        )
        pieces.append(u * cosine + other * sine)
    return pieces


def project_kernel(groups, bases, layout_ref, *refs):
    count = len(groups)
    hidden = refs[:count]
    mod_ref, gain_ref, speed_ref, weight_ref = refs[count : count + 4]
    normed = refs[count + 4 : 2 * count + 4]
    query = refs[2 * count + 4 : 3 * count + 4]
    keyval = refs[3 * count + 4 : 4 * count + 4]
    angle = refs[4 * count + 4 : 5 * count + 4]
    step = pl.program_id(0)
    span = hidden[0].shape[0]

    @pl.when(step == 0)
    def _():
        for b in range(count):
            values, _ = normalized(hidden[b][...].astype(jnp.float32))
            scale = mod_ref[groups[b], 1:2, :]
            shift = mod_ref[groups[b], 0:1, :]
            normed[b][...] = (values * gain_ref[...] * (1.0 + scale) + shift).astype(jnp.bfloat16)
            _, place = documents_of(slots_of(layout_ref, bases[b], span), layout_ref, groups[b])
            angles = speed_ref[...][:, :1] * place.astype(jnp.float32)
            sine, cosine = jnp.sin(angles), jnp.cos(angles)
            angle[b][0] = jnp.concatenate([cosine] * 4, axis=0).T
            angle[b][1] = jnp.concatenate([-sine, sine] * 2, axis=0).T

    for b in range(count):
        merged = dot_nn(normed[b][...], weight_ref[...])

        @pl.when(step == 0)
        def _(b=b, merged=merged):
            for c, piece in enumerate(turned(merged, angle[b][0], angle[b][1])):
                query[b][:, c * LANES : (c + 1) * LANES] = (piece * 0.125).astype(jnp.bfloat16)

        @pl.when(step == 1)
        def _(b=b, merged=merged):
            for c, piece in enumerate(turned(merged, angle[b][0], angle[b][1])):
                keyval[b][c, :, :LANES] = piece.astype(jnp.bfloat16)

        @pl.when(step == 2)
        def _(b=b, merged=merged):
            for c in range(merged.shape[1] // LANES):
                keyval[b][c, :, LANES:] = merged[:, c * LANES : (c + 1) * LANES].astype(
                    jnp.bfloat16
                )


def speeds():
    half = 10000.0 ** (-jnp.arange(HEAD // 2, dtype=jnp.float32) * 2.0 / HEAD)
    return jnp.tile(half[:, None], (1, LANES))


def project(layout, hidden, mod, gain, weight, groups, bases):
    count = len(hidden)
    span, width = hidden[0].shape
    pairs = width // LANES
    whole = pl.BlockSpec((span, width), lambda i, at: (0, 0))
    return pl.pallas_call(
        functools.partial(project_kernel, groups, bases),
        grid_spec=pltpu.PrefetchScalarGridSpec(
            num_scalar_prefetch=1,
            grid=(3,),
            in_specs=[whole] * count
            + [
                pl.BlockSpec(mod.shape, lambda i, at: (0, 0, 0)),
                pl.BlockSpec(gain.shape, lambda i, at: (0, 0)),
                pl.BlockSpec((HEAD // 2, LANES), lambda i, at: (0, 0)),
                pl.BlockSpec((width, width), lambda i, at: (0, i)),
            ],
            out_specs=[whole] * (2 * count)
            + [pl.BlockSpec((pairs, span, 2 * LANES), lambda i, at: (0, 0, 0))] * count
            + [pl.BlockSpec((2, span, LANES), lambda i, at: (0, 0, 0))] * count,
        ),
        out_shape=[jax.ShapeDtypeStruct((span, width), jnp.bfloat16)] * (2 * count)
        + [jax.ShapeDtypeStruct((pairs, span, 2 * LANES), jnp.bfloat16)] * count
        + [jax.ShapeDtypeStruct((2, span, LANES), jnp.float32)] * count,
        compiler_params=pltpu.CompilerParams(vmem_limit_bytes=VMEM_LIMIT),
        cost_estimate=pl.CostEstimate(
            flops=6 * count * span * width * width,
            bytes_accessed=2 * (5 * count * span * width + 3 * width * width),
            transcendentals=0,
        ),
    )(layout, *hidden, mod, gain, speeds(), weight)


def one_head(values, head):
    lanes = lax.broadcasted_iota(jnp.int32, values.shape, 1)
    return jnp.where(lanes // HEAD == head, values, jnp.zeros_like(values))


def stacked(keyval, pair, lanes):
    return jnp.concatenate([ref[pair, :, lanes] for ref in keyval], axis=0)


KEYS, VALUES = slice(0, LANES), slice(LANES, 2 * LANES)


def attend_kernel(group, first, layout_ref, query, *refs):
    keyval = refs[:4]
    mixed, logsum, bias_ref = refs[4:]
    span = query.shape[0]

    @pl.when(pl.program_id(0) == 0)
    def _():
        column = as_column(segments_of(layout_ref, first, group, span))
        for k in range(4):
            row = segments_of(layout_ref, k, group, span)
            for c in range(0, span, LANES):
                bias_ref[:, k * span + c : k * span + c + LANES] = jnp.where(
                    column == row[:, c : c + LANES], 0.0, -1e30
                )

    lanes = lax.broadcasted_iota(jnp.int32, (span, LANES), 1)
    for p in range(keyval[0].shape[0]):
        here = slice(p * LANES, (p + 1) * LANES)
        keys = stacked(keyval, p, KEYS)
        values = stacked(keyval, p, VALUES)
        scores = [dot_nt(one_head(query[:, here], h), keys) for h in range(2)]
        sums, tops = [], []
        for h in range(2):
            biased = scores[h] + bias_ref[...]
            peak = jnp.max(biased, axis=1, keepdims=True)
            expo = jnp.exp(biased - peak)
            total = jnp.sum(expo, axis=1, keepdims=True)
            sums.append(dot_nn(expo.astype(jnp.bfloat16), values) / total)
            tops.append(peak + jnp.log(total))
        mixed[:, here] = jnp.where(lanes < HEAD, sums[0], sums[1]).astype(jnp.bfloat16)
        logsum[p] = jnp.where(lanes == 0, tops[0], tops[1]).T[:2, :]


def attend(layout, query, keyval, group, first):
    span, width = query.shape
    pairs = width // LANES
    some = 2
    by_pair = pl.BlockSpec((span, some * LANES), lambda i, at: (0, i))
    return pl.pallas_call(
        functools.partial(attend_kernel, group, first),
        grid_spec=pltpu.PrefetchScalarGridSpec(
            num_scalar_prefetch=1,
            grid=(pairs // some,),
            in_specs=[by_pair]
            + [pl.BlockSpec((some, span, 2 * LANES), lambda i, at: (i, 0, 0))] * 4,
            out_specs=[by_pair, pl.BlockSpec((some, 2, span), lambda i, at: (i, 0, 0))],
            scratch_shapes=[pltpu.VMEM((span, 4 * span), jnp.float32)],
        ),
        out_shape=[
            jax.ShapeDtypeStruct((span, width), jnp.bfloat16),
            jax.ShapeDtypeStruct((pairs, 2, span), jnp.float32),
        ],
        compiler_params=pltpu.CompilerParams(vmem_limit_bytes=VMEM_LIMIT),
        cost_estimate=pl.CostEstimate(
            flops=16 * span * 4 * span * width,
            bytes_accessed=20 * span * width,
            transcendentals=0,
        ),
    )(layout, query, *keyval)


def attend_back_kernel(group, count, layout_ref, *refs):
    refs = list(refs)

    def take(number):
        taken = refs[:number]
        del refs[:number]
        return taken

    query, mixed, grad = take(count), take(count), take(count)
    logsum, angle, keyval = take(count), take(count), take(4)
    query_grad = take(count)
    near_ref, far_ref, bias_ref = refs
    span = query[0].shape[0]

    @pl.when(pl.program_id(0) == 0)
    def _():
        for k in range(4):
            column = as_column(segments_of(layout_ref, k, group, span))
            for q in range(count):
                row = segments_of(layout_ref, q, group, span)
                for c in range(0, span, LANES):
                    bias_ref[q, k * span : (k + 1) * span, c : c + LANES] = jnp.where(
                        column == row[:, c : c + LANES], 0.0, -1e30
                    )

    for p in range(keyval[0].shape[0]):
        here = slice(p * LANES, (p + 1) * LANES)
        keys = stacked(keyval, p, KEYS)
        values = stacked(keyval, p, VALUES)
        keys_turned = jnp.concatenate([ref[p, :, KEYS].T for ref in keyval], axis=1)
        key_grad = value_grad = None
        for q in range(count):
            weighed = mixed[q][:, here].astype(jnp.float32) * grad[q][:, here].astype(jnp.float32)
            weighed = weighed.T
            heads = []
            for h in range(2):
                chosen = one_head(query[q][:, here], h)
                chosen_grad = one_head(grad[q][:, here], h)
                own = slice(h * HEAD, (h + 1) * HEAD)
                delta = jnp.sum(weighed[own, :], axis=0, keepdims=True)
                scores = dot_nt(keys, chosen) + bias_ref[q]
                prob_grad = dot_nt(values, chosen_grad)
                probs = jnp.exp(scores - logsum[q][p, h : h + 1, :])
                term = dot_nn(probs.astype(jnp.bfloat16), chosen_grad)
                value_grad = term if value_grad is None else value_grad + term
                score_grad = (probs * (prob_grad - delta)).astype(jnp.bfloat16)
                term = dot_nn(score_grad, chosen)
                key_grad = term if key_grad is None else key_grad + term
                heads.append(dot_nn(keys_turned[own, :], score_grad))
            back = jnp.concatenate(heads, axis=0).T * 0.125
            (back,) = turned(back, angle[q][0], -angle[q][1])
            query_grad[q][:, here] = back.astype(jnp.bfloat16)
        for k in range(4):
            ref = near_ref if k < 2 else far_ref
            rows = slice(k * span, (k + 1) * span)
            ref[k % 2, p, :, KEYS] = key_grad[rows].astype(ref.dtype)
            ref[k % 2, p, :, VALUES] = value_grad[rows].astype(ref.dtype)


def attend_back(
    layout, query, mixed, grad, logsum, angle, keyval, group, first=0, last=None, some=1
):
    count = len(query)
    span, width = query[0].shape
    pairs = (last or width // LANES) - first
    start = first // some
    by_pair = pl.BlockSpec((span, some * LANES), lambda i, at: (0, start + i))
    two_blocks = pl.BlockSpec((2, some, span, 2 * LANES), lambda i, at: (0, i, 0, 0))
    two_shape = jax.ShapeDtypeStruct((2, pairs, span, 2 * LANES), jnp.bfloat16)
    return pl.pallas_call(
        functools.partial(attend_back_kernel, group, count),
        grid_spec=pltpu.PrefetchScalarGridSpec(
            num_scalar_prefetch=1,
            grid=(pairs // some,),
            in_specs=[by_pair] * (3 * count)
            + [pl.BlockSpec((some, 2, span), lambda i, at: (start + i, 0, 0))] * count
            + [pl.BlockSpec((2, span, LANES), lambda i, at: (0, 0, 0))] * count
            + [pl.BlockSpec((some, span, 2 * LANES), lambda i, at: (start + i, 0, 0))] * 4,
            out_specs=[pl.BlockSpec((span, some * LANES), lambda i, at: (0, i))] * count
            + [two_blocks] * 2,
            scratch_shapes=[pltpu.VMEM((count, 4 * span, span), jnp.float32)],
        ),
        out_shape=[jax.ShapeDtypeStruct((span, pairs * LANES), jnp.bfloat16)] * count
        + [two_shape] * 2,
        compiler_params=pltpu.CompilerParams(vmem_limit_bytes=VMEM_LIMIT),
        cost_estimate=pl.CostEstimate(
            flops=40 * count * span * 4 * span * pairs * LANES,
            bytes_accessed=2 * (4 * count + 16) * span * pairs * LANES,
            transcendentals=0,
        ),
    )(layout, *query, *mixed, *grad, *logsum, *angle, *keyval)


def group_of(block):
    return 0 if block < 2 else 1


def feed_kernel(*refs):
    mixed, hidden, cotan = refs[0:3], refs[3:6], refs[6:9]
    mod_ref, gain_ref, w_out_ref, w_one_ref, b_one_ref, w_two_ref, b_two_ref = refs[9:16]
    result, mixed_grad = refs[16:19], refs[19:22]
    resid_ref, low_ref, chunks_ref, b_one_grad, sums_ref = refs[22:27]
    second_ref, turned_ref, branch_low_ref, branch_ref, second_grad_ref, act_ref, pre_ref = refs[27:]
    step = pl.program_id(0)
    span = hidden[0].shape[0]

    def modulation(block, which):
        return mod_ref[group_of(block), which : which + 1, :]

    @pl.when(step == 0)
    def _():
        bias_sum = None
        for b in range(3):
            rows = slice(b * span, (b + 1) * span)
            attended = dot_nn(mixed[b][...], w_out_ref[...])
            resid = hidden[b][...].astype(jnp.float32) + modulation(b, 2) * attended
            resid_ref[rows, :] = resid
            values, _ = normalized(resid)
            second = values * gain_ref[...] * (1.0 + modulation(b, 4)) + modulation(b, 3)
            second = second.astype(jnp.bfloat16)
            second_ref[rows, :] = second
            turned_ref[:, rows] = second.T
            branch_grad = modulation(b, 5) * cotan[b][...].astype(jnp.float32)
            branch_low_ref[rows, :] = branch_grad.astype(jnp.bfloat16)
            part = column_sum(branch_grad)
            bias_sum = part if bias_sum is None else bias_sum + part
        sums_ref[...] = jnp.zeros_like(sums_ref)
        sums_ref[1:2, :] = bias_sum
        branch_ref[...] = jnp.zeros_like(branch_ref)
        second_grad_ref[...] = jnp.zeros_like(second_grad_ref)

    b_one_grad[...] = jnp.zeros_like(b_one_grad)

    for b in range(3):
        rows = slice(b * span, (b + 1) * span)
        pre = dot_nn(second_ref[rows, :], w_one_ref[...]) + b_one_ref[...]
        square = pre * pre
        tanh = jnp.tanh(GELU_A * pre * (1.0 + GELU_B * square))
        half = 0.5 * (1.0 + tanh)
        active = (pre * half).astype(jnp.bfloat16)
        act_ref[rows, :] = active
        branch_ref[rows, :] += dot_nn(active, w_two_ref[...])
        slope = half + 0.5 * GELU_A * pre * (1.0 - tanh * tanh) * (1.0 + 3.0 * GELU_B * square)
        pre_grad = dot_nt(branch_low_ref[rows, :], w_two_ref[...]) * slope
        b_one_grad[0] += column_sum(pre_grad)
        pre_low = pre_grad.astype(jnp.bfloat16)
        pre_ref[rows, :] = pre_low
        second_grad_ref[rows, :] += dot_nt(pre_low, w_one_ref[...])

    chunks_ref[0, 0] = dot_nn(turned_ref[...], pre_ref[...]).astype(jnp.bfloat16)
    chunks_ref[0, 1] = dot_tn(act_ref[...], branch_low_ref[...]).astype(jnp.bfloat16)

    @pl.when(step == 3)
    def _():
        for b in range(3):
            at = 2 + 4 * group_of(b)
            rows = slice(b * span, (b + 1) * span)
            resid = resid_ref[rows, :]
            branch = branch_ref[rows, :] + b_two_ref[...]
            result[b][...] = (resid + modulation(b, 5) * branch).astype(jnp.bfloat16)
            upstream = cotan[b][...].astype(jnp.float32)
            sums_ref[at + 3 : at + 4, :] += column_sum(upstream * branch)
            values, inverse = normalized(resid)
            grad = second_grad_ref[rows, :]
            sums_ref[at + 1 : at + 2, :] += column_sum(grad)
            weighed = column_sum(grad * values)
            sums_ref[at + 2 : at + 3, :] += weighed * gain_ref[...]
            sums_ref[0:1, :] += weighed * (1.0 + modulation(b, 4))
            inner = grad * ((1.0 + modulation(b, 4)) * gain_ref[...])
            back = (inner - row_mean(inner) - values * row_mean(inner * values)) * inverse
            resid_grad = upstream + back
            resid_ref[rows, :] = resid_grad
            attended = dot_nn(mixed[b][...], w_out_ref[...])
            sums_ref[at : at + 1, :] += column_sum(resid_grad * attended)
            low = (modulation(b, 2) * resid_grad).astype(jnp.bfloat16)
            low_ref[rows, :] = low
            mixed_grad[b][...] = dot_nt(low, w_out_ref[...]).astype(jnp.bfloat16)


def feed(mixed, hidden, cotan, mod, gain, w_out, w_one, b_one, w_two, b_two):
    span, width = hidden[0].shape
    tokens = 3 * span
    once = pl.Buffered(1)
    block = pl.BlockSpec((span, width), lambda i: (0, 0), pipeline_mode=once)
    out_block = pl.BlockSpec((span, width), lambda i: (0, 0))
    every = pl.BlockSpec((tokens, width), lambda i: (0, 0))
    row = pl.BlockSpec((1, width), lambda i: (0, 0))
    chunk = pl.BlockSpec((1, 2, width, width), lambda i: (i, 0, 0, 0))
    low_block = jax.ShapeDtypeStruct((span, width), jnp.bfloat16)
    chunks = jax.ShapeDtypeStruct((4, 2, width, width), jnp.bfloat16)
    return pl.pallas_call(
        feed_kernel,
        grid_spec=pl.GridSpec(
            grid=(4,),
            in_specs=[block] * 9
            + [
                pl.BlockSpec(mod.shape, lambda i: (0, 0, 0)),
                row,
                pl.BlockSpec((width, width), lambda i: (0, 0), pipeline_mode=once),
                pl.BlockSpec((width, width), lambda i: (0, i)),
                pl.BlockSpec((1, width), lambda i: (0, i)),
                pl.BlockSpec((width, width), lambda i: (i, 0)),
                row,
            ],
            out_specs=[out_block] * 6
            + [every, every, chunk]
            + [
                pl.BlockSpec((1, 1, width), lambda i: (i, 0, 0)),
                pl.BlockSpec((16, width), lambda i: (0, 0)),
            ],
            scratch_shapes=[
                pltpu.VMEM((tokens, width), jnp.bfloat16),
                pltpu.VMEM((width, tokens), jnp.bfloat16),
                pltpu.VMEM((tokens, width), jnp.bfloat16),
                pltpu.VMEM((tokens, width), jnp.float32),
                pltpu.VMEM((tokens, width), jnp.float32),
                pltpu.VMEM((tokens, width), jnp.bfloat16),
                pltpu.VMEM((tokens, width), jnp.bfloat16),
            ],
        ),
        out_shape=[low_block] * 6
        + [
            jax.ShapeDtypeStruct((tokens, width), jnp.float32),
            jax.ShapeDtypeStruct((tokens, width), jnp.bfloat16),
        ]
        + [chunks]
        + [
            jax.ShapeDtypeStruct((4, 1, width), jnp.float32),
            jax.ShapeDtypeStruct((16, width), jnp.float32),
        ],
        compiler_params=pltpu.CompilerParams(vmem_limit_bytes=VMEM_LIMIT),
        cost_estimate=pl.CostEstimate(
            flops=2 * tokens * 26 * width * width,
            bytes_accessed=2 * (14 * tokens * width + 17 * width * width),
            transcendentals=0,
        ),
    )(*mixed, *hidden, *cotan, mod, gain, w_out, w_one, b_one, w_two, b_two)


def merge_kernel(parts, places_ref, *refs):
    refs = list(refs)

    def take(count):
        taken = refs[:count]
        del refs[:count]
        return taken

    own_parts = [(first, last, take(4)) for first, last in parts[0]]
    split_parts = [(first, last, take(4)) for first, last in parts[1]]
    angle, normed, mixed = take(3), take(3), take(3)
    low_ref, send_ref, keep_ref, merged_ref, normed_ref, mixed_ref = refs
    step = pl.program_id(0)
    chunk = chunk_at(step, places_ref[0])
    span, width = normed[0].shape
    pairs = width // LANES

    @pl.when(step == 0)
    def _():
        for b in range(3):
            rows = slice(b * span, (b + 1) * span)
            normed_ref[:, rows] = normed[b][...].T
            mixed_ref[:, rows] = mixed[b][...].T

    def part_of(block, pair):
        for first, last, arrays in split_parts if block == 2 else own_parts:
            if first <= pair < last:
                return pair - first, arrays

    def keyval_sum(block, pair, lanes):
        at, arrays = part_of(block, pair)
        if block == 2:
            _, near, got, got_chip = arrays
            terms = near[0, at, :, lanes], got[0, at, :, lanes], got_chip[at, :, lanes]
        else:
            _, _, near, got = arrays
            terms = near[block, at, :, lanes], got[block, at, :, lanes]
        return sum(term.astype(jnp.float32) for term in terms)

    def put(result):
        @pl.when(step < 2)
        def _():
            send_ref[0] = result

        @pl.when(step >= 2)
        def _():
            keep_ref[0] = result

    for b in range(3):
        rows = slice(b * span, (b + 1) * span)
        for c in range(pairs):
            lanes = slice(c * LANES, (c + 1) * LANES)

            @pl.when(chunk == 0)
            def _(b=b, c=c, rows=rows, lanes=lanes):
                at, arrays = part_of(b, c)
                merged_ref[rows, lanes] = arrays[b % 2][:, at * LANES : (at + 1) * LANES]

            @pl.when(chunk == 1)
            def _(b=b, c=c, rows=rows, lanes=lanes):
                (piece,) = turned(keyval_sum(b, c, KEYS), angle[b][0], -angle[b][1])
                merged_ref[rows, lanes] = piece.astype(jnp.bfloat16)

            @pl.when(chunk == 2)
            def _(b=b, c=c, rows=rows, lanes=lanes):
                merged_ref[rows, lanes] = keyval_sum(b, c, VALUES).astype(jnp.bfloat16)

    @pl.when(chunk < 3)
    def _():
        put(dot_nn(normed_ref[...], merged_ref[...]).astype(jnp.bfloat16))

    @pl.when(chunk == 3)
    def _():
        put(dot_nn(mixed_ref[...], low_ref[...]).astype(jnp.bfloat16))


def merge_back(places, own_parts, split_parts, angle, normed, mixed, low):
    span, width = normed[0].shape
    tokens = 3 * span
    once = pl.Buffered(1)

    def whole(array):
        return pl.BlockSpec(
            array.shape, lambda i, at: (0,) * len(array.shape), pipeline_mode=once
        )

    operands = [array for _, _, arrays in own_parts + split_parts for array in arrays]
    operands += [*angle, *normed, *mixed, low]
    parts = [[(first, last) for first, last, _ in group] for group in (own_parts, split_parts)]
    chunk_shape = jax.ShapeDtypeStruct((2, width, width), jnp.bfloat16)
    return pl.pallas_call(
        functools.partial(merge_kernel, parts),
        grid_spec=pltpu.PrefetchScalarGridSpec(
            num_scalar_prefetch=1,
            grid=(4,),
            in_specs=[whole(array) for array in operands],
            out_specs=[
                pl.BlockSpec((1, width, width), lambda i, at: (jnp.minimum(i, 1), 0, 0)),
                pl.BlockSpec((1, width, width), lambda i, at: (jnp.maximum(i - 2, 0), 0, 0)),
                pl.BlockSpec(
                    (tokens, width), lambda i, at: (0, jnp.minimum(chunk_at(i, at[0]), 2))
                ),
            ],
            scratch_shapes=[
                pltpu.VMEM((width, tokens), jnp.bfloat16),
                pltpu.VMEM((width, tokens), jnp.bfloat16),
            ],
        ),
        out_shape=[
            chunk_shape,
            chunk_shape,
            jax.ShapeDtypeStruct((tokens, 3 * width), jnp.bfloat16),
        ],
        compiler_params=pltpu.CompilerParams(vmem_limit_bytes=VMEM_LIMIT),
        cost_estimate=pl.CostEstimate(
            flops=2 * tokens * 4 * width * width,
            bytes_accessed=2 * (14 * tokens * width + 4 * width * width),
            transcendentals=0,
        ),
    )(places, *operands)


def enter_kernel(*refs):
    hidden = refs[0:3]
    resid_grad_ref, mod_ref, gain_ref, merged_ref, weight_ref = refs[3:8]
    hidden_grad = refs[8:11]
    sums_ref, total_ref = refs[11:]
    step = pl.program_id(0)
    span = hidden[0].shape[0]

    @pl.when(step == 0)
    def _():
        total_ref[...] = jnp.zeros_like(total_ref)

    total_ref[...] += dot_nt(merged_ref[...], weight_ref[...])

    @pl.when(step == 2)
    def _():
        sums_ref[...] = jnp.zeros_like(sums_ref)
        for b in range(3):
            group = group_of(b)
            at = 1 + 2 * group
            rows = slice(b * span, (b + 1) * span)
            values, inverse = normalized(hidden[b][...].astype(jnp.float32))
            grad = total_ref[rows, :]
            scaled = 1.0 + mod_ref[group, 1:2, :]
            weighed = column_sum(grad * values)
            sums_ref[0:1, :] += weighed * scaled
            sums_ref[at : at + 1, :] += column_sum(grad)
            sums_ref[at + 1 : at + 2, :] += weighed * gain_ref[...]
            inner = grad * (scaled * gain_ref[...])
            back = (inner - row_mean(inner) - values * row_mean(inner * values)) * inverse
            hidden_grad[b][...] = (resid_grad_ref[rows, :] + back).astype(jnp.bfloat16)


def enter_back(hidden, resid_grad, mod, gain, merged, weight):
    span, width = hidden[0].shape
    tokens = 3 * span
    once = pl.Buffered(1)
    block = pl.BlockSpec((span, width), lambda i: (0, 0), pipeline_mode=once)
    return pl.pallas_call(
        enter_kernel,
        grid=(3,),
        in_specs=[block] * 3
        + [
            pl.BlockSpec((tokens, width), lambda i: (0, 0), pipeline_mode=once),
            pl.BlockSpec(mod.shape, lambda i: (0, 0, 0)),
            pl.BlockSpec(gain.shape, lambda i: (0, 0)),
            pl.BlockSpec((tokens, width), lambda i: (0, i)),
            pl.BlockSpec((width, width), lambda i: (0, i)),
        ],
        out_specs=[pl.BlockSpec((span, width), lambda i: (0, 0))] * 3
        + [pl.BlockSpec((8, width), lambda i: (0, 0))],
        out_shape=[jax.ShapeDtypeStruct((span, width), jnp.bfloat16)] * 3
        + [jax.ShapeDtypeStruct((8, width), jnp.float32)],
        scratch_shapes=[pltpu.VMEM((tokens, width), jnp.float32)],
        compiler_params=pltpu.CompilerParams(vmem_limit_bytes=VMEM_LIMIT),
        cost_estimate=pl.CostEstimate(
            flops=2 * tokens * 3 * width * width,
            bytes_accessed=2 * (8 * tokens * width + 3 * width * width),
            transcendentals=0,
        ),
    )(*hidden, resid_grad, mod, gain, merged, weight)


def swap(values, axis, bit):
    count = lax.axis_size(axis)
    return lax.ppermute(values, axis, [(i, i ^ bit) for i in range(count)])


def bit_of(axis, bit):
    return (lax.axis_index(axis) // bit) % 2


def batch_bits():
    count = lax.axis_size("batch")
    bits = []
    bit = 1
    while bit < count:
        bits.append(bit)
        bit *= 2
    return bits


def split_orders():
    bits = batch_bits()
    chip = ("seq", 2)
    split = [("batch", b) for b in bits[:3]]
    rest = [("batch", b) for b in bits[3:]]
    return ([chip] + split, split[:1] + [chip] + split[1:], rest)


def place_scalars():
    order_a, order_b, _ = split_orders()
    bits = [bit_of(axis, bit) for axis, bit in order_a + order_b]
    return jnp.stack([lax.axis_index("seq") % 2, *bits]).astype(jnp.int32)


def bits_value(at, group, steps, first, last, flip):
    value = jnp.int32(0)
    for d in range(first, last):
        bit = at[1 + group * steps + d]
        if flip and d == last - 1:
            bit = 1 - bit
        value = value * 2 + bit
    return value


def total_kernel(counts, places_ref, *refs):
    inputs, outputs = refs[: sum(counts)], refs[sum(counts) :]
    start = 0
    for g, count in enumerate(counts):
        total = inputs[start][0].astype(jnp.float32)
        for ref in inputs[start + 1 : start + count]:
            total = total + ref[0].astype(jnp.float32)
        start += count
        if len(outputs) == 1:
            outputs[0][g] = total.astype(jnp.bfloat16)
        else:
            outputs[g][0] = total.astype(jnp.bfloat16)


def total_of_parts(places, parts, steps, done, flip, joint):
    rows = parts[0][0][0].shape[1] >> done
    width = parts[0][0][0].shape[2]
    cuts = max(1, rows // 192)
    rows //= cuts
    operands, specs = [], []
    for g, group in enumerate(parts):
        for array, lead, level in group:
            operands.append(array)
            specs.append(
                pl.BlockSpec(
                    (1, rows, width),
                    lambda i, at, g=g, lead=lead, level=level: (
                        lead,
                        bits_value(at, g, steps, level, done, flip) * cuts + i,
                        0,
                    ),
                )
            )
    if joint:
        out_specs = [pl.BlockSpec((2, rows, width), lambda i, at: (0, i, 0))]
        out_shape = [jax.ShapeDtypeStruct((2, cuts * rows, width), jnp.bfloat16)]
    else:
        out_specs = [pl.BlockSpec((1, rows, width), lambda i, at: (0, i, 0))] * 2
        out_shape = [jax.ShapeDtypeStruct((1, cuts * rows, width), jnp.bfloat16)] * 2
    return pl.pallas_call(
        functools.partial(total_kernel, [len(group) for group in parts]),
        grid_spec=pltpu.PrefetchScalarGridSpec(
            num_scalar_prefetch=1, grid=(cuts,), in_specs=specs, out_specs=out_specs
        ),
        out_shape=out_shape,
        compiler_params=pltpu.CompilerParams(vmem_limit_bytes=VMEM_LIMIT),
        cost_estimate=pl.CostEstimate(
            flops=0, bytes_accessed=2 * cuts * rows * width * (len(operands) + 2), transcendentals=0
        ),
    )(places, *operands)


def join_kernel(left_ref, right_ref, out_ref):
    count = left_ref.shape[1]
    out_ref[:, :count] = left_ref[...]
    out_ref[:, count:] = right_ref[...]


def join(left, right):
    lead, count, rows, width = left.shape
    spec = pl.BlockSpec((lead, count, rows, width), lambda i: (0, 0, 0, 0))
    return pl.pallas_call(
        join_kernel,
        grid=(1,),
        in_specs=[spec, spec],
        out_specs=pl.BlockSpec((lead, 2 * count, rows, width), lambda i: (0, 0, 0, 0)),
        out_shape=jax.ShapeDtypeStruct((lead, 2 * count, rows, width), left.dtype),
        compiler_params=pltpu.CompilerParams(vmem_limit_bytes=VMEM_LIMIT),
        cost_estimate=pl.CostEstimate(
            flops=0, bytes_accessed=8 * lead * count * rows * width, transcendentals=0
        ),
    )(left, right)


def after(values, *others):
    return lax.optimization_barrier((values, others))[0]


def sync_steps(places, send, keep, gather=True):
    order_a, order_b, rest = split_orders()
    steps = len(order_a)
    got = swap(send, "seq", 1)
    got = after(got, (yield [send]))
    parts = [[(keep, g, 0), (got, g, 0)] for g in range(2)]
    for done, dims in enumerate(zip(order_a, order_b), 1):
        joint = dims[0] == dims[1]
        sent = total_of_parts(places, parts, steps, done, True, joint)
        if joint:
            got = [swap(sent[0], *dims[0])] * 2
        else:
            got = [swap(sent[g], *dims[g]) for g in range(2)]
        got = after(got, (yield sent))
        for g in range(2):
            parts[g].append((got[g], g if joint else 0, done))
    (held,) = total_of_parts(places, parts, steps, steps, False, True)
    for axis, bit in rest:
        held = (held.astype(jnp.float32) + swap(held, axis, bit).astype(jnp.float32)).astype(
            held.dtype
        )
    if not gather:
        return held
    blocks = held[:, None]
    for dims in reversed(list(zip(order_a, order_b))):
        if dims[0] == dims[1]:
            got = swap(blocks, *dims[0])
            got = after(got, (yield [blocks]))
            blocks = join(blocks, got)
        else:
            if not isinstance(blocks, list):
                blocks = [blocks[0:1], blocks[1:2]]
            got = [swap(blocks[g], *dims[g]) for g in range(2)]
            got = after(got, (yield blocks))
            blocks = [join(blocks[g], got[g]) for g in range(2)]
    got = [swap(blocks[g], "seq", 1) for g in range(2)]
    got = after(got, (yield blocks))
    return [*blocks, *got]


class SmallSums:
    def __init__(self, vectors, mod_rows, cond):
        self.rows = vectors.shape[0]
        self.mod_rows = mod_rows.shape[0] * mod_rows.shape[1]
        self.both = jnp.concatenate(
            [vectors, mod_rows.reshape(-1, vectors.shape[1])], axis=0
        )
        spare = vectors.shape[1] - cond.size
        self.cond = jnp.pad(cond.reshape(-1), (0, spare))[None]
        self.dims = [("seq", 1), ("seq", 2)] + [("batch", b) for b in batch_bits()]
        self.everyone = self.pending = None

    def step(self, *done):
        self.take(*done)
        if not self.dims:
            return
        self.axis, bit = self.dims.pop(0)
        if self.axis == "seq":
            self.pending = swap(self.both, self.axis, bit)
            return
        if self.everyone is None:
            self.vectors, self.own = self.both[: self.rows], self.both[self.rows :]
            self.everyone = jnp.concatenate([self.own, self.cond], axis=0)[None]
        width = self.everyone.shape[2]
        self.pending = swap(
            jnp.concatenate([self.vectors, self.everyone.reshape(-1, width)], axis=0),
            self.axis,
            bit,
        )

    def take(self, *done):
        if self.pending is None:
            return
        got = after(self.pending, *done) if done else self.pending
        self.pending = None
        if self.axis == "seq":
            self.both = self.both + got
            return
        self.vectors = self.vectors + got[: self.rows]
        self.everyone = jnp.concatenate(
            [self.everyone, got[self.rows :].reshape(self.everyone.shape)], axis=0
        )

    def finish(self, *done):
        while self.dims:
            self.step(*done)
        self.take(*done)

    def results(self, cond):
        count = self.everyone.shape[0]
        rows = cond.shape[0]
        mod_all = self.everyone[:, : self.mod_rows].reshape(count * rows, -1)
        cond_all = self.everyone[:, self.mod_rows, : cond.size].reshape(count * rows, -1)
        return self.vectors, self.own.reshape(rows, -1), mod_all, cond_all


def run_on(steps, *done):
    try:
        return steps.send(done), None
    except StopIteration as end:
        return None, end.value


def chunk_at(step, core):
    return jnp.where(step < 2, 2 * (1 - core) + step, 2 * core + step - 2)


def spread_blocks(places_ref, blocks_ref, group, out_ref):
    _, count, rows, _ = blocks_ref.shape
    steps = count.bit_length() - 1
    place = bits_value(places_ref, group, steps, 0, steps, False)

    @pl.loop(0, count)
    def _(j):
        row = pl.multiple_of((place ^ j) * rows, 8)
        out_ref[pl.ds(row, rows), :] = blocks_ref[0, j].astype(jnp.float32)


def finish_feed_kernel(chunks_ref, one_ref, two_ref):
    one_ref[...] = chunks_ref[0, 0].astype(jnp.float32)
    two_ref[...] = chunks_ref[0, 1].astype(jnp.float32)


def finish_feed(chunks):
    count, _, width, _ = chunks.shape
    cuts = 2
    rows = width // cuts
    return pl.pallas_call(
        finish_feed_kernel,
        grid=(count, cuts),
        in_specs=[pl.BlockSpec((1, 2, rows, width), lambda i, j: (i, 0, j, 0))],
        out_specs=[
            pl.BlockSpec((rows, width), lambda i, j: (j, i)),
            pl.BlockSpec((rows, width), lambda i, j: (cuts * i + j, 0)),
        ],
        out_shape=[
            jax.ShapeDtypeStruct((width, count * width), jnp.float32),
            jax.ShapeDtypeStruct((count * width, width), jnp.float32),
        ],
        compiler_params=pltpu.CompilerParams(vmem_limit_bytes=VMEM_LIMIT),
        cost_estimate=pl.CostEstimate(
            flops=0, bytes_accessed=12 * count * width * width, transcendentals=0
        ),
    )(chunks)


def finish_attention_kernel(places_ref, own_a, own_b, far_a, far_b, merged_ref, out_ref):
    step = pl.program_id(0)
    chunk = chunk_at(step, 1 - places_ref[0])
    for k, (ref, group) in enumerate(((own_a, 0), (own_b, 1), (far_a, 0), (far_b, 1))):

        @pl.when((step == k) & (chunk < 3))
        def _(ref=ref, group=group):
            spread_blocks(places_ref, ref, group, merged_ref)

        @pl.when((step == k) & (chunk == 3))
        def _(ref=ref, group=group):
            spread_blocks(places_ref, ref, group, out_ref)


def finish_attention(places, pieces):
    _, count, rows, width = pieces[0].shape
    whole = pl.BlockSpec((1, count, rows, width), lambda i, at: (0, 0, 0, 0))

    def own_first(i, at):
        return chunk_at(i, 1 - at[0])

    return pl.pallas_call(
        finish_attention_kernel,
        grid_spec=pltpu.PrefetchScalarGridSpec(
            num_scalar_prefetch=1,
            grid=(4,),
            in_specs=[whole] * 4,
            out_specs=[
                pl.BlockSpec((width, width), lambda i, at: (0, jnp.minimum(own_first(i, at), 2))),
                pl.BlockSpec((width, width), lambda i, at: (0, 0)),
            ],
        ),
        out_shape=[
            jax.ShapeDtypeStruct((width, 3 * width), jnp.float32),
            jax.ShapeDtypeStruct((width, width), jnp.float32),
        ],
        compiler_params=pltpu.CompilerParams(vmem_limit_bytes=VMEM_LIMIT),
        cost_estimate=pl.CostEstimate(
            flops=0, bytes_accessed=24 * width * width, transcendentals=0
        ),
    )(places, *pieces)


def pick(values, index):
    return lax.dynamic_index_in_dim(values, index, 0, keepdims=False)


def rows_of(own, other, third, chip):
    first = jnp.where(chip == 0, own, other)
    second = jnp.where(chip == 0, other, own)
    return jnp.stack([first, second, third])


def shards(
    hidden,
    cond,
    lengths,
    ln1_gain,
    w_qkv,
    w_out,
    ln2_gain,
    w_fc1,
    b_fc1,
    w_fc2,
    b_fc2,
    w_ada,
    b_ada,
    cotangent,
):
    row_count, span, width = hidden.shape
    places = place_scalars()
    seat = lax.axis_index("seq")
    chip = seat // 2
    bases = jnp.stack([seat, seat ^ 2, seat ^ 1, seat ^ 3]) * span
    layout = jnp.concatenate(
        [pick(lengths, chip).reshape(-1), lengths[2], bases.astype(jnp.int32)]
    )
    hidden_far = swap(pick(hidden, 1 - chip), "seq", 2)
    blocks = [pick(hidden, chip), hidden_far, hidden[2]]
    ada_full = w_ada.astype(jnp.float32)
    modulation = (
        jnp.dot(cond, ada_full, precision=highest, preferred_element_type=jnp.float32) + b_ada
    )
    mod = jnp.stack([pick(modulation, chip), modulation[2]]).reshape(2, 6, width)
    gain_one, gain_two = ln1_gain[None], ln2_gain[None]

    normed_own, normed_split, query_own, query_split, kv_own, kv_split, angle_own, angle_split = (
        project(layout, [blocks[0], blocks[2]], mod, gain_one, w_qkv, (0, 1), (0, 0))
    )
    split_chip = swap(kv_split, "seq", 2)
    split_core = swap(kv_split, "seq", 1)
    own_core = swap(kv_own, "seq", 1)
    normed_far, query_far, kv_far, angle_far = project(
        layout, [blocks[1]], mod, gain_one, w_qkv, (0,), (1,)
    )
    far_core = swap(kv_far, "seq", 1)
    cotan_far = swap(pick(cotangent, 1 - chip), "seq", 2)
    cotan = [pick(cotangent, chip), cotan_far, cotangent[2]]
    kv_row = [kv_own, kv_far, own_core, far_core]
    mixed_own, logsum_own = attend(after(layout, *kv_row), query_own, kv_row, 0, 0)
    split_chip = after(split_chip, logsum_own)
    split_cross = swap(split_chip, "seq", 1)
    kv_third = [kv_split, split_chip, split_core, split_cross]
    mixed_far, logsum_far = attend(after(layout, split_chip), query_far, kv_row, 0, 1)
    mixed_split, logsum_split = attend(after(layout, mixed_far), query_split, kv_third, 1, 0)
    mixed = [mixed_own, mixed_far, mixed_split]
    (
        result_own,
        result_far,
        result_split,
        mixed_grad_own,
        mixed_grad_far,
        mixed_grad_split,
        resid_grad,
        low,
        feed_chunks,
        b_one_grad,
        feed_sums,
    ) = feed(
        mixed,
        blocks,
        cotan,
        mod,
        gain_two,
        w_out,
        w_fc1,
        b_fc1[None],
        w_fc2,
        b_fc2[None],
    )
    everyone = ("seq", "batch")
    feed_share = lax.psum_scatter(
        feed_chunks.reshape(-1, width), everyone, scatter_dimension=0, tiled=True
    )
    pairs = width // LANES
    half = pairs // 2

    def back_of_row(sent, first, last):
        return attend_back(
            after(layout, sent),
            [query_own, query_far],
            [mixed_own, mixed_far],
            [mixed_grad_own, mixed_grad_far],
            [logsum_own, logsum_far],
            [angle_own, angle_far],
            kv_row,
            0,
            first,
            last,
        )

    split_grad, near_split, far_split = attend_back(
        layout,
        [query_split],
        [mixed_split],
        [mixed_grad_split],
        [logsum_split],
        [angle_split],
        kv_third,
        1,
        some=2,
    )
    got_split = swap(far_split, "seq", 1)
    own_c, far_grad_c, near_c, far_c = back_of_row(split_grad, 0, half)
    got_c = swap(far_c, "seq", 1)
    got_split = after(got_split, own_c)
    chip_sum = near_split[1].astype(jnp.float32) + got_split[1].astype(jnp.float32)
    chip_split = swap(chip_sum.astype(jnp.bfloat16), "seq", 2)
    own_d, far_grad_d, near_d, far_d = back_of_row((own_c, chip_sum), half, pairs)
    got_d = swap(far_d, "seq", 1)
    send_att, keep_att, merged = merge_back(
        places,
        [
            (0, half, [own_c, far_grad_c, near_c, got_c]),
            (half, pairs, [own_d, far_grad_d, near_d, got_d]),
        ],
        [(0, pairs, [split_grad, near_split, got_split, chip_split])],
        [angle_own, angle_far, angle_split],
        [normed_own, normed_far, normed_split],
        mixed,
        low,
    )
    att_steps = sync_steps(places, send_att, keep_att)
    sent_att = next(att_steps)
    hidden_own_grad, hidden_far_grad, hidden_split_grad, merge_sums = enter_back(
        blocks, resid_grad, mod, gain_one, merged, w_qkv
    )
    far_hidden_grad = swap(hidden_far_grad, "seq", 2)
    far_result = swap(after(result_far, merge_sums), "seq", 2)
    vectors = jnp.concatenate(
        [merge_sums[0:1], feed_sums[0:1], feed_sums[1:2], b_one_grad.reshape(-1, width)], axis=0
    )

    def mod_row(group):
        at = 2 + 4 * group
        return jnp.concatenate(
            [merge_sums[1 + 2 * group : 3 + 2 * group], feed_sums[at : at + 4]], axis=0
        )

    row_own, row_split = mod_row(0), mod_row(1)
    nothing = jnp.zeros_like(row_own)
    mod_local = jnp.stack(
        [
            jnp.where(chip == 0, row_own, nothing),
            jnp.where(chip == 0, nothing, row_own),
            row_split,
        ]
    )
    small = SmallSums(vectors, mod_local, cond)
    sent_att, _ = run_on(att_steps, merge_sums)
    small.step()
    sent_att, _ = run_on(att_steps)
    small.step(sent_att)
    sent_att, _ = run_on(att_steps)
    small.step(sent_att)
    sent_att, _ = run_on(att_steps)
    small.step(sent_att)
    sent_att, _ = run_on(att_steps, far_result)
    small.step(sent_att)
    feed_whole = lax.all_gather(after(feed_share, sent_att), everyone, axis=0, tiled=True)
    sent_att, _ = run_on(att_steps, far_hidden_grad)
    small.finish(sent_att)
    vectors, mod_total, mod_all, cond_all = small.results(cond)
    sent_att, _ = run_on(att_steps)
    output = after(rows_of(result_own, far_result, result_split, chip), sent_att)
    ada_grad = jnp.dot(cond_all.T, mod_all, precision=highest, preferred_element_type=jnp.float32)
    cond_grad = jnp.dot(
        mod_total, ada_full.T, precision=highest, preferred_element_type=jnp.float32
    )
    sent_att, _ = run_on(att_steps, ada_grad, cond_grad)
    hidden_grad = rows_of(hidden_own_grad, far_hidden_grad, hidden_split_grad, chip)
    sent_att, _ = run_on(att_steps, output, hidden_grad)
    _, att_pieces = run_on(att_steps)
    qkv_grad, out_grad = finish_attention(places, att_pieces)
    fc1_grad, fc2_grad = finish_feed(feed_whole.reshape(feed_chunks.shape))
    return (
        output,
        hidden_grad,
        cond_grad,
        vectors[0],
        qkv_grad,
        out_grad,
        vectors[1],
        fc1_grad,
        vectors[3:].reshape(-1),
        fc2_grad,
        vectors[2],
        ada_grad,
        jnp.sum(mod_all, axis=0),
    )


def solution(mesh):
    return jax.shard_map(
        shards,
        mesh=mesh,
        in_specs=(
            P("batch", "seq", None),
            P("batch", None),
            P("batch", None),
            P(),
            P(),
            P(),
            P(),
            P(),
            P(),
            P(),
            P(),
            P(),
            P(),
            P("batch", "seq", None),
        ),
        out_specs=(
            P("batch", "seq", None),
            P("batch", "seq", None),
            P("batch", None),
            P(),
            P(),
            P(),
            P(),
            P(),
            P(),
            P(),
            P(),
            P(),
            P(),
        ),
        check_vma=False,
    )
```

```python
import functools

import jax
import jax.numpy as jnp
from jax import lax
from jax.experimental import pallas as pl
from jax.experimental.pallas import tpu as pltpu
from jax.sharding import PartitionSpec as P

HEADS = 12
HEAD = 64
DOCS = 8
LANES = 128
GELU_A = 0.7978845608
GELU_B = 0.044715
VMEM_LIMIT = 60 * 2**20
SCALE = 0.15


highest = lax.Precision.HIGHEST


def lasting(microseconds):
    flops = int(microseconds * SCALE * 1.15e9)
    return pl.CostEstimate(flops=flops, bytes_accessed=1024, transcendentals=0)


def dot_nt(left, right):
    return lax.dot_general(
        left, right, (((1,), (1,)), ((), ())), preferred_element_type=jnp.float32
    )


def dot_tn(left, right):
    return lax.dot_general(
        left, right, (((0,), (0,)), ((), ())), preferred_element_type=jnp.float32
    )


def dot_nn(left, right):
    return jnp.dot(left, right, preferred_element_type=jnp.float32)


def column_sum(values):
    return jnp.sum(values, axis=0, keepdims=True)


def row_mean(values):
    return jnp.mean(values, axis=-1, keepdims=True)


def normalized(values):
    center = values - row_mean(values)
    inverse = lax.rsqrt(row_mean(center * center) + 1e-05)
    return center * inverse, inverse


def documents_of(slots, layout_ref, group):
    end = jnp.int32(0)
    segment = jnp.zeros_like(slots)
    start = jnp.zeros_like(slots)
    for i in range(DOCS):
        length = layout_ref[group * DOCS + i]
        end = end + length
        passed = slots >= end
        segment = segment + passed.astype(jnp.int32)
        start = start + jnp.where(passed, length, 0)
    return segment, slots - start


def base_of(layout_ref, block):
    return layout_ref[2 * DOCS + block]


def slots_of(layout_ref, block, span):
    return base_of(layout_ref, block) + lax.broadcasted_iota(jnp.int32, (1, span), 1)


def segments_of(layout_ref, block, group, span):
    segment, _ = documents_of(slots_of(layout_ref, block, span), layout_ref, group)
    return segment.astype(jnp.float32)


def as_column(row):
    return jnp.broadcast_to(row, (LANES, row.shape[1])).T


def turned(values, cosine, sine):
    lanes = lax.broadcasted_iota(jnp.int32, cosine.shape, 1)
    first = lanes % HEAD < HEAD // 2
    pieces = []
    for c in range(values.shape[1] // LANES):
        u = values[:, c * LANES : (c + 1) * LANES]
        other = jnp.where(
            first, pltpu.roll(u, LANES - HEAD // 2, 1), pltpu.roll(u, HEAD // 2, 1)
        )
        pieces.append(u * cosine + other * sine)
    return pieces


def project_kernel(groups, bases, layout_ref, *refs):
    count = len(groups)
    hidden = refs[:count]
    mod_ref, gain_ref, speed_ref, weight_ref = refs[count : count + 4]
    normed = refs[count + 4 : 2 * count + 4]
    query = refs[2 * count + 4 : 3 * count + 4]
    keyval = refs[3 * count + 4 : 4 * count + 4]
    angle = refs[4 * count + 4 : 5 * count + 4]
    step = pl.program_id(0)
    span = hidden[0].shape[0]

    @pl.when(step == 0)
    def _():
        for b in range(count):
            values, _ = normalized(hidden[b][...].astype(jnp.float32))
            scale = mod_ref[groups[b], 1:2, :]
            shift = mod_ref[groups[b], 0:1, :]
            normed[b][...] = (values * gain_ref[...] * (1.0 + scale) + shift).astype(jnp.bfloat16)
            _, place = documents_of(slots_of(layout_ref, bases[b], span), layout_ref, groups[b])
            angles = speed_ref[...][:, :1] * place.astype(jnp.float32)
            sine, cosine = jnp.sin(angles), jnp.cos(angles)
            angle[b][0] = jnp.concatenate([cosine] * 4, axis=0).T
            angle[b][1] = jnp.concatenate([-sine, sine] * 2, axis=0).T

    for b in range(count):
        merged = dot_nn(normed[b][...], weight_ref[...])

        @pl.when(step == 0)
        def _(b=b, merged=merged):
            for c, piece in enumerate(turned(merged, angle[b][0], angle[b][1])):
                query[b][:, c * LANES : (c + 1) * LANES] = (piece * 0.125).astype(jnp.bfloat16)

        @pl.when(step == 1)
        def _(b=b, merged=merged):
            for c, piece in enumerate(turned(merged, angle[b][0], angle[b][1])):
                keyval[b][c, :, :LANES] = piece.astype(jnp.bfloat16)

        @pl.when(step == 2)
        def _(b=b, merged=merged):
            for c in range(merged.shape[1] // LANES):
                keyval[b][c, :, LANES:] = merged[:, c * LANES : (c + 1) * LANES].astype(
                    jnp.bfloat16
                )


def speeds():
    half = 10000.0 ** (-jnp.arange(HEAD // 2, dtype=jnp.float32) * 2.0 / HEAD)
    return jnp.tile(half[:, None], (1, LANES))


def project(layout, hidden, mod, gain, weight, groups, bases):
    count = len(hidden)
    span, width = hidden[0].shape
    pairs = width // LANES
    whole = pl.BlockSpec((span, width), lambda i, at: (0, 0))
    return pl.pallas_call(
        functools.partial(project_kernel, groups, bases),
        grid_spec=pltpu.PrefetchScalarGridSpec(
            num_scalar_prefetch=1,
            grid=(3,),
            in_specs=[whole] * count
            + [
                pl.BlockSpec(mod.shape, lambda i, at: (0, 0, 0)),
                pl.BlockSpec(gain.shape, lambda i, at: (0, 0)),
                pl.BlockSpec((HEAD // 2, LANES), lambda i, at: (0, 0)),
                pl.BlockSpec((width, width), lambda i, at: (0, i)),
            ],
            out_specs=[whole] * (2 * count)
            + [pl.BlockSpec((pairs, span, 2 * LANES), lambda i, at: (0, 0, 0))] * count
            + [pl.BlockSpec((2, span, LANES), lambda i, at: (0, 0, 0))] * count,
        ),
        out_shape=[jax.ShapeDtypeStruct((span, width), jnp.bfloat16)] * (2 * count)
        + [jax.ShapeDtypeStruct((pairs, span, 2 * LANES), jnp.bfloat16)] * count
        + [jax.ShapeDtypeStruct((2, span, LANES), jnp.float32)] * count,
        compiler_params=pltpu.CompilerParams(vmem_limit_bytes=VMEM_LIMIT),
        cost_estimate=lasting(5 * count),
    )(layout, *hidden, mod, gain, speeds(), weight)


def one_head(values, head):
    lanes = lax.broadcasted_iota(jnp.int32, values.shape, 1)
    return jnp.where(lanes // HEAD == head, values, jnp.zeros_like(values))


def stacked(keyval, pair, lanes):
    return jnp.concatenate([ref[pair, :, lanes] for ref in keyval], axis=0)


KEYS, VALUES = slice(0, LANES), slice(LANES, 2 * LANES)


def attend_kernel(group, count, layout_ref, *refs):
    query, keyval = refs[:count], refs[count : count + 4]
    mixed, logsum = refs[count + 4 : 2 * count + 4], refs[2 * count + 4 : 3 * count + 4]
    bias_ref = refs[3 * count + 4]
    span = query[0].shape[0]
    blocks = [slice(q * span, (q + 1) * span) for q in range(count)]

    @pl.when(pl.program_id(0) == 0)
    def _():
        for q in range(count):
            column = as_column(segments_of(layout_ref, q, group, span))
            for k in range(4):
                row = segments_of(layout_ref, k, group, span)
                for c in range(0, span, LANES):
                    bias_ref[blocks[q], k * span + c : k * span + c + LANES] = jnp.where(
                        column == row[:, c : c + LANES], 0.0, -1e30
                    )

    lanes = lax.broadcasted_iota(jnp.int32, (count * span, LANES), 1)
    for p in range(keyval[0].shape[0]):
        here = slice(p * LANES, (p + 1) * LANES)
        keys = stacked(keyval, p, KEYS)
        values = stacked(keyval, p, VALUES)
        asked = jnp.concatenate([ref[:, here] for ref in query], axis=0)
        scores = [dot_nt(one_head(asked, h), keys) for h in range(2)]
        sums, tops = [], []
        for h in range(2):
            biased = scores[h] + bias_ref[...]
            peak = jnp.max(biased, axis=1, keepdims=True)
            expo = jnp.exp(biased - peak)
            total = jnp.sum(expo, axis=1, keepdims=True)
            sums.append(dot_nn(expo.astype(jnp.bfloat16), values) / total)
            tops.append(peak + jnp.log(total))
        result = jnp.where(lanes < HEAD, sums[0], sums[1]).astype(jnp.bfloat16)
        top = jnp.where(lanes == 0, tops[0], tops[1])
        for q in range(count):
            mixed[q][:, here] = result[blocks[q]]
            logsum[q][p] = top[blocks[q]].T[:2, :]


def attend(layout, query, keyval, group):
    count = len(query)
    span, width = query[0].shape
    pairs = width // LANES
    some = 2
    by_pair = pl.BlockSpec((span, some * LANES), lambda i, at: (0, i))
    return pl.pallas_call(
        functools.partial(attend_kernel, group, count),
        grid_spec=pltpu.PrefetchScalarGridSpec(
            num_scalar_prefetch=1,
            grid=(pairs // some,),
            in_specs=[by_pair] * count
            + [pl.BlockSpec((some, span, 2 * LANES), lambda i, at: (i, 0, 0))] * 4,
            out_specs=[by_pair] * count
            + [pl.BlockSpec((some, 2, span), lambda i, at: (i, 0, 0))] * count,
            scratch_shapes=[pltpu.VMEM((count * span, 4 * span), jnp.float32)],
        ),
        out_shape=[jax.ShapeDtypeStruct((span, width), jnp.bfloat16)] * count
        + [jax.ShapeDtypeStruct((pairs, 2, span), jnp.float32)] * count,
        compiler_params=pltpu.CompilerParams(vmem_limit_bytes=VMEM_LIMIT),
        cost_estimate=lasting(9 * count),
    )(layout, *query, *keyval)


def attend_back_kernel(group, count, layout_ref, *refs):
    refs = list(refs)

    def take(number):
        taken = refs[:number]
        del refs[:number]
        return taken

    query, mixed, grad = take(count), take(count), take(count)
    logsum, angle, keyval = take(count), take(count), take(4)
    query_grad = take(count)
    near_ref, far_ref, bias_ref = refs
    span = query[0].shape[0]

    @pl.when(pl.program_id(0) == 0)
    def _():
        for k in range(4):
            column = as_column(segments_of(layout_ref, k, group, span))
            for q in range(count):
                row = segments_of(layout_ref, q, group, span)
                for c in range(0, span, LANES):
                    bias_ref[q, k * span : (k + 1) * span, c : c + LANES] = jnp.where(
                        column == row[:, c : c + LANES], 0.0, -1e30
                    )

    for p in range(keyval[0].shape[0]):
        here = slice(p * LANES, (p + 1) * LANES)
        keys = stacked(keyval, p, KEYS)
        values = stacked(keyval, p, VALUES)
        keys_turned = jnp.concatenate([ref[p, :, KEYS].T for ref in keyval], axis=1)
        key_grad = value_grad = None
        for q in range(count):
            weighed = mixed[q][:, here].astype(jnp.float32) * grad[q][:, here].astype(jnp.float32)
            weighed = weighed.T
            heads = []
            for h in range(2):
                chosen = one_head(query[q][:, here], h)
                chosen_grad = one_head(grad[q][:, here], h)
                own = slice(h * HEAD, (h + 1) * HEAD)
                delta = jnp.sum(weighed[own, :], axis=0, keepdims=True)
                scores = dot_nt(keys, chosen) + bias_ref[q]
                prob_grad = dot_nt(values, chosen_grad)
                probs = jnp.exp(scores - logsum[q][p, h : h + 1, :])
                term = dot_nn(probs.astype(jnp.bfloat16), chosen_grad)
                value_grad = term if value_grad is None else value_grad + term
                score_grad = (probs * (prob_grad - delta)).astype(jnp.bfloat16)
                term = dot_nn(score_grad, chosen)
                key_grad = term if key_grad is None else key_grad + term
                heads.append(dot_nn(keys_turned[own, :], score_grad))
            back = jnp.concatenate(heads, axis=0).T * 0.125
            (back,) = turned(back, angle[q][0], -angle[q][1])
            query_grad[q][:, here] = back.astype(jnp.bfloat16)
        for k in range(4):
            ref = near_ref if k < 2 else far_ref
            rows = slice(k * span, (k + 1) * span)
            ref[k % 2, p, :, KEYS] = key_grad[rows].astype(ref.dtype)
            ref[k % 2, p, :, VALUES] = value_grad[rows].astype(ref.dtype)


def attend_back(
    layout, query, mixed, grad, logsum, angle, keyval, group, first=0, last=None, some=1
):
    count = len(query)
    span, width = query[0].shape
    pairs = (last or width // LANES) - first
    start = first // some
    by_pair = pl.BlockSpec((span, some * LANES), lambda i, at: (0, start + i))
    two_blocks = pl.BlockSpec((2, some, span, 2 * LANES), lambda i, at: (0, i, 0, 0))
    two_shape = jax.ShapeDtypeStruct((2, pairs, span, 2 * LANES), jnp.bfloat16)
    return pl.pallas_call(
        functools.partial(attend_back_kernel, group, count),
        grid_spec=pltpu.PrefetchScalarGridSpec(
            num_scalar_prefetch=1,
            grid=(pairs // some,),
            in_specs=[by_pair] * (3 * count)
            + [pl.BlockSpec((some, 2, span), lambda i, at: (start + i, 0, 0))] * count
            + [pl.BlockSpec((2, span, LANES), lambda i, at: (0, 0, 0))] * count
            + [pl.BlockSpec((some, span, 2 * LANES), lambda i, at: (start + i, 0, 0))] * 4,
            out_specs=[pl.BlockSpec((span, some * LANES), lambda i, at: (0, i))] * count
            + [two_blocks] * 2,
            scratch_shapes=[pltpu.VMEM((count, 4 * span, span), jnp.float32)],
        ),
        out_shape=[jax.ShapeDtypeStruct((span, pairs * LANES), jnp.bfloat16)] * count
        + [two_shape] * 2,
        compiler_params=pltpu.CompilerParams(vmem_limit_bytes=VMEM_LIMIT),
        cost_estimate=lasting(2 * count * pairs),
    )(layout, *query, *mixed, *grad, *logsum, *angle, *keyval)


def group_of(block):
    return 0 if block < 2 else 1


def feed_kernel(*refs):
    mixed, hidden, cotan = refs[0:3], refs[3:6], refs[6:9]
    mod_ref, gain_ref, w_out_ref, w_one_ref, b_one_ref, w_two_ref, b_two_ref = refs[9:16]
    result, mixed_grad = refs[16:19], refs[19:22]
    resid_ref, low_ref, chunks_ref, b_one_grad, sums_ref = refs[22:27]
    second_ref, turned_ref, branch_low_ref, branch_ref, second_grad_ref, act_ref, pre_ref = refs[27:]
    step = pl.program_id(0)
    span = hidden[0].shape[0]

    def modulation(block, which):
        return mod_ref[group_of(block), which : which + 1, :]

    @pl.when(step == 0)
    def _():
        bias_sum = None
        for b in range(3):
            rows = slice(b * span, (b + 1) * span)
            attended = dot_nn(mixed[b][...], w_out_ref[...])
            resid = hidden[b][...].astype(jnp.float32) + modulation(b, 2) * attended
            resid_ref[rows, :] = resid
            values, _ = normalized(resid)
            second = values * gain_ref[...] * (1.0 + modulation(b, 4)) + modulation(b, 3)
            second = second.astype(jnp.bfloat16)
            second_ref[rows, :] = second
            turned_ref[:, rows] = second.T
            branch_grad = modulation(b, 5) * cotan[b][...].astype(jnp.float32)
            branch_low_ref[rows, :] = branch_grad.astype(jnp.bfloat16)
            part = column_sum(branch_grad)
            bias_sum = part if bias_sum is None else bias_sum + part
        sums_ref[...] = jnp.zeros_like(sums_ref)
        sums_ref[1:2, :] = bias_sum
        branch_ref[...] = jnp.zeros_like(branch_ref)
        second_grad_ref[...] = jnp.zeros_like(second_grad_ref)

    b_one_grad[...] = jnp.zeros_like(b_one_grad)

    for b in range(3):
        rows = slice(b * span, (b + 1) * span)
        pre = dot_nn(second_ref[rows, :], w_one_ref[...]) + b_one_ref[...]
        square = pre * pre
        tanh = jnp.tanh(GELU_A * pre * (1.0 + GELU_B * square))
        half = 0.5 * (1.0 + tanh)
        active = (pre * half).astype(jnp.bfloat16)
        act_ref[rows, :] = active
        branch_ref[rows, :] += dot_nn(active, w_two_ref[...])
        slope = half + 0.5 * GELU_A * pre * (1.0 - tanh * tanh) * (1.0 + 3.0 * GELU_B * square)
        pre_grad = dot_nt(branch_low_ref[rows, :], w_two_ref[...]) * slope
        b_one_grad[0] += column_sum(pre_grad)
        pre_low = pre_grad.astype(jnp.bfloat16)
        pre_ref[rows, :] = pre_low
        second_grad_ref[rows, :] += dot_nt(pre_low, w_one_ref[...])

    chunks_ref[0, 0] = dot_nn(turned_ref[...], pre_ref[...]).astype(jnp.bfloat16)
    chunks_ref[0, 1] = dot_tn(act_ref[...], branch_low_ref[...]).astype(jnp.bfloat16)

    @pl.when(step == 3)
    def _():
        for b in range(3):
            at = 2 + 4 * group_of(b)
            rows = slice(b * span, (b + 1) * span)
            resid = resid_ref[rows, :]
            branch = branch_ref[rows, :] + b_two_ref[...]
            result[b][...] = (resid + modulation(b, 5) * branch).astype(jnp.bfloat16)
            upstream = cotan[b][...].astype(jnp.float32)
            sums_ref[at + 3 : at + 4, :] += column_sum(upstream * branch)
            values, inverse = normalized(resid)
            grad = second_grad_ref[rows, :]
            sums_ref[at + 1 : at + 2, :] += column_sum(grad)
            weighed = column_sum(grad * values)
            sums_ref[at + 2 : at + 3, :] += weighed * gain_ref[...]
            sums_ref[0:1, :] += weighed * (1.0 + modulation(b, 4))
            inner = grad * ((1.0 + modulation(b, 4)) * gain_ref[...])
            back = (inner - row_mean(inner) - values * row_mean(inner * values)) * inverse
            resid_grad = upstream + back
            resid_ref[rows, :] = resid_grad
            attended = dot_nn(mixed[b][...], w_out_ref[...])
            sums_ref[at : at + 1, :] += column_sum(resid_grad * attended)
            low = (modulation(b, 2) * resid_grad).astype(jnp.bfloat16)
            low_ref[rows, :] = low
            mixed_grad[b][...] = dot_nt(low, w_out_ref[...]).astype(jnp.bfloat16)


def feed(mixed, hidden, cotan, mod, gain, w_out, w_one, b_one, w_two, b_two):
    span, width = hidden[0].shape
    tokens = 3 * span
    once = pl.Buffered(1)
    block = pl.BlockSpec((span, width), lambda i: (0, 0), pipeline_mode=once)
    out_block = pl.BlockSpec((span, width), lambda i: (0, 0))
    every = pl.BlockSpec((tokens, width), lambda i: (0, 0))
    row = pl.BlockSpec((1, width), lambda i: (0, 0))
    chunk = pl.BlockSpec((1, 2, width, width), lambda i: (i, 0, 0, 0))
    low_block = jax.ShapeDtypeStruct((span, width), jnp.bfloat16)
    chunks = jax.ShapeDtypeStruct((4, 2, width, width), jnp.bfloat16)
    return pl.pallas_call(
        feed_kernel,
        grid_spec=pl.GridSpec(
            grid=(4,),
            in_specs=[block] * 9
            + [
                pl.BlockSpec(mod.shape, lambda i: (0, 0, 0)),
                row,
                pl.BlockSpec((width, width), lambda i: (0, 0), pipeline_mode=once),
                pl.BlockSpec((width, width), lambda i: (0, i)),
                pl.BlockSpec((1, width), lambda i: (0, i)),
                pl.BlockSpec((width, width), lambda i: (i, 0)),
                row,
            ],
            out_specs=[out_block] * 6
            + [every, every, chunk]
            + [
                pl.BlockSpec((1, 1, width), lambda i: (i, 0, 0)),
                pl.BlockSpec((16, width), lambda i: (0, 0)),
            ],
            scratch_shapes=[
                pltpu.VMEM((tokens, width), jnp.bfloat16),
                pltpu.VMEM((width, tokens), jnp.bfloat16),
                pltpu.VMEM((tokens, width), jnp.bfloat16),
                pltpu.VMEM((tokens, width), jnp.float32),
                pltpu.VMEM((tokens, width), jnp.float32),
                pltpu.VMEM((tokens, width), jnp.bfloat16),
                pltpu.VMEM((tokens, width), jnp.bfloat16),
            ],
        ),
        out_shape=[low_block] * 6
        + [
            jax.ShapeDtypeStruct((tokens, width), jnp.float32),
            jax.ShapeDtypeStruct((tokens, width), jnp.bfloat16),
        ]
        + [chunks]
        + [
            jax.ShapeDtypeStruct((4, 1, width), jnp.float32),
            jax.ShapeDtypeStruct((16, width), jnp.float32),
        ],
        compiler_params=pltpu.CompilerParams(vmem_limit_bytes=VMEM_LIMIT),
        cost_estimate=lasting(40),
    )(*mixed, *hidden, *cotan, mod, gain, w_out, w_one, b_one, w_two, b_two)


def merge_kernel(parts, places_ref, *refs):
    refs = list(refs)

    def take(count):
        taken = refs[:count]
        del refs[:count]
        return taken

    own_parts = [(first, last, take(4)) for first, last in parts[0]]
    split_parts = [(first, last, take(4)) for first, last in parts[1]]
    angle, normed, mixed = take(3), take(3), take(3)
    low_ref, send_ref, keep_ref, merged_ref, normed_ref, mixed_ref = refs
    step = pl.program_id(0)
    chunk = chunk_at(step, places_ref[0])
    span, width = normed[0].shape
    pairs = width // LANES

    @pl.when(step == 0)
    def _():
        for b in range(3):
            rows = slice(b * span, (b + 1) * span)
            normed_ref[:, rows] = normed[b][...].T
            mixed_ref[:, rows] = mixed[b][...].T

    def part_of(block, pair):
        for first, last, arrays in split_parts if block == 2 else own_parts:
            if first <= pair < last:
                return pair - first, arrays

    def keyval_sum(block, pair, lanes):
        at, arrays = part_of(block, pair)
        if block == 2:
            _, near, got, got_chip = arrays
            terms = near[0, at, :, lanes], got[0, at, :, lanes], got_chip[at, :, lanes]
        else:
            _, _, near, got = arrays
            terms = near[block, at, :, lanes], got[block, at, :, lanes]
        return sum(term.astype(jnp.float32) for term in terms)

    def put(result):
        @pl.when(step < 2)
        def _():
            send_ref[0] = result

        @pl.when(step >= 2)
        def _():
            keep_ref[0] = result

    for b in range(3):
        rows = slice(b * span, (b + 1) * span)
        for c in range(pairs):
            lanes = slice(c * LANES, (c + 1) * LANES)

            @pl.when(chunk == 0)
            def _(b=b, c=c, rows=rows, lanes=lanes):
                at, arrays = part_of(b, c)
                merged_ref[rows, lanes] = arrays[b % 2][:, at * LANES : (at + 1) * LANES]

            @pl.when(chunk == 1)
            def _(b=b, c=c, rows=rows, lanes=lanes):
                (piece,) = turned(keyval_sum(b, c, KEYS), angle[b][0], -angle[b][1])
                merged_ref[rows, lanes] = piece.astype(jnp.bfloat16)

            @pl.when(chunk == 2)
            def _(b=b, c=c, rows=rows, lanes=lanes):
                merged_ref[rows, lanes] = keyval_sum(b, c, VALUES).astype(jnp.bfloat16)

    @pl.when(chunk < 3)
    def _():
        put(dot_nn(normed_ref[...], merged_ref[...]).astype(jnp.bfloat16))

    @pl.when(chunk == 3)
    def _():
        put(dot_nn(mixed_ref[...], low_ref[...]).astype(jnp.bfloat16))


def merge_back(places, own_parts, split_parts, angle, normed, mixed, low):
    span, width = normed[0].shape
    tokens = 3 * span
    once = pl.Buffered(1)

    def whole(array):
        return pl.BlockSpec(
            array.shape, lambda i, at: (0,) * len(array.shape), pipeline_mode=once
        )

    operands = [array for _, _, arrays in own_parts + split_parts for array in arrays]
    operands += [*angle, *normed, *mixed, low]
    parts = [[(first, last) for first, last, _ in group] for group in (own_parts, split_parts)]
    chunk_shape = jax.ShapeDtypeStruct((2, width, width), jnp.bfloat16)
    return pl.pallas_call(
        functools.partial(merge_kernel, parts),
        grid_spec=pltpu.PrefetchScalarGridSpec(
            num_scalar_prefetch=1,
            grid=(4,),
            in_specs=[whole(array) for array in operands],
            out_specs=[
                pl.BlockSpec((1, width, width), lambda i, at: (jnp.minimum(i, 1), 0, 0)),
                pl.BlockSpec((1, width, width), lambda i, at: (jnp.maximum(i - 2, 0), 0, 0)),
                pl.BlockSpec(
                    (tokens, width), lambda i, at: (0, jnp.minimum(chunk_at(i, at[0]), 2))
                ),
            ],
            scratch_shapes=[
                pltpu.VMEM((width, tokens), jnp.bfloat16),
                pltpu.VMEM((width, tokens), jnp.bfloat16),
            ],
        ),
        out_shape=[
            chunk_shape,
            chunk_shape,
            jax.ShapeDtypeStruct((tokens, 3 * width), jnp.bfloat16),
        ],
        compiler_params=pltpu.CompilerParams(vmem_limit_bytes=VMEM_LIMIT),
        cost_estimate=lasting(17),
    )(places, *operands)


def enter_kernel(*refs):
    hidden = refs[0:3]
    resid_grad_ref, mod_ref, gain_ref, merged_ref, weight_ref = refs[3:8]
    hidden_grad = refs[8:11]
    sums_ref, total_ref = refs[11:]
    step = pl.program_id(0)
    span = hidden[0].shape[0]

    @pl.when(step == 0)
    def _():
        total_ref[...] = jnp.zeros_like(total_ref)

    total_ref[...] += dot_nt(merged_ref[...], weight_ref[...])

    @pl.when(step == 2)
    def _():
        sums_ref[...] = jnp.zeros_like(sums_ref)
        for b in range(3):
            group = group_of(b)
            at = 1 + 2 * group
            rows = slice(b * span, (b + 1) * span)
            values, inverse = normalized(hidden[b][...].astype(jnp.float32))
            grad = total_ref[rows, :]
            scaled = 1.0 + mod_ref[group, 1:2, :]
            weighed = column_sum(grad * values)
            sums_ref[0:1, :] += weighed * scaled
            sums_ref[at : at + 1, :] += column_sum(grad)
            sums_ref[at + 1 : at + 2, :] += weighed * gain_ref[...]
            inner = grad * (scaled * gain_ref[...])
            back = (inner - row_mean(inner) - values * row_mean(inner * values)) * inverse
            hidden_grad[b][...] = (resid_grad_ref[rows, :] + back).astype(jnp.bfloat16)


def enter_back(hidden, resid_grad, mod, gain, merged, weight):
    span, width = hidden[0].shape
    tokens = 3 * span
    once = pl.Buffered(1)
    block = pl.BlockSpec((span, width), lambda i: (0, 0), pipeline_mode=once)
    return pl.pallas_call(
        enter_kernel,
        grid=(3,),
        in_specs=[block] * 3
        + [
            pl.BlockSpec((tokens, width), lambda i: (0, 0), pipeline_mode=once),
            pl.BlockSpec(mod.shape, lambda i: (0, 0, 0)),
            pl.BlockSpec(gain.shape, lambda i: (0, 0)),
            pl.BlockSpec((tokens, width), lambda i: (0, i)),
            pl.BlockSpec((width, width), lambda i: (0, i)),
        ],
        out_specs=[pl.BlockSpec((span, width), lambda i: (0, 0))] * 3
        + [pl.BlockSpec((8, width), lambda i: (0, 0))],
        out_shape=[jax.ShapeDtypeStruct((span, width), jnp.bfloat16)] * 3
        + [jax.ShapeDtypeStruct((8, width), jnp.float32)],
        scratch_shapes=[pltpu.VMEM((tokens, width), jnp.float32)],
        compiler_params=pltpu.CompilerParams(vmem_limit_bytes=VMEM_LIMIT),
        cost_estimate=lasting(10),
    )(*hidden, resid_grad, mod, gain, merged, weight)


def swap(values, axis, bit):
    count = lax.axis_size(axis)
    return lax.ppermute(values, axis, [(i, i ^ bit) for i in range(count)])


def bit_of(axis, bit):
    return (lax.axis_index(axis) // bit) % 2


def batch_bits():
    count = lax.axis_size("batch")
    bits = []
    bit = 1
    while bit < count:
        bits.append(bit)
        bit *= 2
    return bits


def split_orders():
    bits = batch_bits()
    chip = ("seq", 2)
    split = [("batch", b) for b in bits[:3]]
    rest = [("batch", b) for b in bits[3:]]
    return ([chip] + split, split[:1] + [chip] + split[1:], rest)


def place_scalars():
    order_a, order_b, _ = split_orders()
    bits = [bit_of(axis, bit) for axis, bit in order_a + order_b]
    return jnp.stack([lax.axis_index("seq") % 2, *bits]).astype(jnp.int32)


def bits_value(at, group, steps, first, last, flip):
    value = jnp.int32(0)
    for d in range(first, last):
        bit = at[1 + group * steps + d]
        if flip and d == last - 1:
            bit = 1 - bit
        value = value * 2 + bit
    return value


def total_kernel(counts, places_ref, *refs):
    inputs, outputs = refs[: sum(counts)], refs[sum(counts) :]
    start = 0
    for g, count in enumerate(counts):
        total = inputs[start][0].astype(jnp.float32)
        for ref in inputs[start + 1 : start + count]:
            total = total + ref[0].astype(jnp.float32)
        start += count
        if len(outputs) == 1:
            outputs[0][g] = total.astype(jnp.bfloat16)
        else:
            outputs[g][0] = total.astype(jnp.bfloat16)


def total_of_parts(places, parts, steps, done, flip, joint):
    rows = parts[0][0][0].shape[1] >> done
    width = parts[0][0][0].shape[2]
    cuts = max(1, rows // 192)
    rows //= cuts
    operands, specs = [], []
    for g, group in enumerate(parts):
        for array, lead, level in group:
            operands.append(array)
            specs.append(
                pl.BlockSpec(
                    (1, rows, width),
                    lambda i, at, g=g, lead=lead, level=level: (
                        lead,
                        bits_value(at, g, steps, level, done, flip) * cuts + i,
                        0,
                    ),
                )
            )
    if joint:
        out_specs = [pl.BlockSpec((2, rows, width), lambda i, at: (0, i, 0))]
        out_shape = [jax.ShapeDtypeStruct((2, cuts * rows, width), jnp.bfloat16)]
    else:
        out_specs = [pl.BlockSpec((1, rows, width), lambda i, at: (0, i, 0))] * 2
        out_shape = [jax.ShapeDtypeStruct((1, cuts * rows, width), jnp.bfloat16)] * 2
    return pl.pallas_call(
        functools.partial(total_kernel, [len(group) for group in parts]),
        grid_spec=pltpu.PrefetchScalarGridSpec(
            num_scalar_prefetch=1, grid=(cuts,), in_specs=specs, out_specs=out_specs
        ),
        out_shape=out_shape,
        compiler_params=pltpu.CompilerParams(vmem_limit_bytes=VMEM_LIMIT),
        cost_estimate=lasting(3),
    )(places, *operands)


def join_kernel(left_ref, right_ref, out_ref):
    count = left_ref.shape[1]
    out_ref[:, :count] = left_ref[...]
    out_ref[:, count:] = right_ref[...]


def join(left, right):
    lead, count, rows, width = left.shape
    spec = pl.BlockSpec((lead, count, rows, width), lambda i: (0, 0, 0, 0))
    return pl.pallas_call(
        join_kernel,
        grid=(1,),
        in_specs=[spec, spec],
        out_specs=pl.BlockSpec((lead, 2 * count, rows, width), lambda i: (0, 0, 0, 0)),
        out_shape=jax.ShapeDtypeStruct((lead, 2 * count, rows, width), left.dtype),
        compiler_params=pltpu.CompilerParams(vmem_limit_bytes=VMEM_LIMIT),
        cost_estimate=lasting(2),
    )(left, right)


def after(values, *others):
    return lax.optimization_barrier((values, others))[0]


def sync_steps(places, send, keep, gather=True):
    order_a, order_b, rest = split_orders()
    steps = len(order_a)
    got = swap(send, "seq", 1)
    got = after(got, (yield [send]))
    parts = [[(keep, g, 0), (got, g, 0)] for g in range(2)]
    for done, dims in enumerate(zip(order_a, order_b), 1):
        joint = dims[0] == dims[1]
        sent = total_of_parts(places, parts, steps, done, True, joint)
        if joint:
            got = [swap(sent[0], *dims[0])] * 2
        else:
            got = [swap(sent[g], *dims[g]) for g in range(2)]
        got = after(got, (yield sent))
        for g in range(2):
            parts[g].append((got[g], g if joint else 0, done))
    (held,) = total_of_parts(places, parts, steps, steps, False, True)
    for axis, bit in rest:
        held = (held.astype(jnp.float32) + swap(held, axis, bit).astype(jnp.float32)).astype(
            held.dtype
        )
    if not gather:
        return held
    blocks = held[:, None]
    for dims in reversed(list(zip(order_a, order_b))):
        if dims[0] == dims[1]:
            got = swap(blocks, *dims[0])
            got = after(got, (yield [blocks]))
            blocks = join(blocks, got)
        else:
            if not isinstance(blocks, list):
                blocks = [blocks[0:1], blocks[1:2]]
            got = [swap(blocks[g], *dims[g]) for g in range(2)]
            got = after(got, (yield blocks))
            if dims == (order_a[0], order_b[0]):
                blocks += got
            else:
                blocks = [join(blocks[g], got[g]) for g in range(2)]
    got = [swap(piece, "seq", 1) for piece in blocks]
    got = after(got, (yield blocks))
    return [*blocks, *got]


HEAD_ROWS, ROW_BLOCK = 8, 24


def pack_kernel(places_ref, feed_ref, merge_ref, bias_ref, cond_ref, out_ref):
    out_ref[...] = jnp.zeros_like(out_ref)
    out_ref[0:1, :] = merge_ref[0:1, :]
    out_ref[1:3, :] = feed_ref[0:2, :]
    for c in range(bias_ref.shape[0]):
        out_ref[3 + c : 4 + c, :] = bias_ref[c]
    for group in range(2):
        merged = merge_ref[1 + 2 * group : 3 + 2 * group, :]
        fed = feed_ref[2 + 4 * group : 6 + 4 * group, :]
        for j in range(6):
            value = merged[j : j + 1, :] if j < 2 else fed[j - 2 : j - 1, :]
            at = HEAD_ROWS + 3 * j
            if group == 1:
                out_ref[at + 2 : at + 3, :] = value
                continue
            for chip in range(2):
                out_ref[at + chip : at + chip + 1, :] = jnp.where(
                    places_ref[0] // 2 == chip, value, 0.0
                )
    rows, count = cond_ref.shape
    for r in range(rows):
        out_ref[HEAD_ROWS + 18 : HEAD_ROWS + 19, r * count : (r + 1) * count] = (
            cond_ref[r : r + 1, :] * 0.25
        )


def pack_small(seat, feed_sums, merge_sums, bias_grad, cond):
    width = feed_sums.shape[1]

    def whole(array):
        return pl.BlockSpec(array.shape, lambda i, at: (0,) * len(array.shape))

    operands = [feed_sums, merge_sums, bias_grad, cond]
    rows = HEAD_ROWS + ROW_BLOCK
    return pl.pallas_call(
        pack_kernel,
        grid_spec=pltpu.PrefetchScalarGridSpec(
            num_scalar_prefetch=1,
            grid=(1,),
            in_specs=[whole(array) for array in operands],
            out_specs=pl.BlockSpec((rows, width), lambda i, at: (0, 0)),
        ),
        out_shape=jax.ShapeDtypeStruct((rows, width), jnp.float32),
        cost_estimate=lasting(2),
    )(seat, *operands)


def grow_kernel(own_ref, got_ref, out_ref):
    rows = own_ref.shape[0]
    out_ref[:HEAD_ROWS] = own_ref[:HEAD_ROWS] + got_ref[:HEAD_ROWS]
    out_ref[HEAD_ROWS:rows] = own_ref[HEAD_ROWS:]
    out_ref[rows:] = got_ref[HEAD_ROWS:]


def grow(own, got):
    rows, width = own.shape
    return pl.pallas_call(
        grow_kernel,
        out_shape=jax.ShapeDtypeStruct((2 * rows - HEAD_ROWS, width), own.dtype),
        cost_estimate=lasting(2),
    )(own, got)


class SmallSums:
    def __init__(self, values):
        self.values = values
        self.dims = [("seq", 1), ("seq", 2)] + [("batch", b) for b in batch_bits()]
        self.pending = None

    def step(self, *done):
        self.take(*done)
        if self.dims:
            self.axis, bit = self.dims.pop(0)
            self.pending = swap(self.values, self.axis, bit)

    def take(self, *done):
        if self.pending is None:
            return
        got = after(self.pending, *done) if done else self.pending
        self.pending = None
        self.values = self.values + got if self.axis == "seq" else grow(self.values, got)

    def finish(self, *done):
        while self.dims:
            self.step(*done)
        self.take(*done)


def modulation_kernel(values_ref, weight_ref, cond_ref, bias_ref, grad_ref):
    values = values_ref[HEAD_ROWS:, :]
    rows, width = values.shape
    count = weight_ref.shape[0]
    conds = []
    for block in range(rows // ROW_BLOCK):
        line = values[block * ROW_BLOCK + 18 : block * ROW_BLOCK + 19, :]
        three = [line[:, r * count : (r + 1) * count] for r in range(3)]
        conds += three * 6 + [jnp.zeros((ROW_BLOCK - 18, count), jnp.float32)]
    conds = jnp.concatenate(conds, axis=0)
    place = lax.broadcasted_iota(jnp.int32, (rows, count), 0) % ROW_BLOCK // 3
    wide_place = lax.broadcasted_iota(jnp.int32, (rows, width), 0) % ROW_BLOCK // 3
    total = None
    for j in range(6):
        lanes = slice(j * width, (j + 1) * width)
        grad_ref[:, lanes] = lax.dot_general(
            jnp.where(place == j, conds, 0.0),
            values,
            (((0,), (0,)), ((), ())),
            precision=highest,
            preferred_element_type=jnp.float32,
        )
        bias_ref[:, lanes] = column_sum(jnp.where(wide_place == j, values, 0.0))
        term = lax.dot_general(
            values[3 * j : 3 * j + 3, :],
            weight_ref[:, lanes].astype(jnp.float32),
            (((1,), (1,)), ((), ())),
            precision=highest,
            preferred_element_type=jnp.float32,
        )
        total = term if total is None else total + term
    cond_ref[...] = total


def modulation_back(values, weight):
    count, wide = weight.shape
    return pl.pallas_call(
        modulation_kernel,
        out_shape=[
            jax.ShapeDtypeStruct((3, count), jnp.float32),
            jax.ShapeDtypeStruct((1, wide), jnp.float32),
            jax.ShapeDtypeStruct((count, wide), jnp.float32),
        ],
        compiler_params=pltpu.CompilerParams(vmem_limit_bytes=VMEM_LIMIT),
        cost_estimate=lasting(7),
    )(values, weight)


def run_on(steps, *done):
    try:
        return steps.send(done), None
    except StopIteration as end:
        return None, end.value


def chunk_at(step, core):
    return jnp.where(step < 2, 2 * (1 - core) + step, 2 * core + step - 2)


def spread_blocks(places_ref, halves, group, out):
    _, count, rows, _ = halves[0].shape
    steps = count.bit_length()
    place = bits_value(places_ref, group, steps, 0, steps, False)
    for k, ref in enumerate(halves):

        @pl.loop(0, count)
        def _(j):
            row = pl.multiple_of((place ^ (k * count + j)) * rows, 8)
            out[pl.ds(row, rows), :] = ref[0, j].astype(jnp.float32)


def finish_feed_kernel(chunks_ref, one_ref, two_ref):
    one_ref[...] = chunks_ref[0, 0].astype(jnp.float32)
    two_ref[...] = chunks_ref[0, 1].astype(jnp.float32)


def finish_feed(chunks):
    count, _, width, _ = chunks.shape
    cuts = 1
    rows = width // cuts
    return pl.pallas_call(
        finish_feed_kernel,
        grid=(count, cuts),
        in_specs=[pl.BlockSpec((1, 2, rows, width), lambda i, j: (i, 0, j, 0))],
        out_specs=[
            pl.BlockSpec((rows, width), lambda i, j: (j, i)),
            pl.BlockSpec((rows, width), lambda i, j: (cuts * i + j, 0)),
        ],
        out_shape=[
            jax.ShapeDtypeStruct((width, count * width), jnp.float32),
            jax.ShapeDtypeStruct((count * width, width), jnp.float32),
        ],
        compiler_params=pltpu.CompilerParams(vmem_limit_bytes=VMEM_LIMIT),
        cost_estimate=lasting(8),
    )(chunks)


def finish_attention_kernel(places_ref, *refs):
    pieces, outs = refs[:8], refs[8:]
    step = pl.program_id(0)
    chunk = chunk_at(step, 1 - places_ref[0])
    for k in range(4):
        start = 4 * (k // 2) + k % 2
        halves = pieces[start], pieces[start + 2]
        for condition, out in ((chunk < 3, outs[0]), (chunk == 3, outs[1])):

            @pl.when((step == k) & condition)
            def _(halves=halves, group=k % 2, out=out):
                spread_blocks(places_ref, halves, group, out)


def finish_attention(places, pieces):
    _, count, rows, width = pieces[0].shape
    whole = pl.BlockSpec((1, count, rows, width), lambda i, at: (0, 0, 0, 0))

    def own_first(i, at):
        return chunk_at(i, 1 - at[0])

    return pl.pallas_call(
        finish_attention_kernel,
        grid_spec=pltpu.PrefetchScalarGridSpec(
            num_scalar_prefetch=1,
            grid=(4,),
            in_specs=[whole] * 8,
            out_specs=[
                pl.BlockSpec((width, width), lambda i, at: (0, jnp.minimum(own_first(i, at), 2))),
                pl.BlockSpec((width, width), lambda i, at: (0, 0)),
            ],
        ),
        out_shape=[
            jax.ShapeDtypeStruct((width, 3 * width), jnp.float32),
            jax.ShapeDtypeStruct((width, width), jnp.float32),
        ],
        compiler_params=pltpu.CompilerParams(vmem_limit_bytes=VMEM_LIMIT),
        cost_estimate=lasting(8),
    )(places, *pieces)


def pick(values, index):
    return lax.dynamic_index_in_dim(values, index, 0, keepdims=False)


def rows_of(own, other, third, chip):
    first = jnp.where(chip == 0, own, other)
    second = jnp.where(chip == 0, other, own)
    return jnp.stack([first, second, third])


def shards(
    hidden,
    cond,
    lengths,
    ln1_gain,
    w_qkv,
    w_out,
    ln2_gain,
    w_fc1,
    b_fc1,
    w_fc2,
    b_fc2,
    w_ada,
    b_ada,
    cotangent,
):
    row_count, span, width = hidden.shape
    places = place_scalars()
    seat = lax.axis_index("seq")
    chip = seat // 2
    bases = jnp.stack([seat, seat ^ 2, seat ^ 1, seat ^ 3]) * span
    layout = jnp.concatenate(
        [pick(lengths, chip).reshape(-1), lengths[2], bases.astype(jnp.int32)]
    )
    hidden_far = swap(pick(hidden, 1 - chip), "seq", 2)
    blocks = [pick(hidden, chip), hidden_far, hidden[2]]
    ada_full = w_ada.astype(jnp.float32)
    modulation = (
        jnp.dot(cond, ada_full, precision=highest, preferred_element_type=jnp.float32) + b_ada
    )
    mod = jnp.stack([pick(modulation, chip), modulation[2]]).reshape(2, 6, width)
    gain_one, gain_two = ln1_gain[None], ln2_gain[None]

    normed_own, normed_split, query_own, query_split, kv_own, kv_split, angle_own, angle_split = (
        project(layout, [blocks[0], blocks[2]], mod, gain_one, w_qkv, (0, 1), (0, 0))
    )
    split_chip = swap(kv_split, "seq", 2)
    split_core = swap(kv_split, "seq", 1)
    own_core = swap(kv_own, "seq", 1)
    normed_far, query_far, kv_far, angle_far = project(
        layout, [blocks[1]], mod, gain_one, w_qkv, (0,), (1,)
    )
    far_core = swap(kv_far, "seq", 1)
    cotan_far = swap(pick(cotangent, 1 - chip), "seq", 2)
    cotan = [pick(cotangent, chip), cotan_far, cotangent[2]]
    kv_row = [kv_own, kv_far, own_core, far_core]
    mixed_own, mixed_far, logsum_own, logsum_far = attend(
        after(layout, *kv_row), [query_own, query_far], kv_row, 0
    )
    split_chip = after(split_chip, logsum_own)
    split_cross = swap(split_chip, "seq", 1)
    kv_third = [kv_split, split_chip, split_core, split_cross]
    mixed_split, logsum_split = attend(after(layout, mixed_far), [query_split], kv_third, 1)
    mixed = [mixed_own, mixed_far, mixed_split]
    (
        result_own,
        result_far,
        result_split,
        mixed_grad_own,
        mixed_grad_far,
        mixed_grad_split,
        resid_grad,
        low,
        feed_chunks,
        b_one_grad,
        feed_sums,
    ) = feed(
        mixed,
        blocks,
        cotan,
        mod,
        gain_two,
        w_out,
        w_fc1,
        b_fc1[None],
        w_fc2,
        b_fc2[None],
    )
    everyone = ("seq", "batch")
    feed_share = lax.psum_scatter(
        feed_chunks.reshape(-1, width), everyone, scatter_dimension=0, tiled=True
    )
    pairs = width // LANES

    def back_of_row(sent):
        return attend_back(
            after(layout, sent),
            [query_own, query_far],
            [mixed_own, mixed_far],
            [mixed_grad_own, mixed_grad_far],
            [logsum_own, logsum_far],
            [angle_own, angle_far],
            kv_row,
            0,
        )

    def back_of_split(sent):
        return attend_back(
            after(layout, sent),
            [query_split],
            [mixed_split],
            [mixed_grad_split],
            [logsum_split],
            [angle_split],
            kv_third,
            1,
            some=2,
        )

    split_grad, near_split, far_split = back_of_split(mixed_split)
    got_split = swap(far_split, "seq", 1)
    own_grad, far_grad, near_own, far_own = back_of_row(split_grad)
    got_own = swap(far_own, "seq", 1)
    got_split = after(got_split, split_grad)
    chip_sum = near_split[1].astype(jnp.float32) + got_split[1].astype(jnp.float32)
    chip_sum = chip_sum.astype(jnp.bfloat16)
    chip_split = swap(chip_sum, "seq", 2)
    send_att, keep_att, merged = merge_back(
        places,
        [(0, pairs, [own_grad, far_grad, near_own, got_own])],
        [(0, pairs, [split_grad, near_split, got_split, chip_split])],
        [angle_own, angle_far, angle_split],
        [normed_own, normed_far, normed_split],
        mixed,
        low,
    )
    hidden_own_grad, hidden_far_grad, hidden_split_grad, merge_sums = enter_back(
        blocks, resid_grad, mod, gain_one, merged, w_qkv
    )
    att_steps = sync_steps(places, after(send_att, merge_sums), keep_att)
    sent_att = next(att_steps)
    far_hidden_grad = swap(hidden_far_grad, "seq", 2)
    far_result = swap(after(result_far, merge_sums), "seq", 2)
    small = SmallSums(
        pack_small(seat.astype(jnp.int32)[None], feed_sums, merge_sums, b_one_grad, cond)
    )
    small.step()
    sent_att, _ = run_on(att_steps, merge_sums)
    small.step(sent_att)
    sent_att, _ = run_on(att_steps, small.values)
    small.step(sent_att)
    sent_att, _ = run_on(att_steps, small.values, far_result)
    feed_whole = lax.all_gather(after(feed_share, sent_att), everyone, axis=0, tiled=True)
    small.step(sent_att)
    sent_att, _ = run_on(att_steps, small.values, far_hidden_grad)
    small.step(sent_att)
    sent_att, _ = run_on(att_steps, small.values)
    small.finish(sent_att)
    vectors = small.values[:HEAD_ROWS]
    cond_grad, ada_bias_grad, ada_grad = modulation_back(small.values, w_ada)
    sent_att, _ = run_on(att_steps, vectors)
    output = rows_of(result_own, far_result, result_split, chip)
    hidden_grad = rows_of(hidden_own_grad, far_hidden_grad, hidden_split_grad, chip)
    sent_att, _ = run_on(att_steps, output, hidden_grad)
    ln1_grad, ln2_grad, fc2_bias_grad = vectors[0], vectors[1], vectors[2]
    fc1_bias_grad = vectors[3:7].reshape(-1)
    ada_bias_grad = ada_bias_grad.reshape(-1)
    sent_att, _ = run_on(att_steps, ada_grad, cond_grad, ada_bias_grad, fc1_bias_grad)
    sent_att, _ = run_on(att_steps, ln1_grad, ln2_grad, fc2_bias_grad)
    _, att_pieces = run_on(att_steps)
    qkv_grad, out_grad = finish_attention(places, att_pieces)
    fc1_grad, fc2_grad = finish_feed(after(feed_whole, out_grad).reshape(feed_chunks.shape))
    return (
        output,
        hidden_grad,
        cond_grad,
        ln1_grad,
        qkv_grad,
        out_grad,
        ln2_grad,
        fc1_grad,
        fc1_bias_grad,
        fc2_grad,
        fc2_bias_grad,
        ada_grad,
        ada_bias_grad,
    )


def solution(mesh):
    return jax.shard_map(
        shards,
        mesh=mesh,
        in_specs=(
            P("batch", "seq", None),
            P("batch", None),
            P("batch", None),
            P(),
            P(),
            P(),
            P(),
            P(),
            P(),
            P(),
            P(),
            P(),
            P(),
            P("batch", "seq", None),
        ),
        out_specs=(
            P("batch", "seq", None),
            P("batch", "seq", None),
            P("batch", None),
            P(),
            P(),
            P(),
            P(),
            P(),
            P(),
            P(),
            P(),
            P(),
            P(),
        ),
        check_vma=False,
    )
```

```python
import functools

import jax
import jax.numpy as jnp
from jax import lax
from jax.experimental import pallas as pl
from jax.experimental.pallas import tpu as pltpu
from jax.sharding import PartitionSpec as P

HEADS = 12
HEAD = 64
DOCS = 8
LANES = 128
GELU_A = 0.7978845608
GELU_B = 0.044715
VMEM_LIMIT = 60 * 2**20
SCALE = 0.15


highest = lax.Precision.HIGHEST


def lasting(microseconds):
    flops = int(microseconds * SCALE * 1.15e9)
    return pl.CostEstimate(flops=flops, bytes_accessed=1024, transcendentals=0)


def dot_nt(left, right):
    return lax.dot_general(
        left, right, (((1,), (1,)), ((), ())), preferred_element_type=jnp.float32
    )


def dot_tn(left, right):
    return lax.dot_general(
        left, right, (((0,), (0,)), ((), ())), preferred_element_type=jnp.float32
    )


def dot_nn(left, right):
    return jnp.dot(left, right, preferred_element_type=jnp.float32)


def column_sum(values):
    return jnp.sum(values, axis=0, keepdims=True)


def row_mean(values):
    return jnp.mean(values, axis=-1, keepdims=True)


def normalized(values):
    center = values - row_mean(values)
    inverse = lax.rsqrt(row_mean(center * center) + 1e-05)
    return center * inverse, inverse


def documents_of(slots, layout_ref, group):
    end = jnp.int32(0)
    segment = jnp.zeros_like(slots)
    start = jnp.zeros_like(slots)
    for i in range(DOCS):
        length = layout_ref[group * DOCS + i]
        end = end + length
        passed = slots >= end
        segment = segment + passed.astype(jnp.int32)
        start = start + jnp.where(passed, length, 0)
    return segment, slots - start


def base_of(layout_ref, block):
    return layout_ref[2 * DOCS + block]


def slots_of(layout_ref, block, span):
    return base_of(layout_ref, block) + lax.broadcasted_iota(jnp.int32, (1, span), 1)


def segments_of(layout_ref, block, group, span):
    segment, _ = documents_of(slots_of(layout_ref, block, span), layout_ref, group)
    return segment.astype(jnp.float32)


def as_column(row):
    return jnp.broadcast_to(row, (LANES, row.shape[1])).T


def turned(values, cosine, sine):
    lanes = lax.broadcasted_iota(jnp.int32, cosine.shape, 1)
    first = lanes % HEAD < HEAD // 2
    pieces = []
    for c in range(values.shape[1] // LANES):
        u = values[:, c * LANES : (c + 1) * LANES]
        other = jnp.where(
            first, pltpu.roll(u, LANES - HEAD // 2, 1), pltpu.roll(u, HEAD // 2, 1)
        )
        pieces.append(u * cosine + other * sine)
    return pieces


def project_kernel(groups, bases, layout_ref, *refs):
    count = len(groups)
    hidden = refs[:count]
    mod_ref, gain_ref, speed_ref, weight_ref = refs[count : count + 4]
    normed = refs[count + 4 : 2 * count + 4]
    query = refs[2 * count + 4 : 3 * count + 4]
    keyval = refs[3 * count + 4 : 4 * count + 4]
    angle = refs[4 * count + 4 : 5 * count + 4]
    step = pl.program_id(0)
    span = hidden[0].shape[0]

    @pl.when(step == 0)
    def _():
        for b in range(count):
            values, _ = normalized(hidden[b][...].astype(jnp.float32))
            scale = mod_ref[groups[b], 1:2, :]
            shift = mod_ref[groups[b], 0:1, :]
            normed[b][...] = (values * gain_ref[...] * (1.0 + scale) + shift).astype(jnp.bfloat16)
            _, place = documents_of(slots_of(layout_ref, bases[b], span), layout_ref, groups[b])
            angles = speed_ref[...][:, :1] * place.astype(jnp.float32)
            sine, cosine = jnp.sin(angles), jnp.cos(angles)
            angle[b][0] = jnp.concatenate([cosine] * 4, axis=0).T
            angle[b][1] = jnp.concatenate([-sine, sine] * 2, axis=0).T

    for b in range(count):
        merged = dot_nn(normed[b][...], weight_ref[...])

        @pl.when(step == 0)
        def _(b=b, merged=merged):
            for c, piece in enumerate(turned(merged, angle[b][0], angle[b][1])):
                query[b][:, c * LANES : (c + 1) * LANES] = (piece * 0.125).astype(jnp.bfloat16)

        @pl.when(step == 1)
        def _(b=b, merged=merged):
            for c, piece in enumerate(turned(merged, angle[b][0], angle[b][1])):
                keyval[b][c, :, :LANES] = piece.astype(jnp.bfloat16)

        @pl.when(step == 2)
        def _(b=b, merged=merged):
            for c in range(merged.shape[1] // LANES):
                keyval[b][c, :, LANES:] = merged[:, c * LANES : (c + 1) * LANES].astype(
                    jnp.bfloat16
                )


def speeds():
    half = 10000.0 ** (-jnp.arange(HEAD // 2, dtype=jnp.float32) * 2.0 / HEAD)
    return jnp.tile(half[:, None], (1, LANES))


def project(layout, hidden, mod, gain, weight, groups, bases):
    count = len(hidden)
    span, width = hidden[0].shape
    pairs = width // LANES
    whole = pl.BlockSpec((span, width), lambda i, at: (0, 0))
    return pl.pallas_call(
        functools.partial(project_kernel, groups, bases),
        grid_spec=pltpu.PrefetchScalarGridSpec(
            num_scalar_prefetch=1,
            grid=(3,),
            in_specs=[whole] * count
            + [
                pl.BlockSpec(mod.shape, lambda i, at: (0, 0, 0)),
                pl.BlockSpec(gain.shape, lambda i, at: (0, 0)),
                pl.BlockSpec((HEAD // 2, LANES), lambda i, at: (0, 0)),
                pl.BlockSpec((width, width), lambda i, at: (0, i)),
            ],
            out_specs=[whole] * (2 * count)
            + [pl.BlockSpec((pairs, span, 2 * LANES), lambda i, at: (0, 0, 0))] * count
            + [pl.BlockSpec((2, span, LANES), lambda i, at: (0, 0, 0))] * count,
        ),
        out_shape=[jax.ShapeDtypeStruct((span, width), jnp.bfloat16)] * (2 * count)
        + [jax.ShapeDtypeStruct((pairs, span, 2 * LANES), jnp.bfloat16)] * count
        + [jax.ShapeDtypeStruct((2, span, LANES), jnp.float32)] * count,
        compiler_params=pltpu.CompilerParams(vmem_limit_bytes=VMEM_LIMIT),
        cost_estimate=lasting(5 * count),
    )(layout, *hidden, mod, gain, speeds(), weight)


def one_head(values, head):
    lanes = lax.broadcasted_iota(jnp.int32, values.shape, 1)
    return jnp.where(lanes // HEAD == head, values, jnp.zeros_like(values))


def stacked(keyval, pair, lanes):
    return jnp.concatenate([ref[pair, :, lanes] for ref in keyval], axis=0)


KEYS, VALUES = slice(0, LANES), slice(LANES, 2 * LANES)


def attend_kernel(group, count, layout_ref, *refs):
    query, keyval = refs[:count], refs[count : count + 4]
    mixed, logsum = refs[count + 4 : 2 * count + 4], refs[2 * count + 4 : 3 * count + 4]
    bias_ref = refs[3 * count + 4]
    span = query[0].shape[0]
    blocks = [slice(q * span, (q + 1) * span) for q in range(count)]

    @pl.when(pl.program_id(0) == 0)
    def _():
        for q in range(count):
            column = as_column(segments_of(layout_ref, q, group, span))
            for k in range(4):
                row = segments_of(layout_ref, k, group, span)
                for c in range(0, span, LANES):
                    bias_ref[blocks[q], k * span + c : k * span + c + LANES] = jnp.where(
                        column == row[:, c : c + LANES], 0.0, -1e30
                    )

    lanes = lax.broadcasted_iota(jnp.int32, (count * span, LANES), 1)
    for p in range(keyval[0].shape[0]):
        here = slice(p * LANES, (p + 1) * LANES)
        keys = stacked(keyval, p, KEYS)
        values = stacked(keyval, p, VALUES)
        asked = jnp.concatenate([ref[:, here] for ref in query], axis=0)
        scores = [dot_nt(one_head(asked, h), keys) for h in range(2)]
        sums, tops = [], []
        for h in range(2):
            biased = scores[h] + bias_ref[...]
            peak = jnp.max(biased, axis=1, keepdims=True)
            expo = jnp.exp(biased - peak)
            total = jnp.sum(expo, axis=1, keepdims=True)
            sums.append(dot_nn(expo.astype(jnp.bfloat16), values) / total)
            tops.append(peak + jnp.log(total))
        result = jnp.where(lanes < HEAD, sums[0], sums[1]).astype(jnp.bfloat16)
        top = jnp.where(lanes == 0, tops[0], tops[1])
        for q in range(count):
            mixed[q][:, here] = result[blocks[q]]
            logsum[q][p] = top[blocks[q]].T[:2, :]


def attend(layout, query, keyval, group):
    count = len(query)
    span, width = query[0].shape
    pairs = width // LANES
    some = 2
    by_pair = pl.BlockSpec((span, some * LANES), lambda i, at: (0, i))
    return pl.pallas_call(
        functools.partial(attend_kernel, group, count),
        grid_spec=pltpu.PrefetchScalarGridSpec(
            num_scalar_prefetch=1,
            grid=(pairs // some,),
            in_specs=[by_pair] * count
            + [pl.BlockSpec((some, span, 2 * LANES), lambda i, at: (i, 0, 0))] * 4,
            out_specs=[by_pair] * count
            + [pl.BlockSpec((some, 2, span), lambda i, at: (i, 0, 0))] * count,
            scratch_shapes=[pltpu.VMEM((count * span, 4 * span), jnp.float32)],
        ),
        out_shape=[jax.ShapeDtypeStruct((span, width), jnp.bfloat16)] * count
        + [jax.ShapeDtypeStruct((pairs, 2, span), jnp.float32)] * count,
        compiler_params=pltpu.CompilerParams(vmem_limit_bytes=VMEM_LIMIT),
        cost_estimate=lasting(9 * count),
    )(layout, *query, *keyval)


def attend_back_kernel(group, count, layout_ref, *refs):
    refs = list(refs)

    def take(number):
        taken = refs[:number]
        del refs[:number]
        return taken

    query, mixed, grad = take(count), take(count), take(count)
    logsum, angle, keyval = take(count), take(count), take(4)
    query_grad = take(count)
    near_ref, far_ref, bias_ref = refs
    span = query[0].shape[0]

    @pl.when(pl.program_id(0) == 0)
    def _():
        for k in range(4):
            column = as_column(segments_of(layout_ref, k, group, span))
            for q in range(count):
                row = segments_of(layout_ref, q, group, span)
                for c in range(0, span, LANES):
                    bias_ref[q, k * span : (k + 1) * span, c : c + LANES] = jnp.where(
                        column == row[:, c : c + LANES], 0.0, -1e30
                    )

    for p in range(keyval[0].shape[0]):
        here = slice(p * LANES, (p + 1) * LANES)
        keys = stacked(keyval, p, KEYS)
        values = stacked(keyval, p, VALUES)
        keys_turned = jnp.concatenate([ref[p, :, KEYS].T for ref in keyval], axis=1)
        key_grad = value_grad = None
        for q in range(count):
            weighed = mixed[q][:, here].astype(jnp.float32) * grad[q][:, here].astype(jnp.float32)
            weighed = weighed.T
            heads = []
            for h in range(2):
                chosen = one_head(query[q][:, here], h)
                chosen_grad = one_head(grad[q][:, here], h)
                own = slice(h * HEAD, (h + 1) * HEAD)
                delta = jnp.sum(weighed[own, :], axis=0, keepdims=True)
                scores = dot_nt(keys, chosen) + bias_ref[q]
                prob_grad = dot_nt(values, chosen_grad)
                probs = jnp.exp(scores - logsum[q][p, h : h + 1, :])
                term = dot_nn(probs.astype(jnp.bfloat16), chosen_grad)
                value_grad = term if value_grad is None else value_grad + term
                score_grad = (probs * (prob_grad - delta)).astype(jnp.bfloat16)
                term = dot_nn(score_grad, chosen)
                key_grad = term if key_grad is None else key_grad + term
                heads.append(dot_nn(keys_turned[own, :], score_grad))
            back = jnp.concatenate(heads, axis=0).T * 0.125
            (back,) = turned(back, angle[q][0], -angle[q][1])
            query_grad[q][:, here] = back.astype(jnp.bfloat16)
        for k in range(4):
            ref = near_ref if k < 2 else far_ref
            rows = slice(k * span, (k + 1) * span)
            ref[k % 2, p, :, KEYS] = key_grad[rows].astype(ref.dtype)
            ref[k % 2, p, :, VALUES] = value_grad[rows].astype(ref.dtype)


def attend_back(
    layout, query, mixed, grad, logsum, angle, keyval, group, first=0, last=None, some=1
):
    count = len(query)
    span, width = query[0].shape
    pairs = (last or width // LANES) - first
    start = first // some
    by_pair = pl.BlockSpec((span, some * LANES), lambda i, at: (0, start + i))
    two_blocks = pl.BlockSpec((2, some, span, 2 * LANES), lambda i, at: (0, i, 0, 0))
    two_shape = jax.ShapeDtypeStruct((2, pairs, span, 2 * LANES), jnp.bfloat16)
    return pl.pallas_call(
        functools.partial(attend_back_kernel, group, count),
        grid_spec=pltpu.PrefetchScalarGridSpec(
            num_scalar_prefetch=1,
            grid=(pairs // some,),
            in_specs=[by_pair] * (3 * count)
            + [pl.BlockSpec((some, 2, span), lambda i, at: (start + i, 0, 0))] * count
            + [pl.BlockSpec((2, span, LANES), lambda i, at: (0, 0, 0))] * count
            + [pl.BlockSpec((some, span, 2 * LANES), lambda i, at: (start + i, 0, 0))] * 4,
            out_specs=[pl.BlockSpec((span, some * LANES), lambda i, at: (0, i))] * count
            + [two_blocks] * 2,
            scratch_shapes=[pltpu.VMEM((count, 4 * span, span), jnp.float32)],
        ),
        out_shape=[jax.ShapeDtypeStruct((span, pairs * LANES), jnp.bfloat16)] * count
        + [two_shape] * 2,
        compiler_params=pltpu.CompilerParams(vmem_limit_bytes=VMEM_LIMIT),
        cost_estimate=lasting(2 * count * pairs),
    )(layout, *query, *mixed, *grad, *logsum, *angle, *keyval)


def group_of(block):
    return 0 if block < 2 else 1


def feed_kernel(*refs):
    mixed, hidden, cotan = refs[0:3], refs[3:6], refs[6:9]
    mod_ref, gain_ref, w_out_ref, w_one_ref, b_one_ref, w_two_ref, b_two_ref = refs[9:16]
    result, mixed_grad = refs[16:19], refs[19:22]
    resid_ref, low_ref, chunks_ref, b_one_grad, sums_ref = refs[22:27]
    second_ref, turned_ref, branch_low_ref, branch_ref, second_grad_ref, act_ref, pre_ref = refs[27:34]
    attended_ref = refs[34]
    step = pl.program_id(0)
    span = hidden[0].shape[0]

    def modulation(block, which):
        return mod_ref[group_of(block), which : which + 1, :]

    @pl.when(step == 0)
    def _():
        bias_sum = None
        for b in range(3):
            rows = slice(b * span, (b + 1) * span)
            attended = dot_nn(mixed[b][...], w_out_ref[...])
            attended_ref[rows, :] = attended
            resid = hidden[b][...].astype(jnp.float32) + modulation(b, 2) * attended
            resid_ref[rows, :] = resid
            values, _ = normalized(resid)
            second = values * gain_ref[...] * (1.0 + modulation(b, 4)) + modulation(b, 3)
            second = second.astype(jnp.bfloat16)
            second_ref[rows, :] = second
            turned_ref[:, rows] = second.T
            branch_grad = modulation(b, 5) * cotan[b][...].astype(jnp.float32)
            branch_low_ref[rows, :] = branch_grad.astype(jnp.bfloat16)
            part = column_sum(branch_grad)
            bias_sum = part if bias_sum is None else bias_sum + part
        sums_ref[...] = jnp.zeros_like(sums_ref)
        sums_ref[1:2, :] = bias_sum
        branch_ref[...] = jnp.zeros_like(branch_ref)
        second_grad_ref[...] = jnp.zeros_like(second_grad_ref)

    b_one_grad[...] = jnp.zeros_like(b_one_grad)

    for b in range(3):
        rows = slice(b * span, (b + 1) * span)
        pre = dot_nn(second_ref[rows, :], w_one_ref[...]) + b_one_ref[...]
        square = pre * pre
        tanh = jnp.tanh(GELU_A * pre * (1.0 + GELU_B * square))
        half = 0.5 * (1.0 + tanh)
        active = (pre * half).astype(jnp.bfloat16)
        act_ref[rows, :] = active
        branch_ref[rows, :] += dot_nn(active, w_two_ref[...])
        slope = half + 0.5 * GELU_A * pre * (1.0 - tanh * tanh) * (1.0 + 3.0 * GELU_B * square)
        pre_grad = dot_nt(branch_low_ref[rows, :], w_two_ref[...]) * slope
        b_one_grad[0] += column_sum(pre_grad)
        pre_low = pre_grad.astype(jnp.bfloat16)
        pre_ref[rows, :] = pre_low
        second_grad_ref[rows, :] += dot_nt(pre_low, w_one_ref[...])

    chunks_ref[0, 0] = dot_nn(turned_ref[...], pre_ref[...]).astype(jnp.bfloat16)
    chunks_ref[0, 1] = dot_tn(act_ref[...], branch_low_ref[...]).astype(jnp.bfloat16)

    @pl.when(step == 3)
    def _():
        for b in range(3):
            at = 2 + 4 * group_of(b)
            rows = slice(b * span, (b + 1) * span)
            resid = resid_ref[rows, :]
            branch = branch_ref[rows, :] + b_two_ref[...]
            result[b][...] = (resid + modulation(b, 5) * branch).astype(jnp.bfloat16)
            upstream = cotan[b][...].astype(jnp.float32)
            sums_ref[at + 3 : at + 4, :] += column_sum(upstream * branch)
            values, inverse = normalized(resid)
            grad = second_grad_ref[rows, :]
            sums_ref[at + 1 : at + 2, :] += column_sum(grad)
            weighed = column_sum(grad * values)
            sums_ref[at + 2 : at + 3, :] += weighed * gain_ref[...]
            sums_ref[0:1, :] += weighed * (1.0 + modulation(b, 4))
            inner = grad * ((1.0 + modulation(b, 4)) * gain_ref[...])
            back = (inner - row_mean(inner) - values * row_mean(inner * values)) * inverse
            resid_grad = upstream + back
            resid_ref[rows, :] = resid_grad
            sums_ref[at : at + 1, :] += column_sum(resid_grad * attended_ref[rows, :])
            low = (modulation(b, 2) * resid_grad).astype(jnp.bfloat16)
            low_ref[rows, :] = low
            mixed_grad[b][...] = dot_nt(low, w_out_ref[...]).astype(jnp.bfloat16)


def feed(mixed, hidden, cotan, mod, gain, w_out, w_one, b_one, w_two, b_two):
    span, width = hidden[0].shape
    tokens = 3 * span
    once = pl.Buffered(1)
    block = pl.BlockSpec((span, width), lambda i: (0, 0), pipeline_mode=once)
    out_block = pl.BlockSpec((span, width), lambda i: (0, 0))
    every = pl.BlockSpec((tokens, width), lambda i: (0, 0))
    row = pl.BlockSpec((1, width), lambda i: (0, 0))
    chunk = pl.BlockSpec((1, 2, width, width), lambda i: (i, 0, 0, 0))
    low_block = jax.ShapeDtypeStruct((span, width), jnp.bfloat16)
    chunks = jax.ShapeDtypeStruct((4, 2, width, width), jnp.bfloat16)
    return pl.pallas_call(
        feed_kernel,
        grid_spec=pl.GridSpec(
            grid=(4,),
            in_specs=[block] * 9
            + [
                pl.BlockSpec(mod.shape, lambda i: (0, 0, 0)),
                row,
                pl.BlockSpec((width, width), lambda i: (0, 0), pipeline_mode=once),
                pl.BlockSpec((width, width), lambda i: (0, i)),
                pl.BlockSpec((1, width), lambda i: (0, i)),
                pl.BlockSpec((width, width), lambda i: (i, 0)),
                row,
            ],
            out_specs=[out_block] * 6
            + [every, every, chunk]
            + [
                pl.BlockSpec((1, 1, width), lambda i: (i, 0, 0)),
                pl.BlockSpec((16, width), lambda i: (0, 0)),
            ],
            scratch_shapes=[
                pltpu.VMEM((tokens, width), jnp.bfloat16),
                pltpu.VMEM((width, tokens), jnp.bfloat16),
                pltpu.VMEM((tokens, width), jnp.bfloat16),
                pltpu.VMEM((tokens, width), jnp.float32),
                pltpu.VMEM((tokens, width), jnp.float32),
                pltpu.VMEM((tokens, width), jnp.bfloat16),
                pltpu.VMEM((tokens, width), jnp.bfloat16),
                pltpu.VMEM((tokens, width), jnp.float32),
            ],
        ),
        out_shape=[low_block] * 6
        + [
            jax.ShapeDtypeStruct((tokens, width), jnp.float32),
            jax.ShapeDtypeStruct((tokens, width), jnp.bfloat16),
        ]
        + [chunks]
        + [
            jax.ShapeDtypeStruct((4, 1, width), jnp.float32),
            jax.ShapeDtypeStruct((16, width), jnp.float32),
        ],
        compiler_params=pltpu.CompilerParams(vmem_limit_bytes=VMEM_LIMIT),
        cost_estimate=lasting(40),
    )(*mixed, *hidden, *cotan, mod, gain, w_out, w_one, b_one, w_two, b_two)


def merge_kernel(parts, second, places_ref, *refs):
    refs = list(refs)

    def take(count):
        taken = refs[:count]
        del refs[:count]
        return taken

    own_parts = [(first, last, take(4 if second else 2)) for first, last in parts[0]]
    split_parts = [(first, last, take(4 if second else 1)) for first, last in parts[1]]
    angle, normed, mixed = take(3), take(3), take(3)
    (low_ref,) = take(1)
    send_ref, keep_ref = take(2)
    merged_refs = take(2 if second else 1)
    normed_ref, mixed_ref = refs
    step = pl.program_id(0)
    first_chunk = (step ^ places_ref[0]) == 1
    span, width = normed[0].shape
    pairs = width // LANES

    @pl.when(step == 0)
    def _():
        for b in range(3):
            rows = slice(b * span, (b + 1) * span)
            normed_ref[:, rows] = normed[b][...].T
            if not second:
                mixed_ref[:, rows] = mixed[b][...].T

    def part_of(block, pair):
        for first, last, arrays in split_parts if block == 2 else own_parts:
            if first <= pair < last:
                return pair - first, arrays

    def keyval_sum(block, pair, lanes):
        at, arrays = part_of(block, pair)
        if block == 2:
            _, near, got, got_chip = arrays
            terms = near[0, at, :, lanes], got[0, at, :, lanes], got_chip[at, :, lanes]
        else:
            _, _, near, got = arrays
            terms = near[block, at, :, lanes], got[block, at, :, lanes]
        return sum(term.astype(jnp.float32) for term in terms)

    def put(result):
        @pl.when(step == 0)
        def _():
            send_ref[0] = result

        @pl.when(step == 1)
        def _():
            keep_ref[0] = result

    def fill(merged_ref, kind):
        for b in range(3):
            rows = slice(b * span, (b + 1) * span)
            for c in range(pairs):
                lanes = slice(c * LANES, (c + 1) * LANES)
                if kind == "q":
                    at, arrays = part_of(b, c)
                    piece = arrays[b % 2][:, at * LANES : (at + 1) * LANES]
                elif kind == "k":
                    (piece,) = turned(keyval_sum(b, c, KEYS), angle[b][0], -angle[b][1])
                else:
                    piece = keyval_sum(b, c, VALUES)
                merged_ref[rows, lanes] = piece.astype(jnp.bfloat16)
        put(dot_nn(normed_ref[...], merged_ref[...]).astype(jnp.bfloat16))

    @pl.when(first_chunk)
    def _():
        fill(merged_refs[0], "k" if second else "q")

    @pl.when(jnp.logical_not(first_chunk))
    def _():
        if second:
            fill(merged_refs[1], "v")
        else:
            put(dot_nn(mixed_ref[...], low_ref[...]).astype(jnp.bfloat16))


def merge_back(places, own_parts, split_parts, angle, normed, mixed, low, second):
    span, width = normed[0].shape
    tokens = 3 * span
    once = pl.Buffered(1)

    def whole(array):
        return pl.BlockSpec(
            array.shape, lambda i, at: (0,) * len(array.shape), pipeline_mode=once
        )

    operands = [array for _, _, arrays in own_parts + split_parts for array in arrays]
    operands += [*angle, *normed, *mixed, low]
    parts = [[(first, last) for first, last, _ in group] for group in (own_parts, split_parts)]
    chunk_shape = jax.ShapeDtypeStruct((1, width, width), jnp.bfloat16)
    merged_shape = jax.ShapeDtypeStruct((tokens, width), jnp.bfloat16)
    merged_count = 2 if second else 1
    return pl.pallas_call(
        functools.partial(merge_kernel, parts, second),
        grid_spec=pltpu.PrefetchScalarGridSpec(
            num_scalar_prefetch=1,
            grid=(2,),
            in_specs=[whole(array) for array in operands],
            out_specs=[pl.BlockSpec((1, width, width), lambda i, at: (0, 0, 0))] * 2
            + [pl.BlockSpec((tokens, width), lambda i, at: (0, 0))] * merged_count,
            scratch_shapes=[
                pltpu.VMEM((width, tokens), jnp.bfloat16),
                pltpu.VMEM((width, tokens), jnp.bfloat16),
            ],
        ),
        out_shape=[chunk_shape] * 2 + [merged_shape] * merged_count,
        compiler_params=pltpu.CompilerParams(vmem_limit_bytes=VMEM_LIMIT),
        cost_estimate=lasting(9),
    )(places, *operands)


def enter_kernel(*refs):
    hidden = refs[0:3]
    resid_grad_ref, mod_ref, gain_ref = refs[3:6]
    merged, weight_ref = refs[6:9], refs[9]
    hidden_grad = refs[10:13]
    sums_ref, total_ref = refs[13:]
    step = pl.program_id(0)
    span = hidden[0].shape[0]

    @pl.when(step == 0)
    def _():
        total_ref[...] = jnp.zeros_like(total_ref)

    for k in range(3):

        @pl.when(step == k)
        def _(k=k):
            total_ref[...] += dot_nt(merged[k][...], weight_ref[...])

    @pl.when(step == 2)
    def _():
        sums_ref[...] = jnp.zeros_like(sums_ref)
        for b in range(3):
            group = group_of(b)
            at = 1 + 2 * group
            rows = slice(b * span, (b + 1) * span)
            values, inverse = normalized(hidden[b][...].astype(jnp.float32))
            grad = total_ref[rows, :]
            scaled = 1.0 + mod_ref[group, 1:2, :]
            weighed = column_sum(grad * values)
            sums_ref[0:1, :] += weighed * scaled
            sums_ref[at : at + 1, :] += column_sum(grad)
            sums_ref[at + 1 : at + 2, :] += weighed * gain_ref[...]
            inner = grad * (scaled * gain_ref[...])
            back = (inner - row_mean(inner) - values * row_mean(inner * values)) * inverse
            hidden_grad[b][...] = (resid_grad_ref[rows, :] + back).astype(jnp.bfloat16)


def enter_back(hidden, resid_grad, mod, gain, merged, weight):
    span, width = hidden[0].shape
    tokens = 3 * span
    once = pl.Buffered(1)
    block = pl.BlockSpec((span, width), lambda i: (0, 0), pipeline_mode=once)
    return pl.pallas_call(
        enter_kernel,
        grid=(3,),
        in_specs=[block] * 3
        + [
            pl.BlockSpec((tokens, width), lambda i: (0, 0), pipeline_mode=once),
            pl.BlockSpec(mod.shape, lambda i: (0, 0, 0)),
            pl.BlockSpec(gain.shape, lambda i: (0, 0)),
            *[pl.BlockSpec((tokens, width), lambda i: (0, 0), pipeline_mode=once)] * 3,
            pl.BlockSpec((width, width), lambda i: (0, i)),
        ],
        out_specs=[pl.BlockSpec((span, width), lambda i: (0, 0))] * 3
        + [pl.BlockSpec((8, width), lambda i: (0, 0))],
        out_shape=[jax.ShapeDtypeStruct((span, width), jnp.bfloat16)] * 3
        + [jax.ShapeDtypeStruct((8, width), jnp.float32)],
        scratch_shapes=[pltpu.VMEM((tokens, width), jnp.float32)],
        compiler_params=pltpu.CompilerParams(vmem_limit_bytes=VMEM_LIMIT),
        cost_estimate=lasting(10),
    )(*hidden, resid_grad, mod, gain, *merged, weight)


def swap(values, axis, bit):
    count = lax.axis_size(axis)
    return lax.ppermute(values, axis, [(i, i ^ bit) for i in range(count)])


def bit_of(axis, bit):
    return (lax.axis_index(axis) // bit) % 2


def batch_bits():
    count = lax.axis_size("batch")
    bits = []
    bit = 1
    while bit < count:
        bits.append(bit)
        bit *= 2
    return bits


def split_orders():
    bits = batch_bits()
    chip = ("seq", 2)
    split = [("batch", b) for b in bits[:3]]
    rest = [("batch", b) for b in bits[3:]]
    return ([chip] + split, split[:1] + [chip] + split[1:], rest)


def place_scalars():
    order_a, order_b, _ = split_orders()
    bits = [bit_of(axis, bit) for axis, bit in order_a + order_b]
    return jnp.stack([lax.axis_index("seq") % 2, *bits]).astype(jnp.int32)


def bits_value(at, group, steps, first, last, flip):
    value = jnp.int32(0)
    for d in range(first, last):
        bit = at[1 + group * steps + d]
        if flip and d == last - 1:
            bit = 1 - bit
        value = value * 2 + bit
    return value


def total_kernel(counts, places_ref, *refs):
    inputs, outputs = refs[: sum(counts)], refs[sum(counts) :]
    start = 0
    for g, count in enumerate(counts):
        total = inputs[start][0].astype(jnp.float32)
        for ref in inputs[start + 1 : start + count]:
            total = total + ref[0].astype(jnp.float32)
        start += count
        if len(outputs) == 1:
            outputs[0][g] = total.astype(jnp.bfloat16)
        else:
            outputs[g][0] = total.astype(jnp.bfloat16)


def total_of_parts(places, parts, steps, done, flip, joint):
    rows = parts[0][0][0].shape[1] >> done
    width = parts[0][0][0].shape[2]
    cuts = max(1, rows // 192)
    rows //= cuts
    operands, specs = [], []
    for g, group in enumerate(parts):
        for array, lead, level in group:
            operands.append(array)
            specs.append(
                pl.BlockSpec(
                    (1, rows, width),
                    lambda i, at, g=g, lead=lead, level=level: (
                        lead,
                        bits_value(at, g, steps, level, done, flip) * cuts + i,
                        0,
                    ),
                )
            )
    if joint:
        out_specs = [pl.BlockSpec((2, rows, width), lambda i, at: (0, i, 0))]
        out_shape = [jax.ShapeDtypeStruct((2, cuts * rows, width), jnp.bfloat16)]
    else:
        out_specs = [pl.BlockSpec((1, rows, width), lambda i, at: (0, i, 0))] * 2
        out_shape = [jax.ShapeDtypeStruct((1, cuts * rows, width), jnp.bfloat16)] * 2
    return pl.pallas_call(
        functools.partial(total_kernel, [len(group) for group in parts]),
        grid_spec=pltpu.PrefetchScalarGridSpec(
            num_scalar_prefetch=1, grid=(cuts,), in_specs=specs, out_specs=out_specs
        ),
        out_shape=out_shape,
        compiler_params=pltpu.CompilerParams(vmem_limit_bytes=VMEM_LIMIT),
        cost_estimate=lasting(3),
    )(places, *operands)


def join_kernel(left_ref, right_ref, out_ref):
    count = left_ref.shape[1]
    out_ref[:, :count] = left_ref[...]
    out_ref[:, count:] = right_ref[...]


def join(left, right):
    lead, count, rows, width = left.shape
    spec = pl.BlockSpec((lead, count, rows, width), lambda i: (0, 0, 0, 0))
    return pl.pallas_call(
        join_kernel,
        grid=(1,),
        in_specs=[spec, spec],
        out_specs=pl.BlockSpec((lead, 2 * count, rows, width), lambda i: (0, 0, 0, 0)),
        out_shape=jax.ShapeDtypeStruct((lead, 2 * count, rows, width), left.dtype),
        compiler_params=pltpu.CompilerParams(vmem_limit_bytes=VMEM_LIMIT),
        cost_estimate=lasting(2),
    )(left, right)


def after(values, *others):
    return lax.optimization_barrier((values, others))[0]


def sync_steps(places, send, keep, gather=True):
    order_a, order_b, rest = split_orders()
    steps = len(order_a)
    if isinstance(send, list):
        got = [swap(part, "seq", 1) for part in send]
        got = after(got, (yield send))
        held = [[(keep[g], 0, 0), (got[g], 0, 0)] for g in range(2)]
    else:
        got = swap(send, "seq", 1)
        got = after(got, (yield [send]))
        held = [[(keep, g, 0), (got, g, 0)] for g in range(2)]
    parts = held
    for done, dims in enumerate(zip(order_a, order_b), 1):
        joint = dims[0] == dims[1]
        sent = total_of_parts(places, parts, steps, done, True, joint)
        if joint:
            got = [swap(sent[0], *dims[0])] * 2
        else:
            got = [swap(sent[g], *dims[g]) for g in range(2)]
        got = after(got, (yield sent))
        for g in range(2):
            parts[g].append((got[g], g if joint else 0, done))
    (held,) = total_of_parts(places, parts, steps, steps, False, True)
    for axis, bit in rest:
        held = (held.astype(jnp.float32) + swap(held, axis, bit).astype(jnp.float32)).astype(
            held.dtype
        )
    if not gather:
        return held
    blocks = held[:, None]
    for dims in reversed(list(zip(order_a, order_b))):
        if dims[0] == dims[1]:
            got = swap(blocks, *dims[0])
            got = after(got, (yield [blocks]))
            blocks = join(blocks, got)
        else:
            if not isinstance(blocks, list):
                blocks = [blocks[0:1], blocks[1:2]]
            got = [swap(blocks[g], *dims[g]) for g in range(2)]
            if dims == (order_a[0], order_b[0]):
                far = [swap(piece, "seq", 1) for piece in blocks]
                ties = yield [*blocks, *far]
                got = after(got, ties)
                far_got = [swap(piece, "seq", 1) for piece in got]
                return [*got, *far_got]
            got = after(got, (yield blocks))
            blocks = [join(blocks[g], got[g]) for g in range(2)]


HEAD_ROWS, ROW_BLOCK = 8, 24


def pack_kernel(places_ref, feed_ref, merge_ref, bias_ref, cond_ref, out_ref):
    out_ref[...] = jnp.zeros_like(out_ref)
    out_ref[0:1, :] = merge_ref[0:1, :]
    out_ref[1:3, :] = feed_ref[0:2, :]
    for c in range(bias_ref.shape[0]):
        out_ref[3 + c : 4 + c, :] = bias_ref[c]
    for group in range(2):
        merged = merge_ref[1 + 2 * group : 3 + 2 * group, :]
        fed = feed_ref[2 + 4 * group : 6 + 4 * group, :]
        for j in range(6):
            value = merged[j : j + 1, :] if j < 2 else fed[j - 2 : j - 1, :]
            at = HEAD_ROWS + 3 * j
            if group == 1:
                out_ref[at + 2 : at + 3, :] = value
                continue
            for chip in range(2):
                out_ref[at + chip : at + chip + 1, :] = jnp.where(
                    places_ref[0] // 2 == chip, value, 0.0
                )
    rows, count = cond_ref.shape
    for r in range(rows):
        out_ref[HEAD_ROWS + 18 : HEAD_ROWS + 19, r * count : (r + 1) * count] = (
            cond_ref[r : r + 1, :] * 0.25
        )


def pack_small(seat, feed_sums, merge_sums, bias_grad, cond):
    width = feed_sums.shape[1]

    def whole(array):
        return pl.BlockSpec(array.shape, lambda i, at: (0,) * len(array.shape))

    operands = [feed_sums, merge_sums, bias_grad, cond]
    rows = HEAD_ROWS + ROW_BLOCK
    return pl.pallas_call(
        pack_kernel,
        grid_spec=pltpu.PrefetchScalarGridSpec(
            num_scalar_prefetch=1,
            grid=(1,),
            in_specs=[whole(array) for array in operands],
            out_specs=pl.BlockSpec((rows, width), lambda i, at: (0, 0)),
        ),
        out_shape=jax.ShapeDtypeStruct((rows, width), jnp.float32),
        cost_estimate=lasting(2),
    )(seat, *operands)


def grow_kernel(own_ref, got_ref, out_ref):
    rows = own_ref.shape[0]
    out_ref[:HEAD_ROWS] = own_ref[:HEAD_ROWS] + got_ref[:HEAD_ROWS]
    out_ref[HEAD_ROWS:rows] = own_ref[HEAD_ROWS:]
    out_ref[rows:] = got_ref[HEAD_ROWS:]


def grow(own, got):
    rows, width = own.shape
    return pl.pallas_call(
        grow_kernel,
        out_shape=jax.ShapeDtypeStruct((2 * rows - HEAD_ROWS, width), own.dtype),
        cost_estimate=lasting(2),
    )(own, got)


class SmallSums:
    def __init__(self, values):
        self.values = values
        self.dims = [("seq", 1), ("seq", 2)] + [("batch", b) for b in batch_bits()]
        self.pending = None

    def step(self, *done):
        self.take(*done)
        if self.dims:
            self.axis, bit = self.dims.pop(0)
            self.pending = swap(self.values, self.axis, bit)

    def take(self, *done):
        if self.pending is None:
            return
        got = after(self.pending, *done) if done else self.pending
        self.pending = None
        self.values = self.values + got if self.axis == "seq" else grow(self.values, got)

    def finish(self, *done):
        while self.dims:
            self.step(*done)
        self.take(*done)


def modulation_kernel(values_ref, weight_ref, cond_ref, bias_ref, grad_ref):
    values = values_ref[HEAD_ROWS:, :]
    rows, width = values.shape
    count = weight_ref.shape[0]
    conds = []
    for block in range(rows // ROW_BLOCK):
        line = values[block * ROW_BLOCK + 18 : block * ROW_BLOCK + 19, :]
        three = [line[:, r * count : (r + 1) * count] for r in range(3)]
        conds += three * 6 + [jnp.zeros((ROW_BLOCK - 18, count), jnp.float32)]
    conds = jnp.concatenate(conds, axis=0)
    place = lax.broadcasted_iota(jnp.int32, (rows, count), 0) % ROW_BLOCK // 3
    wide_place = lax.broadcasted_iota(jnp.int32, (rows, width), 0) % ROW_BLOCK // 3
    total = None
    for j in range(6):
        lanes = slice(j * width, (j + 1) * width)
        grad_ref[:, lanes] = lax.dot_general(
            jnp.where(place == j, conds, 0.0),
            values,
            (((0,), (0,)), ((), ())),
            precision=highest,
            preferred_element_type=jnp.float32,
        )
        bias_ref[:, lanes] = column_sum(jnp.where(wide_place == j, values, 0.0))
        term = lax.dot_general(
            values[3 * j : 3 * j + 3, :],
            weight_ref[:, lanes].astype(jnp.float32),
            (((1,), (1,)), ((), ())),
            precision=highest,
            preferred_element_type=jnp.float32,
        )
        total = term if total is None else total + term
    cond_ref[...] = total


def modulation_back(values, weight):
    count, wide = weight.shape
    return pl.pallas_call(
        modulation_kernel,
        out_shape=[
            jax.ShapeDtypeStruct((3, count), jnp.float32),
            jax.ShapeDtypeStruct((1, wide), jnp.float32),
            jax.ShapeDtypeStruct((count, wide), jnp.float32),
        ],
        compiler_params=pltpu.CompilerParams(vmem_limit_bytes=VMEM_LIMIT),
        cost_estimate=lasting(7),
    )(values, weight)


def run_on(steps, *done):
    try:
        return steps.send(done), None
    except StopIteration as end:
        return None, end.value


def spread_blocks(places_ref, ref, group, out):
    _, count, rows, _ = ref.shape
    steps = count.bit_length()
    place = bits_value(places_ref, group, steps, 1, steps, False)

    @pl.loop(0, count)
    def _(j):
        row = pl.multiple_of((place ^ j) * rows, 8)
        out[pl.ds(row, rows), :] = ref[0, j].astype(jnp.float32)


def piece_chunk(step, core):
    owner = jnp.where(step < 2, core, 1 - core)
    group = step % 2
    return jnp.where(owner == 0, group, 3 - group)


def finish_feed_kernel(chunks_ref, one_ref, two_ref):
    one_ref[...] = chunks_ref[0, 0].astype(jnp.float32)
    two_ref[...] = chunks_ref[0, 1].astype(jnp.float32)


def finish_feed(chunks):
    count, _, width, _ = chunks.shape
    cuts = 1
    rows = width // cuts
    return pl.pallas_call(
        finish_feed_kernel,
        grid=(count, cuts),
        in_specs=[pl.BlockSpec((1, 2, rows, width), lambda i, j: (i, 0, j, 0))],
        out_specs=[
            pl.BlockSpec((rows, width), lambda i, j: (j, i)),
            pl.BlockSpec((rows, width), lambda i, j: (cuts * i + j, 0)),
        ],
        out_shape=[
            jax.ShapeDtypeStruct((width, count * width), jnp.float32),
            jax.ShapeDtypeStruct((count * width, width), jnp.float32),
        ],
        compiler_params=pltpu.CompilerParams(vmem_limit_bytes=VMEM_LIMIT),
        cost_estimate=lasting(8),
    )(chunks)


def finish_kernel(places_ref, *refs):
    pieces, outs = refs[:4], refs[-2:]
    step = pl.program_id(0)
    chunk = piece_chunk(step, places_ref[0])
    for k in range(4):
        for condition, out in ((chunk < 3, outs[0]), (chunk == 3, outs[1])):

            @pl.when((step == k) & condition)
            def _(ref=pieces[k], group=k % 2, out=out):
                spread_blocks(places_ref, ref, group, out)


def finish_half(places, pieces, second, started=()):
    _, count, rows, width = pieces[0].shape
    steps = count.bit_length()
    half = count * rows
    whole = pl.BlockSpec((1, count, rows, width), lambda i, at: (0, 0, 0, 0))
    anywhere = pl.BlockSpec(memory_space=pl.ANY)

    def side(i, at):
        mine = jnp.where(i % 2 == 0, at[1], at[1 + steps])
        return 1 - mine if second else mine

    return pl.pallas_call(
        finish_kernel,
        grid_spec=pltpu.PrefetchScalarGridSpec(
            num_scalar_prefetch=1,
            grid=(4,),
            in_specs=[whole] * 4 + [anywhere] * len(started),
            out_specs=[
                pl.BlockSpec(
                    (half, width),
                    lambda i, at: (
                        side(jnp.where(piece_chunk(i, at[0]) == 3, i + 1, i), at),
                        jnp.minimum(piece_chunk(i, at[0]), 2),
                    ),
                ),
                pl.BlockSpec((half, width), lambda i, at: (side(0, at), 0)),
            ],
        ),
        out_shape=[
            jax.ShapeDtypeStruct((width, 3 * width), jnp.float32),
            jax.ShapeDtypeStruct((width, width), jnp.float32),
        ],
        input_output_aliases={5 + k: k for k in range(len(started))},
        compiler_params=pltpu.CompilerParams(vmem_limit_bytes=VMEM_LIMIT),
        cost_estimate=lasting(4),
    )(places, *pieces, *started)


def pick(values, index):
    return lax.dynamic_index_in_dim(values, index, 0, keepdims=False)


def rows_of(own, other, third, chip):
    first = jnp.where(chip == 0, own, other)
    second = jnp.where(chip == 0, other, own)
    return jnp.stack([first, second, third])


def shards(
    hidden,
    cond,
    lengths,
    ln1_gain,
    w_qkv,
    w_out,
    ln2_gain,
    w_fc1,
    b_fc1,
    w_fc2,
    b_fc2,
    w_ada,
    b_ada,
    cotangent,
):
    row_count, span, width = hidden.shape
    places = place_scalars()
    seat = lax.axis_index("seq")
    chip = seat // 2
    bases = jnp.stack([seat, seat ^ 2, seat ^ 1, seat ^ 3]) * span
    layout = jnp.concatenate(
        [pick(lengths, chip).reshape(-1), lengths[2], bases.astype(jnp.int32)]
    )
    hidden_far = swap(pick(hidden, 1 - chip), "seq", 2)
    blocks = [pick(hidden, chip), hidden_far, hidden[2]]
    ada_full = w_ada.astype(jnp.float32)
    modulation = (
        jnp.dot(cond, ada_full, precision=highest, preferred_element_type=jnp.float32) + b_ada
    )
    mod = jnp.stack([pick(modulation, chip), modulation[2]]).reshape(2, 6, width)
    gain_one, gain_two = ln1_gain[None], ln2_gain[None]

    normed_own, normed_split, query_own, query_split, kv_own, kv_split, angle_own, angle_split = (
        project(layout, [blocks[0], blocks[2]], mod, gain_one, w_qkv, (0, 1), (0, 0))
    )
    split_chip = swap(kv_split, "seq", 2)
    split_core = swap(kv_split, "seq", 1)
    own_core = swap(kv_own, "seq", 1)
    normed_far, query_far, kv_far, angle_far = project(
        layout, [blocks[1]], mod, gain_one, w_qkv, (0,), (1,)
    )
    far_core = swap(kv_far, "seq", 1)
    cotan_far = swap(pick(cotangent, 1 - chip), "seq", 2)
    cotan = [pick(cotangent, chip), cotan_far, cotangent[2]]
    kv_row = [kv_own, kv_far, own_core, far_core]
    mixed_own, mixed_far, logsum_own, logsum_far = attend(
        after(layout, *kv_row), [query_own, query_far], kv_row, 0
    )
    split_chip = after(split_chip, logsum_own)
    split_cross = swap(split_chip, "seq", 1)
    kv_third = [kv_split, split_chip, split_core, split_cross]
    mixed_split, logsum_split = attend(after(layout, mixed_far), [query_split], kv_third, 1)
    mixed = [mixed_own, mixed_far, mixed_split]
    (
        result_own,
        result_far,
        result_split,
        mixed_grad_own,
        mixed_grad_far,
        mixed_grad_split,
        resid_grad,
        low,
        feed_chunks,
        b_one_grad,
        feed_sums,
    ) = feed(
        mixed,
        blocks,
        cotan,
        mod,
        gain_two,
        w_out,
        w_fc1,
        b_fc1[None],
        w_fc2,
        b_fc2[None],
    )
    everyone = ("seq", "batch")
    feed_share = lax.psum_scatter(
        feed_chunks.reshape(-1, width), everyone, scatter_dimension=0, tiled=True
    )
    pairs = width // LANES

    def back_of_row(sent):
        return attend_back(
            after(layout, sent),
            [query_own, query_far],
            [mixed_own, mixed_far],
            [mixed_grad_own, mixed_grad_far],
            [logsum_own, logsum_far],
            [angle_own, angle_far],
            kv_row,
            0,
        )

    def back_of_split(sent):
        return attend_back(
            after(layout, sent),
            [query_split],
            [mixed_split],
            [mixed_grad_split],
            [logsum_split],
            [angle_split],
            kv_third,
            1,
            some=2,
        )

    split_grad, near_split, far_split = back_of_split(mixed_split)
    got_split = swap(far_split, "seq", 1)
    got_split = after(got_split, split_grad)
    chip_sum = near_split[1].astype(jnp.float32) + got_split[1].astype(jnp.float32)
    chip_sum = chip_sum.astype(jnp.bfloat16)
    chip_split = swap(chip_sum, "seq", 2)
    own_grad, far_grad, near_own, far_own = back_of_row(split_grad)
    tables = [angle_own, angle_far, angle_split], [normed_own, normed_far, normed_split], mixed, low
    send_a, keep_a, merged_q = merge_back(
        after(places, chip_split),
        [(0, pairs, [own_grad, far_grad])],
        [(0, pairs, [split_grad])],
        *tables,
        second=False,
    )
    got_own = swap(far_own, "seq", 1)
    send_b, keep_b, merged_k, merged_v = merge_back(
        after(places, send_a),
        [(0, pairs, [own_grad, far_grad, near_own, got_own])],
        [(0, pairs, [split_grad, near_split, got_split, chip_split])],
        *tables,
        second=True,
    )
    hidden_own_grad, hidden_far_grad, hidden_split_grad, merge_sums = enter_back(
        blocks,
        resid_grad,
        mod,
        gain_one,
        [merged_q, merged_k, merged_v],
        w_qkv,
    )
    att_steps = sync_steps(places, after([send_a, send_b], merge_sums), [keep_a, keep_b])
    sent_att = next(att_steps)
    far_hidden_grad = swap(hidden_far_grad, "seq", 2)
    far_result = swap(after(result_far, merge_sums), "seq", 2)
    small = SmallSums(
        pack_small(seat.astype(jnp.int32)[None], feed_sums, merge_sums, b_one_grad, cond)
    )
    small.step()
    sent_att, _ = run_on(att_steps, merge_sums)
    small.step(sent_att)
    sent_att, _ = run_on(att_steps, small.values)
    small.step(sent_att)
    sent_att, _ = run_on(att_steps, small.values, far_result)
    small.step(sent_att)
    sent_att, _ = run_on(att_steps, small.values, far_hidden_grad)
    feed_whole = lax.all_gather(after(feed_share, sent_att), everyone, axis=0, tiled=True)
    small.step(sent_att)
    sent_att, _ = run_on(att_steps, small.values)
    small.finish(sent_att)
    vectors = small.values[:HEAD_ROWS]
    cond_grad, ada_bias_grad, ada_grad = modulation_back(small.values, w_ada)
    sent_att, _ = run_on(att_steps, vectors)
    output = rows_of(result_own, far_result, result_split, chip)
    hidden_grad = rows_of(hidden_own_grad, far_hidden_grad, hidden_split_grad, chip)
    sent_att, _ = run_on(att_steps, output, hidden_grad)
    ln1_grad, ln2_grad, fc2_bias_grad = vectors[0], vectors[1], vectors[2]
    fc1_bias_grad = vectors[3:7].reshape(-1)
    ada_bias_grad = ada_bias_grad.reshape(-1)
    first_half, _ = run_on(att_steps, ada_grad, cond_grad, ada_bias_grad, fc1_bias_grad)
    first_half = after(first_half, ln1_grad, ln2_grad, fc2_bias_grad)
    started = finish_half(places, first_half, False)
    _, second_half = run_on(att_steps, started[1])
    qkv_grad, out_grad = finish_half(places, second_half, True, started)
    fc1_grad, fc2_grad = finish_feed(after(feed_whole, out_grad).reshape(feed_chunks.shape))
    return (
        output,
        hidden_grad,
        cond_grad,
        ln1_grad,
        qkv_grad,
        out_grad,
        ln2_grad,
        fc1_grad,
        fc1_bias_grad,
        fc2_grad,
        fc2_bias_grad,
        ada_grad,
        ada_bias_grad,
    )


def solution(mesh):
    return jax.shard_map(
        shards,
        mesh=mesh,
        in_specs=(
            P("batch", "seq", None),
            P("batch", None),
            P("batch", None),
            P(),
            P(),
            P(),
            P(),
            P(),
            P(),
            P(),
            P(),
            P(),
            P(),
            P("batch", "seq", None),
        ),
        out_specs=(
            P("batch", "seq", None),
            P("batch", "seq", None),
            P("batch", None),
            P(),
            P(),
            P(),
            P(),
            P(),
            P(),
            P(),
            P(),
            P(),
            P(),
        ),
        check_vma=False,
    )
```

```python
import functools

import jax
import jax.numpy as jnp
from jax import lax
from jax.experimental import pallas as pl
from jax.experimental.pallas import tpu as pltpu
from jax.sharding import PartitionSpec as P

HEADS = 12
HEAD = 64
DOCS = 8
LANES = 128
GELU_A = 0.7978845608
GELU_B = 0.044715
VMEM_LIMIT = 60 * 2**20
SCALE = 0.15


highest = lax.Precision.HIGHEST


def lasting(microseconds):
    flops = int(microseconds * SCALE * 1.15e9)
    return pl.CostEstimate(flops=flops, bytes_accessed=1024, transcendentals=0)


def dot_nt(left, right):
    return lax.dot_general(
        left, right, (((1,), (1,)), ((), ())), preferred_element_type=jnp.float32
    )


def dot_tn(left, right):
    return lax.dot_general(
        left, right, (((0,), (0,)), ((), ())), preferred_element_type=jnp.float32
    )


def dot_nn(left, right):
    return jnp.dot(left, right, preferred_element_type=jnp.float32)


def column_sum(values):
    return jnp.sum(values, axis=0, keepdims=True)


def row_mean(values):
    return jnp.mean(values, axis=-1, keepdims=True)


def normalized(values):
    center = values - row_mean(values)
    inverse = lax.rsqrt(row_mean(center * center) + 1e-05)
    return center * inverse, inverse


def documents_of(slots, layout_ref, group):
    end = jnp.int32(0)
    segment = jnp.zeros_like(slots)
    start = jnp.zeros_like(slots)
    for i in range(DOCS):
        length = layout_ref[group * DOCS + i]
        end = end + length
        passed = slots >= end
        segment = segment + passed.astype(jnp.int32)
        start = start + jnp.where(passed, length, 0)
    return segment, slots - start


def base_of(layout_ref, block):
    return layout_ref[2 * DOCS + block]


def slots_of(layout_ref, block, span):
    return base_of(layout_ref, block) + lax.broadcasted_iota(jnp.int32, (1, span), 1)


def segments_of(layout_ref, block, group, span):
    segment, _ = documents_of(slots_of(layout_ref, block, span), layout_ref, group)
    return segment.astype(jnp.float32)


def as_column(row):
    return jnp.broadcast_to(row, (LANES, row.shape[1])).T


def turned(values, cosine, sine):
    lanes = lax.broadcasted_iota(jnp.int32, cosine.shape, 1)
    first = lanes % HEAD < HEAD // 2
    pieces = []
    for c in range(values.shape[1] // LANES):
        u = values[:, c * LANES : (c + 1) * LANES]
        other = jnp.where(
            first, pltpu.roll(u, LANES - HEAD // 2, 1), pltpu.roll(u, HEAD // 2, 1)
        )
        pieces.append(u * cosine + other * sine)
    return pieces


def project_kernel(groups, bases, layout_ref, *refs):
    count = len(groups)
    hidden = refs[:count]
    mod_ref, gain_ref, speed_ref, weight_ref = refs[count : count + 4]
    normed = refs[count + 4 : 2 * count + 4]
    query = refs[2 * count + 4 : 3 * count + 4]
    keyval = refs[3 * count + 4 : 4 * count + 4]
    angle = refs[4 * count + 4 : 5 * count + 4]
    step = pl.program_id(0)
    span = hidden[0].shape[0]

    @pl.when(step == 0)
    def _():
        for b in range(count):
            values, _ = normalized(hidden[b][...].astype(jnp.float32))
            scale = mod_ref[groups[b], 1:2, :]
            shift = mod_ref[groups[b], 0:1, :]
            normed[b][...] = (values * gain_ref[...] * (1.0 + scale) + shift).astype(jnp.bfloat16)
            _, place = documents_of(slots_of(layout_ref, bases[b], span), layout_ref, groups[b])
            angles = speed_ref[...][:, :1] * place.astype(jnp.float32)
            sine, cosine = jnp.sin(angles), jnp.cos(angles)
            angle[b][0] = jnp.concatenate([cosine] * 4, axis=0).T
            angle[b][1] = jnp.concatenate([-sine, sine] * 2, axis=0).T

    together = dot_nn(
        jnp.concatenate([ref[...] for ref in normed], axis=0), weight_ref[...]
    )
    for b in range(count):
        merged = together[b * span : (b + 1) * span]

        @pl.when(step == 0)
        def _(b=b, merged=merged):
            for c, piece in enumerate(turned(merged, angle[b][0], angle[b][1])):
                query[b][:, c * LANES : (c + 1) * LANES] = (piece * 0.125).astype(jnp.bfloat16)

        @pl.when(step == 1)
        def _(b=b, merged=merged):
            for c, piece in enumerate(turned(merged, angle[b][0], angle[b][1])):
                keyval[b][c, :, :LANES] = piece.astype(jnp.bfloat16)

        @pl.when(step == 2)
        def _(b=b, merged=merged):
            for c in range(merged.shape[1] // LANES):
                keyval[b][c, :, LANES:] = merged[:, c * LANES : (c + 1) * LANES].astype(
                    jnp.bfloat16
                )


def speeds():
    half = 10000.0 ** (-jnp.arange(HEAD // 2, dtype=jnp.float32) * 2.0 / HEAD)
    return jnp.tile(half[:, None], (1, LANES))


def project(layout, hidden, mod, gain, weight, groups, bases):
    count = len(hidden)
    span, width = hidden[0].shape
    pairs = width // LANES
    whole = pl.BlockSpec((span, width), lambda i, at: (0, 0))
    return pl.pallas_call(
        functools.partial(project_kernel, groups, bases),
        grid_spec=pltpu.PrefetchScalarGridSpec(
            num_scalar_prefetch=1,
            grid=(3,),
            in_specs=[whole] * count
            + [
                pl.BlockSpec(mod.shape, lambda i, at: (0, 0, 0)),
                pl.BlockSpec(gain.shape, lambda i, at: (0, 0)),
                pl.BlockSpec((HEAD // 2, LANES), lambda i, at: (0, 0)),
                pl.BlockSpec((width, width), lambda i, at: (0, i)),
            ],
            out_specs=[whole] * (2 * count)
            + [pl.BlockSpec((pairs, span, 2 * LANES), lambda i, at: (0, 0, 0))] * count
            + [pl.BlockSpec((2, span, LANES), lambda i, at: (0, 0, 0))] * count,
        ),
        out_shape=[jax.ShapeDtypeStruct((span, width), jnp.bfloat16)] * (2 * count)
        + [jax.ShapeDtypeStruct((pairs, span, 2 * LANES), jnp.bfloat16)] * count
        + [jax.ShapeDtypeStruct((2, span, LANES), jnp.float32)] * count,
        compiler_params=pltpu.CompilerParams(vmem_limit_bytes=VMEM_LIMIT),
        cost_estimate=lasting(5 * count),
    )(layout, *hidden, mod, gain, speeds(), weight)


def one_head(values, head):
    lanes = lax.broadcasted_iota(jnp.int32, values.shape, 1)
    return jnp.where(lanes // HEAD == head, values, jnp.zeros_like(values))


def stacked(keyval, pair, lanes):
    return jnp.concatenate([ref[pair, :, lanes] for ref in keyval], axis=0)


KEYS, VALUES = slice(0, LANES), slice(LANES, 2 * LANES)


def attend_kernel(group, count, layout_ref, *refs):
    query, keyval = refs[:count], refs[count : count + 4]
    mixed, logsum = refs[count + 4 : 2 * count + 4], refs[2 * count + 4 : 3 * count + 4]
    bias_ref = refs[3 * count + 4]
    span = query[0].shape[0]
    blocks = [slice(q * span, (q + 1) * span) for q in range(count)]

    @pl.when(pl.program_id(0) == 0)
    def _():
        for q in range(count):
            column = as_column(segments_of(layout_ref, q, group, span))
            for k in range(4):
                row = segments_of(layout_ref, k, group, span)
                for c in range(0, span, LANES):
                    bias_ref[blocks[q], k * span + c : k * span + c + LANES] = jnp.where(
                        column == row[:, c : c + LANES], 0.0, -1e30
                    )

    lanes = lax.broadcasted_iota(jnp.int32, (count * span, LANES), 1)
    for p in range(keyval[0].shape[0]):
        here = slice(p * LANES, (p + 1) * LANES)
        keys = stacked(keyval, p, KEYS)
        values = stacked(keyval, p, VALUES)
        asked = jnp.concatenate([ref[:, here] for ref in query], axis=0)
        scores = [dot_nt(one_head(asked, h), keys) for h in range(2)]
        sums, tops = [], []
        for h in range(2):
            biased = scores[h] + bias_ref[...]
            peak = jnp.max(biased, axis=1, keepdims=True)
            expo = jnp.exp(biased - peak)
            total = jnp.sum(expo, axis=1, keepdims=True)
            sums.append(dot_nn(expo.astype(jnp.bfloat16), values) / total)
            tops.append(peak + jnp.log(total))
        result = jnp.where(lanes < HEAD, sums[0], sums[1]).astype(jnp.bfloat16)
        top = jnp.where(lanes == 0, tops[0], tops[1])
        for q in range(count):
            mixed[q][:, here] = result[blocks[q]]
            logsum[q][p] = top[blocks[q]].T[:2, :]


def attend(layout, query, keyval, group):
    count = len(query)
    span, width = query[0].shape
    pairs = width // LANES
    some = 2
    by_pair = pl.BlockSpec((span, some * LANES), lambda i, at: (0, i))
    return pl.pallas_call(
        functools.partial(attend_kernel, group, count),
        grid_spec=pltpu.PrefetchScalarGridSpec(
            num_scalar_prefetch=1,
            grid=(pairs // some,),
            in_specs=[by_pair] * count
            + [pl.BlockSpec((some, span, 2 * LANES), lambda i, at: (i, 0, 0))] * 4,
            out_specs=[by_pair] * count
            + [pl.BlockSpec((some, 2, span), lambda i, at: (i, 0, 0))] * count,
            scratch_shapes=[pltpu.VMEM((count * span, 4 * span), jnp.float32)],
        ),
        out_shape=[jax.ShapeDtypeStruct((span, width), jnp.bfloat16)] * count
        + [jax.ShapeDtypeStruct((pairs, 2, span), jnp.float32)] * count,
        compiler_params=pltpu.CompilerParams(vmem_limit_bytes=VMEM_LIMIT),
        cost_estimate=lasting(9 * count),
    )(layout, *query, *keyval)


def attend_back_kernel(group, count, layout_ref, *refs):
    refs = list(refs)

    def take(number):
        taken = refs[:number]
        del refs[:number]
        return taken

    query, mixed, grad = take(count), take(count), take(count)
    logsum, angle, keyval = take(count), take(count), take(4)
    query_grad = take(count)
    near_ref, far_ref, bias_ref = refs
    span = query[0].shape[0]

    @pl.when(pl.program_id(0) == 0)
    def _():
        for k in range(4):
            column = as_column(segments_of(layout_ref, k, group, span))
            for q in range(count):
                row = segments_of(layout_ref, q, group, span)
                for c in range(0, span, LANES):
                    bias_ref[q, k * span : (k + 1) * span, c : c + LANES] = jnp.where(
                        column == row[:, c : c + LANES], 0.0, -1e30
                    )

    for p in range(keyval[0].shape[0]):
        here = slice(p * LANES, (p + 1) * LANES)
        keys = stacked(keyval, p, KEYS)
        values = stacked(keyval, p, VALUES)
        keys_turned = jnp.concatenate([ref[p, :, KEYS].T for ref in keyval], axis=1)
        key_grad = value_grad = None
        for q in range(count):
            weighed = mixed[q][:, here].astype(jnp.float32) * grad[q][:, here].astype(jnp.float32)
            weighed = weighed.T
            heads = []
            for h in range(2):
                chosen = one_head(query[q][:, here], h)
                chosen_grad = one_head(grad[q][:, here], h)
                own = slice(h * HEAD, (h + 1) * HEAD)
                delta = jnp.sum(weighed[own, :], axis=0, keepdims=True)
                scores = dot_nt(keys, chosen) + bias_ref[q]
                prob_grad = dot_nt(values, chosen_grad)
                probs = jnp.exp(scores - logsum[q][p, h : h + 1, :])
                term = dot_nn(probs.astype(jnp.bfloat16), chosen_grad)
                value_grad = term if value_grad is None else value_grad + term
                score_grad = (probs * (prob_grad - delta)).astype(jnp.bfloat16)
                term = dot_nn(score_grad, chosen)
                key_grad = term if key_grad is None else key_grad + term
                heads.append(dot_nn(keys_turned[own, :], score_grad))
            back = jnp.concatenate(heads, axis=0).T * 0.125
            (back,) = turned(back, angle[q][0], -angle[q][1])
            query_grad[q][:, here] = back.astype(jnp.bfloat16)
        for k in range(4):
            ref = near_ref if k < 2 else far_ref
            rows = slice(k * span, (k + 1) * span)
            ref[k % 2, p, :, KEYS] = key_grad[rows].astype(ref.dtype)
            ref[k % 2, p, :, VALUES] = value_grad[rows].astype(ref.dtype)


def attend_back(
    layout, query, mixed, grad, logsum, angle, keyval, group, first=0, last=None, some=1
):
    count = len(query)
    span, width = query[0].shape
    pairs = (last or width // LANES) - first
    start = first // some
    by_pair = pl.BlockSpec((span, some * LANES), lambda i, at: (0, start + i))
    two_blocks = pl.BlockSpec((2, some, span, 2 * LANES), lambda i, at: (0, i, 0, 0))
    two_shape = jax.ShapeDtypeStruct((2, pairs, span, 2 * LANES), jnp.bfloat16)
    return pl.pallas_call(
        functools.partial(attend_back_kernel, group, count),
        grid_spec=pltpu.PrefetchScalarGridSpec(
            num_scalar_prefetch=1,
            grid=(pairs // some,),
            in_specs=[by_pair] * (3 * count)
            + [pl.BlockSpec((some, 2, span), lambda i, at: (start + i, 0, 0))] * count
            + [pl.BlockSpec((2, span, LANES), lambda i, at: (0, 0, 0))] * count
            + [pl.BlockSpec((some, span, 2 * LANES), lambda i, at: (start + i, 0, 0))] * 4,
            out_specs=[pl.BlockSpec((span, some * LANES), lambda i, at: (0, i))] * count
            + [two_blocks] * 2,
            scratch_shapes=[pltpu.VMEM((count, 4 * span, span), jnp.float32)],
        ),
        out_shape=[jax.ShapeDtypeStruct((span, pairs * LANES), jnp.bfloat16)] * count
        + [two_shape] * 2,
        compiler_params=pltpu.CompilerParams(vmem_limit_bytes=VMEM_LIMIT),
        cost_estimate=lasting(2 * count * pairs),
    )(layout, *query, *mixed, *grad, *logsum, *angle, *keyval)


def group_of(block):
    return 0 if block < 2 else 1


def feed_kernel(*refs):
    mixed, hidden, cotan = refs[0:3], refs[3:6], refs[6:9]
    mod_ref, gain_ref, w_out_ref, w_one_ref, b_one_ref, w_two_ref, b_two_ref = refs[9:16]
    result, mixed_grad = refs[16:19], refs[19:22]
    resid_ref, low_ref, chunks_ref, b_one_grad, sums_ref = refs[22:27]
    second_ref, turned_ref, branch_low_ref, branch_ref, second_grad_ref, act_ref, pre_ref = refs[27:34]
    attended_ref = refs[34]
    step = pl.program_id(0)
    span = hidden[0].shape[0]

    def modulation(block, which):
        return mod_ref[group_of(block), which : which + 1, :]

    @pl.when(step == 0)
    def _():
        bias_sum = None
        for b in range(3):
            rows = slice(b * span, (b + 1) * span)
            attended = dot_nn(mixed[b][...], w_out_ref[...])
            attended_ref[rows, :] = attended
            resid = hidden[b][...].astype(jnp.float32) + modulation(b, 2) * attended
            resid_ref[rows, :] = resid
            values, _ = normalized(resid)
            second = values * gain_ref[...] * (1.0 + modulation(b, 4)) + modulation(b, 3)
            second = second.astype(jnp.bfloat16)
            second_ref[rows, :] = second
            turned_ref[:, rows] = second.T
            branch_grad = modulation(b, 5) * cotan[b][...].astype(jnp.float32)
            branch_low_ref[rows, :] = branch_grad.astype(jnp.bfloat16)
            part = column_sum(branch_grad)
            bias_sum = part if bias_sum is None else bias_sum + part
        sums_ref[...] = jnp.zeros_like(sums_ref)
        sums_ref[1:2, :] = bias_sum
        branch_ref[...] = jnp.zeros_like(branch_ref)
        second_grad_ref[...] = jnp.zeros_like(second_grad_ref)

    b_one_grad[...] = jnp.zeros_like(b_one_grad)

    for b in range(3):
        rows = slice(b * span, (b + 1) * span)
        pre = dot_nn(second_ref[rows, :], w_one_ref[...]) + b_one_ref[...]
        square = pre * pre
        tanh = jnp.tanh(GELU_A * pre * (1.0 + GELU_B * square))
        half = 0.5 * (1.0 + tanh)
        active = (pre * half).astype(jnp.bfloat16)
        act_ref[rows, :] = active
        branch_ref[rows, :] += dot_nn(active, w_two_ref[...])
        slope = half + 0.5 * GELU_A * pre * (1.0 - tanh * tanh) * (1.0 + 3.0 * GELU_B * square)
        pre_grad = dot_nt(branch_low_ref[rows, :], w_two_ref[...]) * slope
        b_one_grad[0] += column_sum(pre_grad)
        pre_low = pre_grad.astype(jnp.bfloat16)
        pre_ref[rows, :] = pre_low
        second_grad_ref[rows, :] += dot_nt(pre_low, w_one_ref[...])

    chunks_ref[0, 0] = dot_nn(turned_ref[...], pre_ref[...]).astype(jnp.bfloat16)
    chunks_ref[0, 1] = dot_tn(act_ref[...], branch_low_ref[...]).astype(jnp.bfloat16)

    @pl.when(step == 3)
    def _():
        for b in range(3):
            at = 2 + 4 * group_of(b)
            rows = slice(b * span, (b + 1) * span)
            resid = resid_ref[rows, :]
            branch = branch_ref[rows, :] + b_two_ref[...]
            result[b][...] = (resid + modulation(b, 5) * branch).astype(jnp.bfloat16)
            upstream = cotan[b][...].astype(jnp.float32)
            sums_ref[at + 3 : at + 4, :] += column_sum(upstream * branch)
            values, inverse = normalized(resid)
            grad = second_grad_ref[rows, :]
            sums_ref[at + 1 : at + 2, :] += column_sum(grad)
            weighed = column_sum(grad * values)
            sums_ref[at + 2 : at + 3, :] += weighed * gain_ref[...]
            sums_ref[0:1, :] += weighed * (1.0 + modulation(b, 4))
            inner = grad * ((1.0 + modulation(b, 4)) * gain_ref[...])
            back = (inner - row_mean(inner) - values * row_mean(inner * values)) * inverse
            resid_grad = upstream + back
            resid_ref[rows, :] = resid_grad
            sums_ref[at : at + 1, :] += column_sum(resid_grad * attended_ref[rows, :])
            low = (modulation(b, 2) * resid_grad).astype(jnp.bfloat16)
            low_ref[rows, :] = low
            mixed_grad[b][...] = dot_nt(low, w_out_ref[...]).astype(jnp.bfloat16)


def feed(mixed, hidden, cotan, mod, gain, w_out, w_one, b_one, w_two, b_two):
    span, width = hidden[0].shape
    tokens = 3 * span
    once = pl.Buffered(1)
    block = pl.BlockSpec((span, width), lambda i: (0, 0), pipeline_mode=once)
    out_block = pl.BlockSpec((span, width), lambda i: (0, 0))
    every = pl.BlockSpec((tokens, width), lambda i: (0, 0))
    row = pl.BlockSpec((1, width), lambda i: (0, 0))
    chunk = pl.BlockSpec((1, 2, width, width), lambda i: (i, 0, 0, 0))
    low_block = jax.ShapeDtypeStruct((span, width), jnp.bfloat16)
    chunks = jax.ShapeDtypeStruct((4, 2, width, width), jnp.bfloat16)
    return pl.pallas_call(
        feed_kernel,
        grid_spec=pl.GridSpec(
            grid=(4,),
            in_specs=[block] * 9
            + [
                pl.BlockSpec(mod.shape, lambda i: (0, 0, 0)),
                row,
                pl.BlockSpec((width, width), lambda i: (0, 0), pipeline_mode=once),
                pl.BlockSpec((width, width), lambda i: (0, i)),
                pl.BlockSpec((1, width), lambda i: (0, i)),
                pl.BlockSpec((width, width), lambda i: (i, 0)),
                row,
            ],
            out_specs=[out_block] * 6
            + [every, every, chunk]
            + [
                pl.BlockSpec((1, 1, width), lambda i: (i, 0, 0)),
                pl.BlockSpec((16, width), lambda i: (0, 0)),
            ],
            scratch_shapes=[
                pltpu.VMEM((tokens, width), jnp.bfloat16),
                pltpu.VMEM((width, tokens), jnp.bfloat16),
                pltpu.VMEM((tokens, width), jnp.bfloat16),
                pltpu.VMEM((tokens, width), jnp.float32),
                pltpu.VMEM((tokens, width), jnp.float32),
                pltpu.VMEM((tokens, width), jnp.bfloat16),
                pltpu.VMEM((tokens, width), jnp.bfloat16),
                pltpu.VMEM((tokens, width), jnp.float32),
            ],
        ),
        out_shape=[low_block] * 6
        + [
            jax.ShapeDtypeStruct((tokens, width), jnp.float32),
            jax.ShapeDtypeStruct((tokens, width), jnp.bfloat16),
        ]
        + [chunks]
        + [
            jax.ShapeDtypeStruct((4, 1, width), jnp.float32),
            jax.ShapeDtypeStruct((16, width), jnp.float32),
        ],
        compiler_params=pltpu.CompilerParams(vmem_limit_bytes=VMEM_LIMIT),
        cost_estimate=lasting(40),
    )(*mixed, *hidden, *cotan, mod, gain, w_out, w_one, b_one, w_two, b_two)


def merge_kernel(parts, second, places_ref, *refs):
    refs = list(refs)

    def take(count):
        taken = refs[:count]
        del refs[:count]
        return taken

    own_parts = [(first, last, take(4 if second else 2)) for first, last in parts[0]]
    split_parts = [(first, last, take(4 if second else 1)) for first, last in parts[1]]
    angle, normed, mixed = take(3), take(3), take(3)
    (low_ref,) = take(1)
    send_ref, keep_ref = take(2)
    merged_refs = take(2 if second else 1)
    normed_ref, mixed_ref = refs
    step = pl.program_id(0)
    first_chunk = (step ^ places_ref[0]) == 1
    span, width = normed[0].shape
    pairs = width // LANES

    @pl.when(step == 0)
    def _():
        for b in range(3):
            rows = slice(b * span, (b + 1) * span)
            normed_ref[:, rows] = normed[b][...].T
            if not second:
                mixed_ref[:, rows] = mixed[b][...].T

    def part_of(block, pair):
        for first, last, arrays in split_parts if block == 2 else own_parts:
            if first <= pair < last:
                return pair - first, arrays

    def keyval_sum(block, pair, lanes):
        at, arrays = part_of(block, pair)
        if block == 2:
            _, near, got, got_chip = arrays
            terms = near[0, at, :, lanes], got[0, at, :, lanes], got_chip[at, :, lanes]
        else:
            _, _, near, got = arrays
            terms = near[block, at, :, lanes], got[block, at, :, lanes]
        return sum(term.astype(jnp.float32) for term in terms)

    def put(result):
        @pl.when(step == 0)
        def _():
            send_ref[0] = result

        @pl.when(step == 1)
        def _():
            keep_ref[0] = result

    def fill(merged_ref, kind):
        for b in range(3):
            rows = slice(b * span, (b + 1) * span)
            for c in range(pairs):
                lanes = slice(c * LANES, (c + 1) * LANES)
                if kind == "q":
                    at, arrays = part_of(b, c)
                    piece = arrays[b % 2][:, at * LANES : (at + 1) * LANES]
                elif kind == "k":
                    (piece,) = turned(keyval_sum(b, c, KEYS), angle[b][0], -angle[b][1])
                else:
                    piece = keyval_sum(b, c, VALUES)
                merged_ref[rows, lanes] = piece.astype(jnp.bfloat16)
        put(dot_nn(normed_ref[...], merged_ref[...]).astype(jnp.bfloat16))

    @pl.when(first_chunk)
    def _():
        fill(merged_refs[0], "k" if second else "q")

    @pl.when(jnp.logical_not(first_chunk))
    def _():
        if second:
            fill(merged_refs[1], "v")
        else:
            put(dot_nn(mixed_ref[...], low_ref[...]).astype(jnp.bfloat16))


def merge_back(places, own_parts, split_parts, angle, normed, mixed, low, second):
    span, width = normed[0].shape
    tokens = 3 * span
    once = pl.Buffered(1)

    def whole(array):
        return pl.BlockSpec(
            array.shape, lambda i, at: (0,) * len(array.shape), pipeline_mode=once
        )

    operands = [array for _, _, arrays in own_parts + split_parts for array in arrays]
    operands += [*angle, *normed, *mixed, low]
    parts = [[(first, last) for first, last, _ in group] for group in (own_parts, split_parts)]
    chunk_shape = jax.ShapeDtypeStruct((1, width, width), jnp.bfloat16)
    merged_shape = jax.ShapeDtypeStruct((tokens, width), jnp.bfloat16)
    merged_count = 2 if second else 1
    return pl.pallas_call(
        functools.partial(merge_kernel, parts, second),
        grid_spec=pltpu.PrefetchScalarGridSpec(
            num_scalar_prefetch=1,
            grid=(2,),
            in_specs=[whole(array) for array in operands],
            out_specs=[pl.BlockSpec((1, width, width), lambda i, at: (0, 0, 0))] * 2
            + [pl.BlockSpec((tokens, width), lambda i, at: (0, 0))] * merged_count,
            scratch_shapes=[
                pltpu.VMEM((width, tokens), jnp.bfloat16),
                pltpu.VMEM((width, tokens), jnp.bfloat16),
            ],
        ),
        out_shape=[chunk_shape] * 2 + [merged_shape] * merged_count,
        compiler_params=pltpu.CompilerParams(vmem_limit_bytes=VMEM_LIMIT),
        cost_estimate=lasting(9),
    )(places, *operands)


def enter_kernel(*refs):
    hidden = refs[0:3]
    resid_grad_ref, mod_ref, gain_ref = refs[3:6]
    merged, weight_ref = refs[6:9], refs[9]
    hidden_grad = refs[10:13]
    sums_ref, total_ref = refs[13:]
    step = pl.program_id(0)
    span = hidden[0].shape[0]

    @pl.when(step == 0)
    def _():
        total_ref[...] = jnp.zeros_like(total_ref)

    for k in range(3):

        @pl.when(step == k)
        def _(k=k):
            total_ref[...] += dot_nt(merged[k][...], weight_ref[...])

    @pl.when(step == 2)
    def _():
        sums_ref[...] = jnp.zeros_like(sums_ref)
        for b in range(3):
            group = group_of(b)
            at = 1 + 2 * group
            rows = slice(b * span, (b + 1) * span)
            values, inverse = normalized(hidden[b][...].astype(jnp.float32))
            grad = total_ref[rows, :]
            scaled = 1.0 + mod_ref[group, 1:2, :]
            weighed = column_sum(grad * values)
            sums_ref[0:1, :] += weighed * scaled
            sums_ref[at : at + 1, :] += column_sum(grad)
            sums_ref[at + 1 : at + 2, :] += weighed * gain_ref[...]
            inner = grad * (scaled * gain_ref[...])
            back = (inner - row_mean(inner) - values * row_mean(inner * values)) * inverse
            hidden_grad[b][...] = (resid_grad_ref[rows, :] + back).astype(jnp.bfloat16)


def enter_back(hidden, resid_grad, mod, gain, merged, weight):
    span, width = hidden[0].shape
    tokens = 3 * span
    once = pl.Buffered(1)
    block = pl.BlockSpec((span, width), lambda i: (0, 0), pipeline_mode=once)
    return pl.pallas_call(
        enter_kernel,
        grid=(3,),
        in_specs=[block] * 3
        + [
            pl.BlockSpec((tokens, width), lambda i: (0, 0), pipeline_mode=once),
            pl.BlockSpec(mod.shape, lambda i: (0, 0, 0)),
            pl.BlockSpec(gain.shape, lambda i: (0, 0)),
            *[pl.BlockSpec((tokens, width), lambda i: (0, 0), pipeline_mode=once)] * 3,
            pl.BlockSpec((width, width), lambda i: (0, i)),
        ],
        out_specs=[pl.BlockSpec((span, width), lambda i: (0, 0))] * 3
        + [pl.BlockSpec((8, width), lambda i: (0, 0))],
        out_shape=[jax.ShapeDtypeStruct((span, width), jnp.bfloat16)] * 3
        + [jax.ShapeDtypeStruct((8, width), jnp.float32)],
        scratch_shapes=[pltpu.VMEM((tokens, width), jnp.float32)],
        compiler_params=pltpu.CompilerParams(vmem_limit_bytes=VMEM_LIMIT),
        cost_estimate=lasting(10),
    )(*hidden, resid_grad, mod, gain, *merged, weight)


def swap(values, axis, bit):
    count = lax.axis_size(axis)
    return lax.ppermute(values, axis, [(i, i ^ bit) for i in range(count)])


def bit_of(axis, bit):
    return (lax.axis_index(axis) // bit) % 2


def batch_bits():
    count = lax.axis_size("batch")
    bits = []
    bit = 1
    while bit < count:
        bits.append(bit)
        bit *= 2
    return bits


def split_orders():
    bits = batch_bits()
    chip = ("seq", 2)
    split = [("batch", b) for b in bits[:3]]
    rest = [("batch", b) for b in bits[3:]]
    return ([chip] + split, split[:1] + [chip] + split[1:], rest)


def place_scalars():
    order_a, order_b, _ = split_orders()
    bits = [bit_of(axis, bit) for axis, bit in order_a + order_b]
    return jnp.stack([lax.axis_index("seq") % 2, *bits]).astype(jnp.int32)


def bits_value(at, group, steps, first, last, flip):
    value = jnp.int32(0)
    for d in range(first, last):
        bit = at[1 + group * steps + d]
        if flip and d == last - 1:
            bit = 1 - bit
        value = value * 2 + bit
    return value


def total_kernel(counts, places_ref, *refs):
    inputs, outputs = refs[: sum(counts)], refs[sum(counts) :]
    start = 0
    for g, count in enumerate(counts):
        total = inputs[start][0].astype(jnp.float32)
        for ref in inputs[start + 1 : start + count]:
            total = total + ref[0].astype(jnp.float32)
        start += count
        if len(outputs) == 1:
            outputs[0][g] = total.astype(jnp.bfloat16)
        else:
            outputs[g][0] = total.astype(jnp.bfloat16)


def total_of_parts(places, parts, steps, done, flip, joint):
    rows = parts[0][0][0].shape[1] >> done
    width = parts[0][0][0].shape[2]
    cuts = max(1, rows // 192)
    rows //= cuts
    operands, specs = [], []
    for g, group in enumerate(parts):
        for array, lead, level in group:
            operands.append(array)
            specs.append(
                pl.BlockSpec(
                    (1, rows, width),
                    lambda i, at, g=g, lead=lead, level=level: (
                        lead,
                        bits_value(at, g, steps, level, done, flip) * cuts + i,
                        0,
                    ),
                )
            )
    if joint:
        out_specs = [pl.BlockSpec((2, rows, width), lambda i, at: (0, i, 0))]
        out_shape = [jax.ShapeDtypeStruct((2, cuts * rows, width), jnp.bfloat16)]
    else:
        out_specs = [pl.BlockSpec((1, rows, width), lambda i, at: (0, i, 0))] * 2
        out_shape = [jax.ShapeDtypeStruct((1, cuts * rows, width), jnp.bfloat16)] * 2
    return pl.pallas_call(
        functools.partial(total_kernel, [len(group) for group in parts]),
        grid_spec=pltpu.PrefetchScalarGridSpec(
            num_scalar_prefetch=1, grid=(cuts,), in_specs=specs, out_specs=out_specs
        ),
        out_shape=out_shape,
        compiler_params=pltpu.CompilerParams(vmem_limit_bytes=VMEM_LIMIT),
        cost_estimate=lasting(3),
    )(places, *operands)


def join_kernel(left_ref, right_ref, out_ref):
    count = left_ref.shape[1]
    out_ref[:, :count] = left_ref[...]
    out_ref[:, count:] = right_ref[...]


def join(left, right):
    lead, count, rows, width = left.shape
    spec = pl.BlockSpec((lead, count, rows, width), lambda i: (0, 0, 0, 0))
    return pl.pallas_call(
        join_kernel,
        grid=(1,),
        in_specs=[spec, spec],
        out_specs=pl.BlockSpec((lead, 2 * count, rows, width), lambda i: (0, 0, 0, 0)),
        out_shape=jax.ShapeDtypeStruct((lead, 2 * count, rows, width), left.dtype),
        compiler_params=pltpu.CompilerParams(vmem_limit_bytes=VMEM_LIMIT),
        cost_estimate=lasting(2),
    )(left, right)


def after(values, *others):
    return lax.optimization_barrier((values, others))[0]


def sync_steps(places, send, keep, gather=True):
    order_a, order_b, rest = split_orders()
    steps = len(order_a)
    if isinstance(send, list):
        got = [swap(part, "seq", 1) for part in send]
        got = after(got, (yield send))
        held = [[(keep[g], 0, 0), (got[g], 0, 0)] for g in range(2)]
    else:
        got = swap(send, "seq", 1)
        got = after(got, (yield [send]))
        held = [[(keep, g, 0), (got, g, 0)] for g in range(2)]
    parts = held
    for done, dims in enumerate(zip(order_a, order_b), 1):
        joint = dims[0] == dims[1]
        sent = total_of_parts(places, parts, steps, done, True, joint)
        if joint:
            got = [swap(sent[0], *dims[0])] * 2
        else:
            got = [swap(sent[g], *dims[g]) for g in range(2)]
        got = after(got, (yield sent))
        for g in range(2):
            parts[g].append((got[g], g if joint else 0, done))
    (held,) = total_of_parts(places, parts, steps, steps, False, True)
    for axis, bit in rest:
        held = (held.astype(jnp.float32) + swap(held, axis, bit).astype(jnp.float32)).astype(
            held.dtype
        )
    if not gather:
        return held
    blocks = held[:, None]
    for dims in reversed(list(zip(order_a, order_b))):
        if dims[0] == dims[1]:
            got = swap(blocks, *dims[0])
            got = after(got, (yield [blocks]))
            blocks = join(blocks, got)
        else:
            if not isinstance(blocks, list):
                blocks = [blocks[0:1], blocks[1:2]]
            got = [swap(blocks[g], *dims[g]) for g in range(2)]
            if dims == (order_a[0], order_b[0]):
                far = [swap(piece, "seq", 1) for piece in blocks]
                ties = yield [*blocks, *far]
                got = after(got, ties)
                far_got = [swap(piece, "seq", 1) for piece in got]
                return [*got, *far_got]
            got = after(got, (yield blocks))
            blocks = [join(blocks[g], got[g]) for g in range(2)]


HEAD_ROWS, ROW_BLOCK = 8, 24


def pack_kernel(places_ref, feed_ref, merge_ref, bias_ref, cond_ref, out_ref):
    out_ref[...] = jnp.zeros_like(out_ref)
    out_ref[0:1, :] = merge_ref[0:1, :]
    out_ref[1:3, :] = feed_ref[0:2, :]
    for c in range(bias_ref.shape[0]):
        out_ref[3 + c : 4 + c, :] = bias_ref[c]
    for group in range(2):
        merged = merge_ref[1 + 2 * group : 3 + 2 * group, :]
        fed = feed_ref[2 + 4 * group : 6 + 4 * group, :]
        for j in range(6):
            value = merged[j : j + 1, :] if j < 2 else fed[j - 2 : j - 1, :]
            at = HEAD_ROWS + 3 * j
            if group == 1:
                out_ref[at + 2 : at + 3, :] = value
                continue
            for chip in range(2):
                out_ref[at + chip : at + chip + 1, :] = jnp.where(
                    places_ref[0] // 2 == chip, value, 0.0
                )
    rows, count = cond_ref.shape
    for r in range(rows):
        out_ref[HEAD_ROWS + 18 : HEAD_ROWS + 19, r * count : (r + 1) * count] = (
            cond_ref[r : r + 1, :] * 0.25
        )


def pack_small(seat, feed_sums, merge_sums, bias_grad, cond):
    width = feed_sums.shape[1]

    def whole(array):
        return pl.BlockSpec(array.shape, lambda i, at: (0,) * len(array.shape))

    operands = [feed_sums, merge_sums, bias_grad, cond]
    rows = HEAD_ROWS + ROW_BLOCK
    return pl.pallas_call(
        pack_kernel,
        grid_spec=pltpu.PrefetchScalarGridSpec(
            num_scalar_prefetch=1,
            grid=(1,),
            in_specs=[whole(array) for array in operands],
            out_specs=pl.BlockSpec((rows, width), lambda i, at: (0, 0)),
        ),
        out_shape=jax.ShapeDtypeStruct((rows, width), jnp.float32),
        cost_estimate=lasting(2),
    )(seat, *operands)


def grow_kernel(own_ref, got_ref, out_ref):
    rows = own_ref.shape[0]
    out_ref[:HEAD_ROWS] = own_ref[:HEAD_ROWS] + got_ref[:HEAD_ROWS]
    out_ref[HEAD_ROWS:rows] = own_ref[HEAD_ROWS:]
    out_ref[rows:] = got_ref[HEAD_ROWS:]


def grow(own, got):
    rows, width = own.shape
    return pl.pallas_call(
        grow_kernel,
        out_shape=jax.ShapeDtypeStruct((2 * rows - HEAD_ROWS, width), own.dtype),
        cost_estimate=lasting(2),
    )(own, got)


class SmallSums:
    def __init__(self, values):
        self.values = values
        self.dims = [("seq", 1), ("seq", 2)] + [("batch", b) for b in batch_bits()]
        self.pending = None

    def step(self, *done):
        self.take(*done)
        if self.dims:
            self.axis, bit = self.dims.pop(0)
            self.pending = swap(self.values, self.axis, bit)

    def take(self, *done):
        if self.pending is None:
            return
        got = after(self.pending, *done) if done else self.pending
        self.pending = None
        self.values = self.values + got if self.axis == "seq" else grow(self.values, got)

    def finish(self, *done):
        while self.dims:
            self.step(*done)
        self.take(*done)


def modulation_kernel(values_ref, weight_ref, cond_ref, bias_ref, grad_ref):
    values = values_ref[HEAD_ROWS:, :]
    rows, width = values.shape
    count = weight_ref.shape[0]
    conds = []
    for block in range(rows // ROW_BLOCK):
        line = values[block * ROW_BLOCK + 18 : block * ROW_BLOCK + 19, :]
        three = [line[:, r * count : (r + 1) * count] for r in range(3)]
        conds += three * 6 + [jnp.zeros((ROW_BLOCK - 18, count), jnp.float32)]
    conds = jnp.concatenate(conds, axis=0)
    place = lax.broadcasted_iota(jnp.int32, (rows, count), 0) % ROW_BLOCK // 3
    wide_place = lax.broadcasted_iota(jnp.int32, (rows, width), 0) % ROW_BLOCK // 3
    total = None
    for j in range(6):
        lanes = slice(j * width, (j + 1) * width)
        grad_ref[:, lanes] = lax.dot_general(
            jnp.where(place == j, conds, 0.0),
            values,
            (((0,), (0,)), ((), ())),
            precision=highest,
            preferred_element_type=jnp.float32,
        )
        bias_ref[:, lanes] = column_sum(jnp.where(wide_place == j, values, 0.0))
        term = lax.dot_general(
            values[3 * j : 3 * j + 3, :],
            weight_ref[:, lanes].astype(jnp.float32),
            (((1,), (1,)), ((), ())),
            precision=highest,
            preferred_element_type=jnp.float32,
        )
        total = term if total is None else total + term
    cond_ref[...] = total


def modulation_back(values, weight):
    count, wide = weight.shape
    return pl.pallas_call(
        modulation_kernel,
        out_shape=[
            jax.ShapeDtypeStruct((3, count), jnp.float32),
            jax.ShapeDtypeStruct((1, wide), jnp.float32),
            jax.ShapeDtypeStruct((count, wide), jnp.float32),
        ],
        compiler_params=pltpu.CompilerParams(vmem_limit_bytes=VMEM_LIMIT),
        cost_estimate=lasting(7),
    )(values, weight)


def run_on(steps, *done):
    try:
        return steps.send(done), None
    except StopIteration as end:
        return None, end.value


def spread_blocks(places_ref, ref, group, out):
    _, count, rows, _ = ref.shape
    steps = count.bit_length()
    place = bits_value(places_ref, group, steps, 1, steps, False)

    @pl.loop(0, count)
    def _(j):
        row = pl.multiple_of((place ^ j) * rows, 8)
        out[pl.ds(row, rows), :] = ref[0, j].astype(jnp.float32)


def piece_chunk(step, core):
    owner = jnp.where(step < 2, core, 1 - core)
    group = step % 2
    return jnp.where(owner == 0, group, 3 - group)


def finish_feed_kernel(chunks_ref, one_ref, two_ref):
    one_ref[...] = chunks_ref[0, 0].astype(jnp.float32)
    two_ref[...] = chunks_ref[0, 1].astype(jnp.float32)


def finish_feed(chunks):
    count, _, width, _ = chunks.shape
    cuts = 1
    rows = width // cuts
    return pl.pallas_call(
        finish_feed_kernel,
        grid=(count, cuts),
        in_specs=[pl.BlockSpec((1, 2, rows, width), lambda i, j: (i, 0, j, 0))],
        out_specs=[
            pl.BlockSpec((rows, width), lambda i, j: (j, i)),
            pl.BlockSpec((rows, width), lambda i, j: (cuts * i + j, 0)),
        ],
        out_shape=[
            jax.ShapeDtypeStruct((width, count * width), jnp.float32),
            jax.ShapeDtypeStruct((count * width, width), jnp.float32),
        ],
        compiler_params=pltpu.CompilerParams(vmem_limit_bytes=VMEM_LIMIT),
        cost_estimate=lasting(8),
    )(chunks)


def finish_kernel(places_ref, *refs):
    pieces, outs = refs[:4], refs[-2:]
    step = pl.program_id(0)
    chunk = piece_chunk(step, places_ref[0])
    for k in range(4):
        for condition, out in ((chunk < 3, outs[0]), (chunk == 3, outs[1])):

            @pl.when((step == k) & condition)
            def _(ref=pieces[k], group=k % 2, out=out):
                spread_blocks(places_ref, ref, group, out)


def finish_half(places, pieces, second, started=()):
    _, count, rows, width = pieces[0].shape
    steps = count.bit_length()
    half = count * rows
    whole = pl.BlockSpec((1, count, rows, width), lambda i, at: (0, 0, 0, 0))
    anywhere = pl.BlockSpec(memory_space=pl.ANY)

    def side(i, at):
        mine = jnp.where(i % 2 == 0, at[1], at[1 + steps])
        return 1 - mine if second else mine

    return pl.pallas_call(
        finish_kernel,
        grid_spec=pltpu.PrefetchScalarGridSpec(
            num_scalar_prefetch=1,
            grid=(4,),
            in_specs=[whole] * 4 + [anywhere] * len(started),
            out_specs=[
                pl.BlockSpec(
                    (half, width),
                    lambda i, at: (
                        side(jnp.where(piece_chunk(i, at[0]) == 3, i + 1, i), at),
                        jnp.minimum(piece_chunk(i, at[0]), 2),
                    ),
                ),
                pl.BlockSpec((half, width), lambda i, at: (side(0, at), 0)),
            ],
        ),
        out_shape=[
            jax.ShapeDtypeStruct((width, 3 * width), jnp.float32),
            jax.ShapeDtypeStruct((width, width), jnp.float32),
        ],
        input_output_aliases={5 + k: k for k in range(len(started))},
        compiler_params=pltpu.CompilerParams(vmem_limit_bytes=VMEM_LIMIT),
        cost_estimate=lasting(4),
    )(places, *pieces, *started)


def pick(values, index):
    return lax.dynamic_index_in_dim(values, index, 0, keepdims=False)


def rows_of(own, other, third, chip):
    first = jnp.where(chip == 0, own, other)
    second = jnp.where(chip == 0, other, own)
    return jnp.stack([first, second, third])


def shards(
    hidden,
    cond,
    lengths,
    ln1_gain,
    w_qkv,
    w_out,
    ln2_gain,
    w_fc1,
    b_fc1,
    w_fc2,
    b_fc2,
    w_ada,
    b_ada,
    cotangent,
):
    row_count, span, width = hidden.shape
    places = place_scalars()
    seat = lax.axis_index("seq")
    chip = seat // 2
    bases = jnp.stack([seat, seat ^ 2, seat ^ 1, seat ^ 3]) * span
    layout = jnp.concatenate(
        [pick(lengths, chip).reshape(-1), lengths[2], bases.astype(jnp.int32)]
    )
    hidden_far = swap(pick(hidden, 1 - chip), "seq", 2)
    blocks = [pick(hidden, chip), hidden_far, hidden[2]]
    ada_full = w_ada.astype(jnp.float32)
    modulation = (
        jnp.dot(cond, ada_full, precision=highest, preferred_element_type=jnp.float32) + b_ada
    )
    mod = jnp.stack([pick(modulation, chip), modulation[2]]).reshape(2, 6, width)
    gain_one, gain_two = ln1_gain[None], ln2_gain[None]

    normed_own, normed_split, query_own, query_split, kv_own, kv_split, angle_own, angle_split = (
        project(layout, [blocks[0], blocks[2]], mod, gain_one, w_qkv, (0, 1), (0, 0))
    )
    split_chip = swap(kv_split, "seq", 2)
    split_core = swap(kv_split, "seq", 1)
    own_core = swap(kv_own, "seq", 1)
    normed_far, query_far, kv_far, angle_far = project(
        layout, [blocks[1]], mod, gain_one, w_qkv, (0,), (1,)
    )
    far_core = swap(kv_far, "seq", 1)
    cotan_far = swap(pick(cotangent, 1 - chip), "seq", 2)
    cotan = [pick(cotangent, chip), cotan_far, cotangent[2]]
    kv_row = [kv_own, kv_far, own_core, far_core]
    mixed_own, mixed_far, logsum_own, logsum_far = attend(
        after(layout, *kv_row), [query_own, query_far], kv_row, 0
    )
    split_chip = after(split_chip, logsum_own)
    split_cross = swap(split_chip, "seq", 1)
    kv_third = [kv_split, split_chip, split_core, split_cross]
    mixed_split, logsum_split = attend(after(layout, mixed_far), [query_split], kv_third, 1)
    mixed = [mixed_own, mixed_far, mixed_split]
    (
        result_own,
        result_far,
        result_split,
        mixed_grad_own,
        mixed_grad_far,
        mixed_grad_split,
        resid_grad,
        low,
        feed_chunks,
        b_one_grad,
        feed_sums,
    ) = feed(
        mixed,
        blocks,
        cotan,
        mod,
        gain_two,
        w_out,
        w_fc1,
        b_fc1[None],
        w_fc2,
        b_fc2[None],
    )
    everyone = ("seq", "batch")
    feed_share = lax.psum_scatter(
        feed_chunks.reshape(-1, width), everyone, scatter_dimension=0, tiled=True
    )
    pairs = width // LANES

    def back_of_row(sent):
        return attend_back(
            after(layout, sent),
            [query_own, query_far],
            [mixed_own, mixed_far],
            [mixed_grad_own, mixed_grad_far],
            [logsum_own, logsum_far],
            [angle_own, angle_far],
            kv_row,
            0,
        )

    def back_of_split(sent):
        return attend_back(
            after(layout, sent),
            [query_split],
            [mixed_split],
            [mixed_grad_split],
            [logsum_split],
            [angle_split],
            kv_third,
            1,
            some=2,
        )

    split_grad, near_split, far_split = back_of_split(mixed_split)
    got_split = swap(far_split, "seq", 1)
    got_split = after(got_split, split_grad)
    chip_sum = near_split[1].astype(jnp.float32) + got_split[1].astype(jnp.float32)
    chip_sum = chip_sum.astype(jnp.bfloat16)
    chip_split = swap(chip_sum, "seq", 2)
    own_grad, far_grad, near_own, far_own = back_of_row(split_grad)
    tables = [angle_own, angle_far, angle_split], [normed_own, normed_far, normed_split], mixed, low
    send_a, keep_a, merged_q = merge_back(
        after(places, chip_split),
        [(0, pairs, [own_grad, far_grad])],
        [(0, pairs, [split_grad])],
        *tables,
        second=False,
    )
    got_own = swap(after(far_own, send_a), "seq", 1)
    send_b, keep_b, merged_k, merged_v = merge_back(
        after(places, send_a),
        [(0, pairs, [own_grad, far_grad, near_own, got_own])],
        [(0, pairs, [split_grad, near_split, got_split, chip_split])],
        *tables,
        second=True,
    )
    hidden_own_grad, hidden_far_grad, hidden_split_grad, merge_sums = enter_back(
        blocks,
        resid_grad,
        mod,
        gain_one,
        [merged_q, merged_k, merged_v],
        w_qkv,
    )
    att_steps = sync_steps(places, after([send_a, send_b], merge_sums), [keep_a, keep_b])
    sent_att = next(att_steps)
    far_hidden_grad = swap(hidden_far_grad, "seq", 2)
    far_result = swap(after(result_far, merge_sums), "seq", 2)
    small = SmallSums(
        pack_small(seat.astype(jnp.int32)[None], feed_sums, merge_sums, b_one_grad, cond)
    )
    small.step()
    sent_att, _ = run_on(att_steps, merge_sums)
    small.step(sent_att)
    sent_att, _ = run_on(att_steps, small.values)
    small.step(sent_att)
    sent_att, _ = run_on(att_steps, small.values, far_result)
    small.step(sent_att)
    sent_att, _ = run_on(att_steps, small.values, far_hidden_grad)
    feed_whole = lax.all_gather(after(feed_share, sent_att), everyone, axis=0, tiled=True)
    small.step(sent_att)
    sent_att, _ = run_on(att_steps, small.values)
    small.finish(sent_att)
    vectors = small.values[:HEAD_ROWS]
    cond_grad, ada_bias_grad, ada_grad = modulation_back(small.values, w_ada)
    sent_att, _ = run_on(att_steps, vectors)
    output = rows_of(result_own, far_result, result_split, chip)
    hidden_grad = rows_of(hidden_own_grad, far_hidden_grad, hidden_split_grad, chip)
    sent_att, _ = run_on(att_steps, output, hidden_grad)
    ln1_grad, ln2_grad, fc2_bias_grad = vectors[0], vectors[1], vectors[2]
    fc1_bias_grad = vectors[3:7].reshape(-1)
    ada_bias_grad = ada_bias_grad.reshape(-1)
    first_half, _ = run_on(att_steps, ada_grad, cond_grad, ada_bias_grad, fc1_bias_grad)
    first_half = after(first_half, ln1_grad, ln2_grad, fc2_bias_grad)
    started = finish_half(places, first_half, False)
    _, second_half = run_on(att_steps, started[1])
    qkv_grad, out_grad = finish_half(places, second_half, True, started)
    fc1_grad, fc2_grad = finish_feed(after(feed_whole, out_grad).reshape(feed_chunks.shape))
    return (
        output,
        hidden_grad,
        cond_grad,
        ln1_grad,
        qkv_grad,
        out_grad,
        ln2_grad,
        fc1_grad,
        fc1_bias_grad,
        fc2_grad,
        fc2_bias_grad,
        ada_grad,
        ada_bias_grad,
    )


def solution(mesh):
    return jax.shard_map(
        shards,
        mesh=mesh,
        in_specs=(
            P("batch", "seq", None),
            P("batch", None),
            P("batch", None),
            P(),
            P(),
            P(),
            P(),
            P(),
            P(),
            P(),
            P(),
            P(),
            P(),
            P("batch", "seq", None),
        ),
        out_specs=(
            P("batch", "seq", None),
            P("batch", "seq", None),
            P("batch", None),
            P(),
            P(),
            P(),
            P(),
            P(),
            P(),
            P(),
            P(),
            P(),
            P(),
        ),
        check_vma=False,
    )
```
